32 devices in a mesh: clip: 4 (over z), frame: 8 (over y, x, core).
Axes of the slice: x: 2, y: 2, z: 4, core: 2. Of those that a mesh axis runs over, the one named last changes fastest.
Arguments:
- tokens: bfloat16 [16, 16, 256, 768], P('clip', 'frame'), may hold values from -6 to 6
- frame_counts: int32 [16], P('clip'), may hold values from 8 to 16, as said below
- norm_gain: float32 [2, 2, 768], replicated, may hold values from 0.25 to 1.75
- norm_bias: float32 [2, 2, 768], replicated, may hold values from -2.5 to 2.5
- project_in: bfloat16 [2, 768, 2304], replicated, may hold values from -0.21875 to 0.21875
- project_out: bfloat16 [2, 768, 768], replicated, may hold values from -0.875 to 0.875
- expand_weight: bfloat16 [2, 768, 3072], replicated, may hold values from -0.21875 to 0.21875
- expand_bias: float32 [2, 3072], replicated, may hold values from -3 to 3
- reduce_weight: bfloat16 [2, 3072, 768], replicated, may hold values from -0.109375 to 0.109375
- cotangent: bfloat16 [16, 16, 256, 768], P('clip', 'frame'), may hold values from -6 to 6
Outputs:
- mixed: bfloat16 [16, 16, 256, 768], P('clip', 'frame')
- grad_tokens: bfloat16 [16, 16, 256, 768], P('clip', 'frame')
- grad_norm_gain: float32 [2, 2, 768], P(None, None, 'frame')
- grad_norm_bias: float32 [2, 2, 768], P(None, None, 'frame')
- grad_project_in: float32 [2, 768, 2304], P(None, 'frame')
- grad_project_out: float32 [2, 768, 768], P(None, 'frame')
- grad_expand_weight: float32 [2, 768, 3072], P(None, 'frame')
- grad_expand_bias: float32 [2, 3072], P(None, 'frame')
- grad_reduce_weight: float32 [2, 3072, 768], P(None, 'frame')
The draws below stay inside these ranges and needn't reach their ends.
Inputs may be any that keep to these rules, and one draw needn't show every extreme that they name: `frame_counts`: each entry is 8 or 16; at least one clip has 8 frames and at least one has 16; each aligned block of 4 consecutive clips (the clips of one device along `clip`) holds at least one clip of 16 frames.
All inputs are finite; a program needn't handle non-finite values.
Results may differ from the reference program's by a relative error of at most 0.02.
Values may be sent and summed in bfloat16 or wider, within the bound.
No kernel may reach another device: no remote copies, remote signals or barrier semaphores. Data moves between devices by JAX's collectives and lax.ppermute only.
A program may use at most 1.1875 GiB of HBM per device.

```python
import jax
import jax.numpy as jnp
from jax import lax

D = 768
HEAD_DIM = 64
MLP = 3072
FRAMES = 16
TOK_FRAME = 256
TUBE = 16
TUBES = 16
CLIP_DEV = 4
CLIPS = 16


def draw_frame_counts(key, part):
    key = jax.random.fold_in(key, 11)
    coin = jax.random.randint(jax.random.fold_in(key, 1), (CLIPS,), 0, 4)
    counts = jnp.where(coin == 0, 8, 16).astype(jnp.int32)
    groups = CLIPS // CLIP_DEV
    chosen = jax.random.randint(jax.random.fold_in(key, 3), (), 0, groups).astype(jnp.int32)
    if CLIP_DEV >= 2:
        picked = jax.random.randint(jax.random.fold_in(key, 2), (groups,), 0, CLIP_DEV).astype(jnp.int32)
        forced = jnp.arange(groups, dtype=jnp.int32) * CLIP_DEV + picked
        counts = counts.at[forced].set(16)
        shorter = chosen * CLIP_DEV + (picked[chosen] + 1) % CLIP_DEV
        counts = counts.at[shorter].set(8)
    else:
        counts = counts.at[chosen].set(8)
        counts = counts.at[(chosen + 1) % CLIPS].set(16)
    return counts


def block_levels(stream_key, extent, split, least, high):
    def one(position, shards_of):
        steps = jax.random.uniform(jax.random.fold_in(jax.random.fold_in(stream_key, 6), position), (shards_of,), jnp.float32, least / len(split), high / len(split))
        return jnp.repeat(jnp.exp(steps), extent[position] // shards_of).reshape((-1,) + (1,) * (len(extent) - position - 1))

    level = one(*split[0])
    for cut in split[1:]:
        level = level * one(*cut)
    return level


def bell_draw(own_key, dims, width, reach, cuts=(), kind=jnp.bfloat16):
    array = width * jax.random.normal(own_key, dims, jnp.float32)
    if cuts:
        array = array * block_levels(own_key, dims, cuts, -0.22, 0.18)
    return jnp.clip(array, -reach, reach).astype(kind)


def setup_inputs(seed: int = 0) -> dict:
    streams_of = jax.random.split(jax.random.key(seed), 11)
    tokens = bell_draw(streams_of[0], (CLIPS, FRAMES, TOK_FRAME, D), 1.0, 6.0, ((0, 4), (1, 8)))
    frame_counts = draw_frame_counts(jax.random.fold_in(streams_of[10], 71), 0)
    norm_gain = jnp.clip(1.0 + 0.15 * jax.random.normal(streams_of[2], (2, 2, D), jnp.float32), 0.25, 1.75)
    norm_bias = bell_draw(streams_of[3], (2, 2, D), 0.3, 2.5, (), jnp.float32)
    project_in = bell_draw(streams_of[4], (2, D, 3 * D), D ** -0.5, 0.21875)
    project_out = bell_draw(streams_of[5], (2, D, D), (D // 16) ** -0.5, 0.875)
    expand_weight = bell_draw(streams_of[6], (2, D, MLP), D ** -0.5, 0.21875)
    expand_bias = bell_draw(streams_of[7], (2, MLP), 0.5, 3.0, (), jnp.float32)
    reduce_weight = bell_draw(streams_of[8], (2, MLP, D), MLP ** -0.5, 0.109375)
    cotangent = bell_draw(streams_of[9], (CLIPS, FRAMES, TOK_FRAME, D), 1.0, 6.0, ((0, 4), (1, 8)))
    return dict(tokens=tokens, frame_counts=frame_counts, norm_gain=norm_gain, norm_bias=norm_bias, project_in=project_in, project_out=project_out, expand_weight=expand_weight, expand_bias=expand_bias, reduce_weight=reduce_weight, cotangent=cotangent)


@jax.custom_vjp
def low(v):
    return lax.optimization_barrier(v.astype(jnp.bfloat16)).astype(jnp.float32)

@jax.custom_vjp
def low_back(v):
    return v

def low_keep(v):
    return (low(v), None)

def low_pass(kept, grad):
    return (grad,)

def back_keep(v):
    return (v, None)

def back_low(kept, grad):
    return (low(grad),)
low.defvjp(low_keep, low_pass)
low_back.defvjp(back_keep, back_low)
EPSILON = 1e-05
HIGHEST = lax.Precision.HIGHEST

def norm_rows(stream, gain_row, shift_row):
    center = stream - lax.optimization_barrier(jnp.mean(stream, axis=-1, keepdims=True))
    spread = lax.optimization_barrier(jnp.mean(center * center, axis=-1, keepdims=True))
    return center * lax.rsqrt(spread + EPSILON) * gain_row + shift_row

def attend(queries, keys_in, values, kept_keys):
    scores = jnp.einsum('bftphe,bgtqhe->bthfpgq', queries, keys_in, precision=HIGHEST) * queries.shape[-1] ** (-0.5)
    scores = low_back(scores)
    scores = jnp.where(kept_keys[:, None, None, None, None, :, None], scores, -1e+30)
    layout = scores.shape
    flat_scores = scores.reshape(layout[:5] + (layout[5] * layout[6],))
    softmax_out = low(jax.nn.softmax(flat_scores, axis=-1).reshape(layout))
    attended = jnp.einsum('bthfpgq,bgtqhe->bftphe', softmax_out, values, precision=HIGHEST)
    return low(low_back(attended))

def block(stream, kept_keys, gain_pair, shift_pair, project_in, project_out, expand_weight, expand_bias, reduce_weight):
    model_width = stream.shape[-1]
    head_count = model_width // HEAD_DIM
    normed = low(norm_rows(stream, gain_pair[0], shift_pair[0]))
    triple = low(low_back(jnp.dot(normed, project_in, precision=HIGHEST)))
    triple = triple.reshape(stream.shape[:-1] + (3, head_count, HEAD_DIM))
    attended = attend(triple[..., 0, :, :], triple[..., 1, :, :], triple[..., 2, :, :], kept_keys)
    branch_one = low_back(jnp.dot(attended.reshape(stream.shape), project_out, precision=HIGHEST))
    middle = stream + branch_one
    normed_two = low(norm_rows(middle, gain_pair[1], shift_pair[1]))
    pre_act = low_back(jnp.dot(normed_two, expand_weight, precision=HIGHEST) + expand_bias)
    activated = low(jax.nn.gelu(pre_act, approximate=False))
    branch_two = low_back(jnp.dot(activated, reduce_weight, precision=HIGHEST))
    return middle + branch_two

def clip_layer(clip_tokens, frame_count, weights):
    norm_gain, norm_bias, project_in, project_out, expand_weight, expand_bias, reduce_weight = weights
    model_width = clip_tokens.shape[-1]
    spatial_in = clip_tokens.reshape(FRAMES, 1, 1, TOK_FRAME, model_width)
    all_kept = jnp.ones((FRAMES, 1), dtype=bool)
    spatial_out = block(spatial_in, all_kept, norm_gain[0], norm_bias[0], project_in[0], project_out[0], expand_weight[0], expand_bias[0], reduce_weight[0])
    tube_in = low(low_back(spatial_out)).reshape(1, FRAMES, TUBES, TUBE, model_width)
    frame_kept = (jnp.arange(FRAMES) < frame_count)[None, :]
    tube_out = block(tube_in, frame_kept, norm_gain[1], norm_bias[1], project_in[1], project_out[1], expand_weight[1], expand_bias[1], reduce_weight[1])
    return tube_out.reshape(FRAMES, TOK_FRAME, model_width)

def reference(tokens, frame_counts, norm_gain, norm_bias, project_in, project_out, expand_weight, expand_bias, reduce_weight, cotangent):
    weights = (norm_gain.astype(jnp.float32), norm_bias.astype(jnp.float32), project_in.astype(jnp.float32), project_out.astype(jnp.float32), expand_weight.astype(jnp.float32), expand_bias.astype(jnp.float32), reduce_weight.astype(jnp.float32))

    def clip_step(totals, inputs):
        clip_tokens, frame_count, clip_cotangent = inputs

        def forward(start_tokens, layer_weights):
            return clip_layer(start_tokens, frame_count, layer_weights)
        result, pullback = jax.vjp(forward, clip_tokens.astype(jnp.float32), weights)
        grad_clip, grad_weights = pullback(clip_cotangent.astype(jnp.float32))
        totals = jax.tree.map(jnp.add, totals, grad_weights)
        return (totals, (result.astype(jnp.bfloat16), grad_clip.astype(jnp.bfloat16)))
    empty = jax.tree.map(jnp.zeros_like, weights)
    totals, outputs = lax.scan(clip_step, empty, (tokens, frame_counts, cotangent))
    return (outputs[0], outputs[1], totals[0], totals[1], totals[2], totals[3], totals[4], totals[5], totals[6])
```

```python
import functools

import jax
import jax.numpy as jnp
from jax import lax
from jax.experimental import pallas as pl
from jax.experimental.pallas import tpu as pltpu
from jax.sharding import PartitionSpec as P

HEAD_DIM = 64
TUBE = 16
PAIR = 2 * HEAD_DIM
EPSILON = 1e-05
HALF_ROOT = 0.7071067811865476
BELL_PEAK = 0.3989422804014327
LOW = jnp.bfloat16
WIDE = jnp.float32
VMEM_BYTES = 62 * 1024 * 1024


def dot(left, right, left_dim=1, right_dim=0):
    return lax.dot_general(
        left, right, (((left_dim,), (right_dim,)), ((), ())), preferred_element_type=WIDE
    )


def normalize(x):
    center = x - jnp.mean(x, axis=-1, keepdims=True)
    scale = lax.rsqrt(jnp.mean(center * center, axis=-1, keepdims=True) + EPSILON)
    return center * scale, scale


def normalize_back(n, scale, gain, grad):
    e = grad * gain
    return scale * (
        e - jnp.mean(e, axis=-1, keepdims=True) - n * jnp.mean(e * n, axis=-1, keepdims=True)
    )


def chunks(total, size):
    return [slice(start, start + size) for start in range(0, total, size)]


def load_window(ref, layout, window, length):
    if layout == "rows":
        return ref[window * length : (window + 1) * length, :]
    if layout == "frames":
        block = ref[:, 0, window]
    else:
        block = ref[:, 0, :, window * TUBE : (window + 1) * TUBE, :]
    return block.reshape(length, ref.shape[-1])


def store_window(ref, layout, window, length, value):
    if layout == "rows":
        ref[window * length : (window + 1) * length, :] = value
    elif layout == "frames":
        ref[:, 0, window] = value.reshape(ref.shape[0], ref.shape[3], ref.shape[4])
    else:
        ref[:, 0, :, window * TUBE : (window + 1) * TUBE, :] = value.reshape(
            ref.shape[0], ref.shape[2], TUBE, ref.shape[4]
        )


def load_rows(ref, layout, windows, length):
    if layout == "rows":
        return ref[...]
    return jnp.concatenate([load_window(ref, layout, w, length) for w in range(windows)], axis=0)


def split_heads(first, value):
    zero = jnp.zeros_like(value)
    return jnp.where(first, value, zero), jnp.where(first, zero, value)


def forward_kernel(
    dims, counts, x, gain, shift, w_in, w_out, w_expand, b_expand, w_reduce, *refs
):
    block, windows, length, width, hidden, in_layout, out_layout, first_clip, masked, n_alias = dims
    refs = refs[n_alias:]
    out, normed_o, triple_o, recip_o, raised_o, attended_o, middle_o, normed2_o, active_o, slope_o = refs
    rows = windows * length
    stream = load_rows(x, in_layout, windows, length).astype(WIDE)
    n, unused = normalize(stream)
    normed_o[...] = (n * gain[block, 0] + shift[block, 0]).astype(LOW)
    for c in chunks(3 * width, width):
        triple_o[:, c] = dot(normed_o[...], w_in[:, c]).astype(LOW)
    first = lax.broadcasted_iota(jnp.int32, (length, PAIR), 1) < HEAD_DIM
    ones_a, ones_b = split_heads(first, jnp.ones((length, PAIR), LOW))
    if masked:
        kept = counts[first_clip + pl.program_id(0)] * TUBE
        bias = jnp.where(
            lax.broadcasted_iota(jnp.int32, (1, length), 1) < kept, 0.0, -1e30
        ).astype(WIDE)
    for w in range(windows):
        span = slice(w * length, (w + 1) * length)
        for p, c in enumerate(chunks(width, PAIR)):
            queries = triple_o[span, c] * LOW(HEAD_DIM**-0.5)
            keys = triple_o[span, c.start + width : c.stop + width]
            values = triple_o[span, c.start + 2 * width : c.stop + 2 * width]
            raised = []
            for q in split_heads(first, queries):
                scores = dot(q, keys, 1, 1)
                if masked:
                    scores = scores + bias
                raised.append(
                    jnp.exp(scores - jnp.max(scores, axis=1, keepdims=True)).astype(LOW)
                )
            raised = jnp.concatenate(raised, axis=1)
            raised_o[w, p] = raised
            values_a, values_b = split_heads(first, values)
            sums = dot(
                raised,
                jnp.concatenate(
                    [
                        jnp.concatenate([values_a, ones_a], axis=1),
                        jnp.concatenate([values_b, ones_b], axis=1),
                    ],
                    axis=0,
                ),
            )
            recip = 1.0 / sums[:, PAIR:]
            recip_o[span, c] = recip
            attended_o[span, c] = (sums[:, :PAIR] * recip).astype(LOW)
    middle = stream + dot(attended_o[...], w_out[...])
    middle_o[...] = middle
    n, unused = normalize(middle)
    normed2_o[...] = (n * gain[block, 1] + shift[block, 1]).astype(LOW)
    total = middle
    for c in chunks(hidden, 512):
        pre = dot(normed2_o[...], w_expand[:, c]) + b_expand[block : block + 1, c]
        below = 0.5 + 0.5 * lax.erf(pre * HALF_ROOT)
        active = (pre * below).astype(LOW)
        active_o[:, c] = active
        slope_o[:, c] = (below + pre * (BELL_PEAK * jnp.exp(-0.5 * pre * pre))).astype(LOW)
        total = total + dot(active, w_reduce[c, :])
    total = total.astype(LOW)
    for w in range(windows):
        store_window(out, out_layout, w, length, total[w * length : (w + 1) * length])


def mlp_back_kernel(
    dims, g, slope, middle, gain, w_expand, w_reduce, *refs
):
    block, windows, length, width, hidden, g_layout, n_alias = dims
    refs = refs[n_alias:]
    rows_o, pre_o, mid_o, bias_o, gain_o, shift_o = refs
    grad = load_rows(g, g_layout, windows, length)
    rows_o[...] = grad
    first_step = pl.program_id(0) == 0

    @pl.when(first_step)
    def _():
        bias_o[...] = jnp.zeros_like(bias_o)
        gain_o[...] = jnp.zeros_like(gain_o)
        shift_o[...] = jnp.zeros_like(shift_o)

    total = None
    for c in chunks(hidden, 512):
        pre = (dot(grad, w_reduce[c, :], 1, 1) * slope[:, c].astype(WIDE)).astype(LOW)
        pre_o[:, c] = pre
        bias_o[:, c] += jnp.sum(pre.astype(WIDE), axis=0, keepdims=True)
        part = dot(pre, w_expand[:, c], 1, 1)
        total = part if total is None else total + part
    n, scale = normalize(middle[...])
    gain_o[...] += jnp.sum(total * n, axis=0, keepdims=True)
    shift_o[...] += jnp.sum(total, axis=0, keepdims=True)
    mid_o[...] = (
        grad.astype(WIDE) + normalize_back(n, scale, gain[block, 1], total)
    ).astype(mid_o.dtype)


def attention_back_kernel(
    dims, x, mid, triple, recip, raised, attended, gain, w_in, w_out, *refs
):
    block, windows, length, width, x_layout, out_layout, n_alias = dims
    refs = refs[n_alias:]
    out, triple_o, gain_o, shift_o, grad_s = refs
    first_step = pl.program_id(0) == 0

    @pl.when(first_step)
    def _():
        gain_o[...] = jnp.zeros_like(gain_o)
        shift_o[...] = jnp.zeros_like(shift_o)

    grad_s[...] = dot(mid[...].astype(LOW), w_out[...], 1, 1).astype(LOW)
    first = lax.broadcasted_iota(jnp.int32, (length, PAIR), 1) < HEAD_DIM
    minus = jnp.full((length, PAIR), -1.0, LOW)
    root = HEAD_DIM**-0.5
    for w in range(windows):
        span = slice(w * length, (w + 1) * length)
        for p, c in enumerate(chunks(width, PAIR)):
            c_keys = slice(c.start + width, c.stop + width)
            c_values = slice(c.start + 2 * width, c.stop + 2 * width)
            grad = grad_s[span, c]
            grad_wide = grad.astype(WIDE)
            share = recip[span, c]
            inner = (grad_wide * attended[span, c].astype(WIDE)).astype(LOW)
            grad_scaled = (grad_wide * share).astype(LOW)
            queries = (triple[span, c].astype(WIDE) * (share * root)).astype(LOW)
            keys = triple[span, c_keys] * LOW(root)
            values = jnp.concatenate([triple[span, c_values], minus], axis=1)
            scores = []
            for i, (a, b) in enumerate(zip(split_heads(first, grad), split_heads(first, inner))):
                delta = dot(jnp.concatenate([a, b], axis=1), values, 1, 1)
                e = raised[w, p, :, i * length : (i + 1) * length]
                scores.append((e.astype(WIDE) * delta).astype(LOW))
            grad_q = (
                dot(
                    jnp.concatenate(scores, axis=1),
                    jnp.concatenate(split_heads(first, keys), axis=0),
                )
                * share
            )
            grad_k = dot(
                jnp.concatenate(scores, axis=0),
                jnp.concatenate(split_heads(first, queries), axis=0),
                0,
                0,
            )
            grad_v = dot(
                jnp.concatenate(
                    [raised[w, p, :, :length], raised[w, p, :, length:]], axis=0
                ),
                jnp.concatenate(split_heads(first, grad_scaled), axis=0),
                0,
                0,
            )
            triple_o[span, c] = grad_q.astype(LOW)
            triple_o[span, c_keys] = grad_k.astype(LOW)
            triple_o[span, c_values] = grad_v.astype(LOW)
    total = dot(triple_o[...], w_in[...], 1, 1)
    n, scale = normalize(load_rows(x, x_layout, windows, length).astype(WIDE))
    gain_o[...] += jnp.sum(total * n, axis=0, keepdims=True)
    shift_o[...] += jnp.sum(total, axis=0, keepdims=True)
    grad_x = (
        mid[...].astype(WIDE) + normalize_back(n, scale, gain[block, 0], total)
    ).astype(LOW)
    for w in range(windows):
        store_window(out, out_layout, w, length, grad_x[w * length : (w + 1) * length])


def whole(shape):
    return pl.BlockSpec(shape, lambda i: (0,) * len(shape), pipeline_mode=pl.Buffered(1))


def layer(shape, block):
    return pl.BlockSpec(
        (None,) + shape, lambda i: (block,) + (0,) * len(shape), pipeline_mode=pl.Buffered(1)
    )


def row_spec(rows, width, first):
    return pl.BlockSpec((rows, width), lambda i: (i + first, 0))


def stream_spec(array_shape, layout, rows, first):
    if layout == "rows":
        return row_spec(rows, array_shape[-1], first)
    parts, clips, frames, tokens, width = array_shape
    return pl.BlockSpec((parts, 1, frames, tokens, width), lambda i: (0, i + first, 0, 0, 0))


ANY = pl.BlockSpec(memory_space=pl.ANY)


def params():
    return pltpu.CompilerParams(vmem_limit_bytes=VMEM_BYTES)


def cost(flops, size, exps=0):
    return pl.CostEstimate(flops=int(flops), bytes_accessed=int(size), transcendentals=int(exps))


def forward(
    block, x, in_layout, cut_shape, out_layout, weights, counts, first, clips, all_clips, length, saved, x_first
):
    gain, shift, w_in, w_out, w_expand, b_expand, w_reduce = weights
    width, hidden = w_expand.shape[1:]
    parts, frames, tokens = cut_shape
    windows = frames
    rows = windows * length
    total = all_clips * rows
    out_shape = jax.ShapeDtypeStruct((parts, clips, frames, tokens, width), LOW)
    kept = [
        ((total, width), LOW),
        ((total, 3 * width), LOW),
        ((total, width), WIDE),
        ((all_clips * windows, width // PAIR, length, 2 * length), LOW),
        ((total, width), LOW),
        ((total, width), WIDE),
        ((total, width), LOW),
        ((total, hidden), LOW),
        ((total, hidden), LOW),
    ]
    out_specs = [stream_spec(out_shape.shape, out_layout, rows, 0)]
    for shape, unused in kept:
        if len(shape) == 2:
            out_specs.append(row_spec(rows, shape[1], first))
        else:
            out_specs.append(
                pl.BlockSpec((windows,) + shape[1:], lambda i: (i + first, 0, 0, 0))
            )
    saved = [] if saved is None else list(saved)
    dims = (
        block, windows, length, width, hidden, in_layout, out_layout, first, block == 1, len(saved)
    )
    ins = [counts, x, gain, shift, w_in, w_out, w_expand, b_expand, w_reduce]
    in_specs = [
        pl.BlockSpec(memory_space=pltpu.SMEM),
        stream_spec(x.shape, in_layout, rows, x_first),
        whole(gain.shape),
        whole(shift.shape),
        layer(w_in.shape[1:], block),
        layer(w_out.shape[1:], block),
        layer(w_expand.shape[1:], block),
        whole(b_expand.shape),
        layer(w_reduce.shape[1:], block),
    ]
    got = pl.pallas_call(
        functools.partial(forward_kernel, dims),
        grid=(clips,),
        in_specs=in_specs + [ANY] * len(saved),
        out_specs=out_specs,
        out_shape=[out_shape] + [jax.ShapeDtypeStruct(*k) for k in kept],
        input_output_aliases={len(ins) + i: 1 + i for i in range(len(saved))},
        compiler_params=params(),
        cost_estimate=cost(
            clips * rows * 2 * (4 + 2 * hidden // width) * width * width,
            clips * rows * 40 * width,
            clips * rows * 2 * hidden,
        ),
        name=f"forward_{block}",
    )(*ins, *saved)
    return got[0], got[1:]


def mlp_back(block, g, g_layout, weights, saved, length, windows):
    gain, shift, w_in, w_out, w_expand, b_expand, w_reduce = weights
    width, hidden = w_expand.shape[1:]
    rows = windows * length
    total = saved[5].shape[0]
    dims = (block, windows, length, width, hidden, g_layout, 0)
    shapes = [
        ((total, width), LOW),
        ((total, hidden), LOW),
        ((total, width), WIDE),
        ((1, hidden), WIDE),
        ((1, width), WIDE),
        ((1, width), WIDE),
    ]
    return pl.pallas_call(
        functools.partial(mlp_back_kernel, dims),
        grid=(total // rows,),
        in_specs=[
            stream_spec(g.shape, g_layout, rows, 0),
            row_spec(rows, hidden, 0),
            row_spec(rows, width, 0),
            whole(gain.shape),
            layer(w_expand.shape[1:], block),
            layer(w_reduce.shape[1:], block),
        ],
        out_specs=[row_spec(rows, s[1], 0) for s, unused in shapes[:3]]
        + [pl.BlockSpec(s, lambda i: (0, 0)) for s, unused in shapes[3:]],
        out_shape=[jax.ShapeDtypeStruct(*s) for s in shapes],
        compiler_params=params(),
        cost_estimate=cost(total * 4 * hidden * width, total * 16 * width),
        name=f"mlp_back_{block}",
    )(g, saved[8], saved[5], gain, w_expand, w_reduce)


def attention_back(block, x, x_layout, mid, out_shape, out_layout, weights, saved, length, windows):
    gain, shift, w_in, w_out, w_expand, b_expand, w_reduce = weights
    width = w_out.shape[1]
    rows = windows * length
    total = mid.shape[0]
    normed, triple, recip, raised, attended = saved[:5]
    dims = (block, windows, length, width, x_layout, out_layout, 0)
    return pl.pallas_call(
        functools.partial(attention_back_kernel, dims),
        grid=(total // rows,),
        in_specs=[
            stream_spec(x.shape, x_layout, rows, 0),
            row_spec(rows, width, 0),
            row_spec(rows, 3 * width, 0),
            row_spec(rows, width, 0),
            pl.BlockSpec((windows,) + raised.shape[1:], lambda i: (i, 0, 0, 0)),
            row_spec(rows, width, 0),
            whole(gain.shape),
            layer(w_in.shape[1:], block),
            layer(w_out.shape[1:], block),
        ],
        out_specs=[
            stream_spec(out_shape, out_layout, rows, 0),
            row_spec(rows, 3 * width, 0),
            pl.BlockSpec((1, width), lambda i: (0, 0)),
            pl.BlockSpec((1, width), lambda i: (0, 0)),
        ],
        out_shape=[
            jax.ShapeDtypeStruct(out_shape, LOW),
            jax.ShapeDtypeStruct((total, 3 * width), LOW),
            jax.ShapeDtypeStruct((1, width), WIDE),
            jax.ShapeDtypeStruct((1, width), WIDE),
        ],
        scratch_shapes=[pltpu.VMEM((rows, width), LOW)],
        compiler_params=params(),
        cost_estimate=cost(total * (8 * width * width + 10 * length * width * 2), total * 40 * width),
        name=f"attention_back_{block}",
    )(x, mid, triple, recip, raised, attended, gain, w_in, w_out)


def split_rows(value, same, send, keep):
    value = value.astype(LOW)
    pairs, length = keep.shape[0], keep.shape[1]
    for p in range(pairs):
        low = value[2 * p * length : (2 * p + 1) * length]
        high = value[(2 * p + 1) * length : (2 * p + 2) * length]
        keep[p] = jnp.where(same, low, high)
        send[p] = jnp.where(same, high, low)


def mlp_weights_kernel(core, active, grad, normed2, pre, send_r, keep_r, send_e, keep_e):
    same = core[0] == 0
    split_rows(dot(active[...], grad[...], 0, 0), same, send_r, keep_r)
    split_rows(dot(normed2[...], pre[...], 0, 0), same, send_e, keep_e)


def attention_weights_kernel(core, normed, triple, attended, mid, send, keep):
    same = core[0] == 0
    step = pl.program_id(0)
    last = pl.num_programs(0) - 1

    @pl.when(step < last)
    def _():
        split_rows(dot(normed[...], triple[...], 0, 0), same, send, keep)

    @pl.when(step == last)
    def _():
        split_rows(dot(attended[...], mid[...].astype(LOW), 0, 0), same, send, keep)


def mlp_weights(core, active, grad, normed2, pre, parts):
    total, width = grad.shape
    hidden = pre.shape[1]
    steps = hidden // width
    group = parts // steps
    reduce_rows, expand_rows = hidden // parts, width // parts
    reduce_spec = pl.BlockSpec((group // 2, reduce_rows, width), lambda i: (i, 0, 0))
    expand_spec = pl.BlockSpec((parts // 2, expand_rows, width), lambda i: (0, i, 0))
    reduce_shape = jax.ShapeDtypeStruct((parts // 2, reduce_rows, width), LOW)
    expand_shape = jax.ShapeDtypeStruct((parts // 2, steps * expand_rows, width), LOW)
    return pl.pallas_call(
        mlp_weights_kernel,
        grid=(steps,),
        in_specs=[
            pl.BlockSpec(memory_space=pltpu.SMEM),
            pl.BlockSpec((total, width), lambda i: (0, i)),
            whole((total, width)),
            whole((total, width)),
            pl.BlockSpec((total, width), lambda i: (0, i)),
        ],
        out_specs=[reduce_spec, reduce_spec, expand_spec, expand_spec],
        out_shape=[reduce_shape, reduce_shape, expand_shape, expand_shape],
        compiler_params=params(),
        cost_estimate=cost(4 * total * width * hidden, 4 * total * (width + hidden)),
        name="mlp_weights",
    )(core, active, grad, normed2, pre)


def attention_weights(core, normed, triple, attended, mid, parts):
    total, width = normed.shape
    steps = triple.shape[1] // width + 1
    rows = width // parts
    spec = pl.BlockSpec((parts // 2, rows, width), lambda i: (0, i, 0))
    shape = jax.ShapeDtypeStruct((parts // 2, steps * rows, width), LOW)
    return pl.pallas_call(
        attention_weights_kernel,
        grid=(steps,),
        in_specs=[
            pl.BlockSpec(memory_space=pltpu.SMEM),
            whole((total, width)),
            pl.BlockSpec((total, width), lambda i: (0, jnp.minimum(i, steps - 2))),
            whole((total, width)),
            whole((total, width)),
        ],
        out_specs=[spec, spec],
        out_shape=[shape, shape],
        compiler_params=params(),
        cost_estimate=cost(2 * total * width * width * steps, 16 * total * width),
        name="attention_weights",
    )(core, normed, triple, attended, mid)


def sum_parts(value):
    return jnp.sum(value.astype(WIDE), axis=0)


def swap_core(value):
    size = lax.axis_size("frame")
    return lax.ppermute(value, "frame", [(i, i ^ 1) for i in range(size)])


def across_frames(value):
    size = lax.axis_size("frame")
    groups = [list(range(parity, size, 2)) for parity in range(2)]
    return sum_parts(lax.all_to_all(value, "frame", 0, 0, axis_index_groups=groups)).astype(LOW)


def across_clips(value):
    size = lax.axis_size("clip")
    blocks = value.reshape(size, value.shape[0] // size, value.shape[1])
    mine = sum_parts(lax.all_to_all(blocks, "clip", 0, 0)).astype(LOW)
    return lax.all_to_all(jnp.broadcast_to(mine[None], blocks.shape), "clip", 0, 0).reshape(value.shape)


def reduce_groups(pairs):
    got = [swap_core(send) for send, unused in pairs]
    total = jnp.concatenate(
        [
            (keep.astype(WIDE) + other.astype(WIDE)).astype(LOW)
            for (unused, keep), other in zip(pairs, got)
        ],
        axis=1,
    )
    return across_clips(across_frames(total))


def exchange(value):
    return lax.all_to_all(value, "frame", 0, 0)


def local(
    tokens,
    frame_counts,
    norm_gain,
    norm_bias,
    project_in,
    project_out,
    expand_weight,
    expand_bias,
    reduce_weight,
    cotangent,
):
    clips, frames, length, width = tokens.shape
    hidden = expand_weight.shape[2]
    parts = lax.axis_size("frame")
    owned = length // parts
    cut = (parts, frames, owned)
    half = clips // 2
    weights = (
        norm_gain, norm_bias, project_in, project_out, expand_weight, expand_bias, reduce_weight
    )
    core = (lax.axis_index("frame") % 2).astype(jnp.int32).reshape(1)

    cotangent_tubes = exchange(
        cotangent.reshape(clips, frames, parts, owned, width).transpose(2, 0, 1, 3, 4)
    )
    rows = tokens.reshape(-1, width)
    saved0 = None
    boundary = []
    for start in (0, half):
        out, saved0 = forward(
            0, rows, "rows", cut, "frames", weights, frame_counts, start, half, clips, length, saved0, start
        )
        boundary.append(exchange(out))
    saved1 = None
    mixed = []
    for index, start in enumerate((0, half)):
        out, saved1 = forward(
            1, boundary[index], "tubes", cut, "tubes", weights, frame_counts, start, half, clips, length, saved1, 0
        )
        mixed.append(exchange(out))
    boundary_all = jnp.concatenate(boundary, axis=1)

    grads = {}
    small = {}

    def back(block, g, g_layout, x, x_layout, out_shape, out_layout, saved):
        g_rows, pre, mid, bias_sum, gain2, shift2 = mlp_back(
            block, g, g_layout, weights, saved, length, frames
        )
        send_r, keep_r, send_e, keep_e = mlp_weights(core, saved[7], g_rows, saved[6], pre, parts)
        grads["mlp", block] = ((send_r, keep_r), (send_e, keep_e))
        out, triple, gain1, shift1 = attention_back(
            block, x, x_layout, mid, out_shape, out_layout, weights, saved, length, frames
        )
        pair = attention_weights(core, saved[0], triple, saved[4], mid, parts)
        grads["attention", block] = (pair,)
        small[block] = jnp.concatenate(
            [
                v.reshape(parts, -1)
                for v in (gain1, gain2, shift1, shift2, bias_sum)
            ],
            axis=1,
        )
        return out

    cut_shape = (parts, clips, frames, owned, width)
    grad_boundary = exchange(
        back(1, cotangent_tubes, "tubes", boundary_all, "tubes", cut_shape, "tubes", saved1)
    )
    grad_tokens = back(0, grad_boundary, "frames", rows, "rows", rows.shape, "rows", saved0)

    summed = {key: reduce_groups(value) for key, value in grads.items()}
    small_rows = jnp.stack([small[0], small[1]], axis=1)
    small_sum = lax.psum(
        lax.psum_scatter(small_rows, "frame", scatter_dimension=0, tiled=True), "clip"
    )[0]
    part = width // parts
    norm_gain_grad = small_sum[:, : 2 * part].reshape(2, 2, part)
    norm_bias_grad = small_sum[:, 2 * part : 4 * part].reshape(2, 2, part)
    expand_bias_grad = small_sum[:, 4 * part :]

    def columns(value):
        return value.reshape(-1, part, width).transpose(1, 0, 2).reshape(part, -1)

    per_block = []
    for block in range(2):
        mlp, attention = summed["mlp", block], summed["attention", block]
        per_block.append(
            (
                columns(attention[: 3 * part]),
                attention[3 * part :],
                columns(mlp[hidden // parts :]),
                mlp[: hidden // parts],
            )
        )
    stacked = [jnp.stack(pair).astype(WIDE) for pair in zip(*per_block)]
    mixed_all = (
        jnp.concatenate(mixed, axis=1).transpose(1, 2, 0, 3, 4).reshape(tokens.shape)
    )
    return (
        mixed_all,
        grad_tokens.reshape(tokens.shape),
        norm_gain_grad,
        norm_bias_grad,
        stacked[0],
        stacked[1],
        stacked[2],
        expand_bias_grad,
        stacked[3],
    )


def solution(mesh):
    in_specs = (
        P("clip", "frame", None, None),
        P("clip"),
        P(),
        P(),
        P(),
        P(),
        P(),
        P(),
        P(),
        P("clip", "frame", None, None),
    )
    out_specs = (
        P("clip", "frame", None, None),
        P("clip", "frame", None, None),
        P(None, None, "frame"),
        P(None, None, "frame"),
        P(None, "frame", None),
        P(None, "frame", None),
        P(None, "frame", None),
        P(None, "frame"),
        P(None, "frame", None),
    )
    return jax.shard_map(local, mesh=mesh, in_specs=in_specs, out_specs=out_specs, check_vma=False)
```

```python
import functools

import jax
import jax.numpy as jnp
from jax import lax
from jax.experimental import pallas as pl
from jax.experimental.pallas import tpu as pltpu
from jax.sharding import PartitionSpec as P

HEAD_DIM = 64
TUBE = 16
PAIR = 2 * HEAD_DIM
EPSILON = 1e-05
HALF_ROOT = 0.7071067811865476
BELL_PEAK = 0.3989422804014327
LOW = jnp.bfloat16
WIDE = jnp.float32
VMEM_BYTES = 63 * 1024 * 1024
SMALL_ROWS = 16


def dot(left, right, left_dim=1, right_dim=0):
    return lax.dot_general(
        left, right, (((left_dim,), (right_dim,)), ((), ())), preferred_element_type=WIDE
    )


def normalize(x):
    center = x - jnp.mean(x, axis=-1, keepdims=True)
    scale = lax.rsqrt(jnp.mean(center * center, axis=-1, keepdims=True) + EPSILON)
    return center * scale, scale


def normalize_back(n, scale, gain, grad):
    e = grad * gain
    return scale * (
        e - jnp.mean(e, axis=-1, keepdims=True) - n * jnp.mean(e * n, axis=-1, keepdims=True)
    )


def chunks(total, size):
    return [slice(start, start + size) for start in range(0, total, size)]


def split_heads(first, value):
    zero = jnp.zeros_like(value)
    return jnp.where(first, value, zero), jnp.where(first, zero, value)


def load_window(ref, layout, window):
    if layout == "tokens":
        return ref[0, window]
    if layout == "frames":
        block = ref[:, 0, window]
    else:
        block = ref[:, 0, :, window * TUBE : (window + 1) * TUBE, :]
    return block.reshape(-1, block.shape[-1])


def load_rows(ref, layout, windows):
    if layout == "rows":
        return ref[...]
    return jnp.concatenate([load_window(ref, layout, w) for w in range(windows)], axis=0)


def store_window(ref, layout, window, value):
    if layout == "tokens":
        ref[0, window] = value
    elif layout == "frames":
        ref[:, 0, window] = value.reshape(ref.shape[0], -1, ref.shape[-1])
    else:
        tube = slice(window * TUBE, (window + 1) * TUBE)
        ref[:, 0, :, tube, :] = value.reshape(ref.shape[0], -1, TUBE, ref.shape[-1])


def store_rows(ref, layout, windows, value):
    length = value.shape[0] // windows
    for w in range(windows):
        store_window(ref, layout, w, value[w * length : (w + 1) * length])


def forward_kernel(dims, counts, x, *refs):
    block, windows, length, width, hidden, n_alias, first_clip, passes = dims
    if block == 0:
        cotangent, refs = refs[0], refs[1:]
    gain, shift, w_in, w_out, w_expand, b_expand, w_reduce = refs[:7]
    refs = refs[7 + n_alias :]
    if passes:
        refs = refs[1:]
    if block == 0:
        out, *refs = refs
    normed_o, triple_o, recip_o, raised_o, attended_o, middle_o, normed2_o, active_o, slope_o, extra_o = refs
    stream = load_rows(x, ("tokens", "tubes")[block], windows)
    if block == 0:
        for w in range(windows):
            store_window(extra_o, "frames", w, load_window(cotangent, "tokens", w))
    else:
        extra_o[...] = stream
    stream = stream.astype(WIDE)
    n, unused = normalize(stream)
    normed_o[...] = (n * gain[block, 0] + shift[block, 0]).astype(LOW)
    for c in chunks(3 * width, width):
        triple_o[:, c] = dot(normed_o[...], w_in[:, c]).astype(LOW)
    first = lax.broadcasted_iota(jnp.int32, (length, PAIR), 1) < HEAD_DIM
    ones_a, ones_b = split_heads(first, jnp.ones((length, PAIR), LOW))
    if block == 1:
        key = lax.broadcasted_iota(jnp.int32, (1, length), 1)
        kept = key // TUBE < counts[first_clip + pl.program_id(0)]
        bias = jnp.where(kept, 0.0, -1e30).astype(WIDE)
    for w in range(windows):
        span = slice(w * length, (w + 1) * length)
        for p, c in enumerate(chunks(width, PAIR)):
            queries = triple_o[span, c] * LOW(HEAD_DIM**-0.5)
            keys = triple_o[span, c.start + width : c.stop + width]
            values = triple_o[span, c.start + 2 * width : c.stop + 2 * width]
            raised = []
            for q in split_heads(first, queries):
                scores = dot(q, keys, 1, 1)
                if block == 1:
                    scores = scores + bias
                raised.append(
                    jnp.exp(scores - jnp.max(scores, axis=1, keepdims=True)).astype(LOW)
                )
            raised = jnp.concatenate(raised, axis=1)
            raised_o[w, p] = raised
            values_a, values_b = split_heads(first, values)
            sums = dot(
                raised,
                jnp.concatenate(
                    [
                        jnp.concatenate([values_a, ones_a], axis=1),
                        jnp.concatenate([values_b, ones_b], axis=1),
                    ],
                    axis=0,
                ),
            )
            recip = 1.0 / sums[:, PAIR:]
            recip_o[span, c] = recip
            attended_o[span, c] = (sums[:, :PAIR] * recip).astype(LOW)
    middle = stream + dot(attended_o[...], w_out[...])
    middle_o[...] = middle
    n, unused = normalize(middle)
    normed2_o[...] = (n * gain[block, 1] + shift[block, 1]).astype(LOW)
    total = middle
    for c in chunks(hidden, 512):
        pre = dot(normed2_o[...], w_expand[:, c]) + b_expand[block : block + 1, c]
        below = 0.5 + 0.5 * lax.erf(pre * HALF_ROOT)
        active = (pre * below).astype(LOW)
        active_o[:, c] = active
        slope_o[:, c] = (below + pre * (BELL_PEAK * jnp.exp(-0.5 * pre * pre))).astype(LOW)
        if block == 0:
            total = total + dot(active, w_reduce[c, :])
    if block == 0:
        store_rows(out, "frames", windows, total.astype(LOW))


def output_kernel(windows, active, middle, w_reduce, *refs):
    total = middle[...] + dot(active[...], w_reduce[...])
    store_rows(refs[-1], "tubes", windows, total.astype(LOW))


def mlp_back_kernel(dims, *refs):
    block, windows, width, hidden = dims
    g, slope, middle, gain, w_expand, w_reduce = refs[:6]
    rows_o, pre_o, mid_o, bias_o, gain_o, shift_o = refs[-6:]
    grad = load_rows(g, ("frames", "tubes")[block], windows)
    rows_o[...] = grad

    @pl.when(pl.program_id(0) == 0)
    def _():
        bias_o[...] = jnp.zeros_like(bias_o)
        gain_o[...] = jnp.zeros_like(gain_o)
        shift_o[...] = jnp.zeros_like(shift_o)

    total = None
    for c in chunks(hidden, 512):
        pre = (dot(grad, w_reduce[c, :], 1, 1) * slope[:, c].astype(WIDE)).astype(LOW)
        pre_o[:, c] = pre
        bias_o[:, c] += jnp.sum(pre.astype(WIDE), axis=0, keepdims=True)
        part = dot(pre, w_expand[:, c], 1, 1)
        total = part if total is None else total + part
    n, scale = normalize(middle[...])
    gain_o[...] += jnp.sum(total * n, axis=0, keepdims=True)
    shift_o[...] += jnp.sum(total, axis=0, keepdims=True)
    mid_o[...] = grad.astype(WIDE) + normalize_back(n, scale, gain[block, 1], total)


def attention_back_kernel(dims, *refs):
    block, windows, length, width = dims
    mid, triple, recip, raised, attended, w_out = refs[:6]
    if block == 0:
        triple_o, grad_s = refs[-2:]
    else:
        triple_o, grad_s = refs[-5], refs[-1]
    grad_s[...] = dot(mid[...].astype(LOW), w_out[...], 1, 1).astype(LOW)
    first = lax.broadcasted_iota(jnp.int32, (length, PAIR), 1) < HEAD_DIM
    minus = jnp.full((length, PAIR), -1.0, LOW)
    root = HEAD_DIM**-0.5
    for w in range(windows):
        span = slice(w * length, (w + 1) * length)
        for p, c in enumerate(chunks(width, PAIR)):
            c_keys = slice(c.start + width, c.stop + width)
            c_values = slice(c.start + 2 * width, c.stop + 2 * width)
            grad = grad_s[span, c]
            grad_wide = grad.astype(WIDE)
            share = recip[span, c]
            inner = (grad_wide * attended[span, c].astype(WIDE)).astype(LOW)
            grad_scaled = (grad_wide * share).astype(LOW)
            queries = (triple[span, c].astype(WIDE) * (share * root)).astype(LOW)
            keys = triple[span, c_keys] * LOW(root)
            values = jnp.concatenate([triple[span, c_values], minus], axis=1)
            scores = []
            for i, (a, b) in enumerate(zip(split_heads(first, grad), split_heads(first, inner))):
                delta = dot(jnp.concatenate([a, b], axis=1), values, 1, 1)
                e = raised[w, p, :, i * length : (i + 1) * length]
                scores.append((e.astype(WIDE) * delta).astype(LOW))
            grad_q = (
                dot(
                    jnp.concatenate(scores, axis=1),
                    jnp.concatenate(split_heads(first, keys), axis=0),
                )
                * share
            )
            grad_k = dot(
                jnp.concatenate(scores, axis=0),
                jnp.concatenate(split_heads(first, queries), axis=0),
                0,
                0,
            )
            grad_v = dot(
                jnp.concatenate([raised[w, p, :, :length], raised[w, p, :, length:]], axis=0),
                jnp.concatenate(split_heads(first, grad_scaled), axis=0),
                0,
                0,
            )
            triple_o[span, c] = grad_q.astype(LOW)
            triple_o[span, c_keys] = grad_k.astype(LOW)
            triple_o[span, c_values] = grad_v.astype(LOW)
    if block == 1:
        x, gain, w_in = refs[6:9]
        stream_back(block, windows, "rows", "tubes", x, mid, triple_o, gain, w_in, *refs[-4:-1])


def stream_back(block, windows, x_layout, layout, x, mid, triple, gain, w_in, gain_o, shift_o, out):
    @pl.when(pl.program_id(0) == 0)
    def _():
        gain_o[...] = jnp.zeros_like(gain_o)
        shift_o[...] = jnp.zeros_like(shift_o)

    total = dot(triple[...], w_in[...], 1, 1)
    n, scale = normalize(load_rows(x, x_layout, windows).astype(WIDE))
    gain_o[...] += jnp.sum(total * n, axis=0, keepdims=True)
    shift_o[...] += jnp.sum(total, axis=0, keepdims=True)
    grad_x = (mid[...] + normalize_back(n, scale, gain[block, 0], total)).astype(LOW)
    store_rows(out, layout, windows, grad_x)


def finish_kernel(windows, x, mid, triple, gain, w_in, mixed, *refs):
    gain_o, shift_o, out, mixed_o = refs[-4:]
    stream_back(0, windows, "tokens", "tokens", x, mid, triple, gain, w_in, gain_o, shift_o, out)
    for w in range(windows):
        store_window(mixed_o, "tokens", w, load_window(mixed, "frames", w))


def split_rows(value, place, send, keep):
    value = value.astype(LOW)
    pairs, length = keep.shape[0], keep.shape[1]
    same = place % 2 == 0
    for p in range(pairs):
        low = value[2 * p * length : (2 * p + 1) * length]
        high = value[(2 * p + 1) * length : (2 * p + 2) * length]
        slot = (place // 2 % pairs) ^ p
        keep[slot] = jnp.where(same, low, high)
        send[slot] = jnp.where(same, high, low)


def outer_kernel(has_last, is_split, place, left, right, *refs):
    place = place[0]
    step = pl.program_id(0)
    outs = refs[-2:] if is_split else refs[-1:]

    def store(value):
        if is_split:
            split_rows(value, place, *outs)
        else:
            outs[0][...] = value.astype(LOW).reshape(outs[0].shape)

    if not has_last:
        store(dot(left[...], right[...], 0, 0))
        return
    last = pl.num_programs(0) - 1

    @pl.when(step < last)
    def _():
        store(dot(left[...], right[...], 0, 0))

    @pl.when(step == last)
    def _():
        store(dot(refs[0][...], refs[1][...].astype(LOW), 0, 0))


def whole(shape):
    return pl.BlockSpec(shape, lambda i: (0,) * len(shape), pipeline_mode=pl.Buffered(1))


def layer(shape, block):
    return pl.BlockSpec(
        (None,) + shape, lambda i: (block,) + (0,) * len(shape), pipeline_mode=pl.Buffered(1)
    )


def clip_spec(shape, first=0):
    if len(shape) == 2:
        return pl.BlockSpec(shape, lambda i: (i + first, 0))
    if len(shape) == 3:
        return pl.BlockSpec((1,) + shape, lambda i: (i + first, 0, 0, 0))
    return pl.BlockSpec(
        (shape[0], 1) + shape[1:], lambda i: (0, i + first) + (0,) * (len(shape) - 1)
    )


def all_clips(shape, clips):
    if len(shape) == 2:
        return (clips * shape[0], shape[1])
    if len(shape) == 3:
        return (clips,) + shape
    return (shape[0], clips) + shape[1:]


ANY = pl.BlockSpec(memory_space=pl.ANY)
SCALARS = pl.BlockSpec(memory_space=pltpu.SMEM)


def params():
    return pltpu.CompilerParams(vmem_limit_bytes=VMEM_BYTES)


def cost(micros):
    return pl.CostEstimate(
        flops=int(micros * 350000000), bytes_accessed=int(micros * 1050000), transcendentals=0
    )


def sizes(weights, shapes):
    width, hidden = weights[4].shape[1:]
    clips, windows, length, parts = shapes
    return clips, windows, length, parts, windows * length, width, hidden


def forward(block, counts, x, cotangent, weights, saved, first, shapes, through=None):
    gain, shift, w_in, w_out, w_expand, b_expand, w_reduce = weights
    clips, windows, length, parts, rows, width, hidden = sizes(weights, shapes)
    steps = clips // 2
    travel = (parts, windows, length // parts, width)
    raised = (windows, width // PAIR, length, 2 * length)
    kept = [
        (rows, width), (rows, 3 * width), (rows, width), raised, (rows, width),
        (rows, width), (rows, width), (rows, hidden), (rows, hidden),
        travel if block == 0 else (rows, width),
    ]
    types = [LOW, LOW, WIDE, LOW, LOW, WIDE, LOW, LOW, LOW, LOW]
    specs, outs = [], []
    for index, (shape, kind) in enumerate(zip(kept, types)):
        if index == 3:
            specs.append(pl.BlockSpec(shape, lambda i: (i + first, 0, 0, 0)))
            outs.append(jax.ShapeDtypeStruct((clips * windows,) + shape[1:], kind))
        else:
            specs.append(clip_spec(shape, first))
            outs.append(jax.ShapeDtypeStruct(all_clips(shape, clips), kind))
    if block == 0:
        specs = [clip_spec(travel)] + specs
        outs = [jax.ShapeDtypeStruct(all_clips(travel, steps), LOW)] + outs
        ins = [counts, x, cotangent]
        in_specs = [SCALARS] + [clip_spec(v.shape[1:], first) for v in ins[1:]]
    else:
        ins = [counts, x]
        in_specs = [SCALARS, clip_spec(travel)]
    alias = [] if saved is None else list(saved)
    base = 1 if block == 0 else 0
    if through is not None:
        specs = [ANY] + specs
        outs = [jax.ShapeDtypeStruct(through.shape, through.dtype)] + outs
        alias = [through] + alias
    ins += weights
    in_specs += [
        whole(gain.shape),
        whole(shift.shape),
        layer(w_in.shape[1:], block),
        layer(w_out.shape[1:], block),
        layer(w_expand.shape[1:], block),
        whole(b_expand.shape),
        layer(w_reduce.shape[1:], block),
    ]
    dims = (block, windows, length, width, hidden, len(alias), first, through is not None)
    got = pl.pallas_call(
        functools.partial(forward_kernel, dims),
        grid=(steps,),
        in_specs=in_specs + [ANY] * len(alias),
        out_specs=specs,
        out_shape=outs,
        input_output_aliases={len(ins) + i: base + i for i in range(len(alias))},
        compiler_params=params(),
        cost_estimate=cost(36 if block == 0 else 30),
        name=f"forward_{block}",
    )(*ins, *alias)
    if block == 0 or through is not None:
        return got[0], got[1:]
    return got


def output(active, middle, weights, shapes, through):
    clips, windows, length, parts, rows, width, hidden = sizes(weights, shapes)
    travel = (parts, windows, length // parts, width)
    return pl.pallas_call(
        functools.partial(output_kernel, windows),
        grid=(clips,),
        in_specs=[
            clip_spec((rows, hidden)),
            clip_spec((rows, width)),
            layer(weights[6].shape[1:], 1),
        ]
        + [ANY],
        out_specs=[ANY, clip_spec(travel)],
        out_shape=[
            jax.ShapeDtypeStruct(through.shape, through.dtype),
            jax.ShapeDtypeStruct(all_clips(travel, clips), LOW),
        ],
        input_output_aliases={3: 0},
        compiler_params=params(),
        cost_estimate=cost(14),
        name="output",
    )(active, middle, weights[6], through)


def mlp_back(block, g, slope, middle, weights, shapes, through=()):
    gain, shift, w_in, w_out, w_expand, b_expand, w_reduce = weights
    clips, windows, length, parts, rows, width, hidden = sizes(weights, shapes)
    travel = (parts, windows, length // parts, width)
    kinds = [
        ((rows, width), LOW), ((rows, hidden), LOW), ((rows, width), WIDE),
        ((1, hidden), WIDE), ((1, width), WIDE), ((1, width), WIDE),
    ]
    return pl.pallas_call(
        functools.partial(mlp_back_kernel, (block, windows, width, hidden)),
        grid=(clips,),
        in_specs=[
            clip_spec(travel),
            clip_spec((rows, hidden)),
            clip_spec((rows, width)),
            whole(gain.shape),
            layer(w_expand.shape[1:], block),
            layer(w_reduce.shape[1:], block),
        ]
        + [ANY] * len(through),
        out_specs=[ANY] * len(through)
        + [clip_spec(s) for s, unused in kinds[:3]]
        + [pl.BlockSpec(s, lambda i: (0, 0)) for s, unused in kinds[3:]],
        out_shape=[jax.ShapeDtypeStruct(v.shape, v.dtype) for v in through]
        + [jax.ShapeDtypeStruct(all_clips(s, clips), k) for s, k in kinds[:3]]
        + [jax.ShapeDtypeStruct(s, k) for s, k in kinds[3:]],
        input_output_aliases={6 + i: i for i in range(len(through))},
        compiler_params=params(),
        cost_estimate=cost(100),
        name=f"mlp_back_{block}",
    )(g, slope, middle, gain, w_expand, w_reduce, *through)


def attention_back(block, x, mid, triple, recip, raised, attended, weights, shapes, after=()):
    gain, shift, w_in, w_out, w_expand, b_expand, w_reduce = weights
    clips, windows, length, parts, rows, width, hidden = sizes(weights, shapes)
    travel = (parts, windows, length // parts, width)
    ins = [mid, triple, recip, raised, attended, w_out]
    in_specs = [
        clip_spec((rows, width)),
        clip_spec((rows, 3 * width)),
        clip_spec((rows, width)),
        pl.BlockSpec((windows,) + raised.shape[1:], lambda i: (i, 0, 0, 0)),
        clip_spec((rows, width)),
        layer(w_out.shape[1:], block),
    ]
    out_specs = [clip_spec((rows, 3 * width))]
    out_shape = [jax.ShapeDtypeStruct((clips * rows, 3 * width), LOW)]
    if block == 1:
        ins += [x, gain, w_in]
        in_specs += [clip_spec((rows, width)), whole(gain.shape), layer(w_in.shape[1:], block)]
        out_specs += [pl.BlockSpec((1, width), lambda i: (0, 0))] * 2 + [clip_spec(travel)]
        out_shape += [jax.ShapeDtypeStruct((1, width), WIDE)] * 2
        out_shape += [jax.ShapeDtypeStruct(all_clips(travel, clips), LOW)]
    return pl.pallas_call(
        functools.partial(attention_back_kernel, (block, windows, length, width)),
        grid=(clips,),
        in_specs=in_specs + [ANY] * len(after),
        out_specs=out_specs,
        out_shape=out_shape,
        scratch_shapes=[pltpu.VMEM((rows, width), LOW)],
        compiler_params=params(),
        cost_estimate=cost(42 if block else 30),
        name=f"attention_back_{block}",
    )(*ins, *after)


def finish(x, mid, triple, mixed, weights, shapes, through, after=()):
    gain, shift, w_in, w_out, w_expand, b_expand, w_reduce = weights
    clips, windows, length, parts, rows, width, hidden = sizes(weights, shapes)
    travel = (parts, windows, length // parts, width)
    tokens = (windows, length, width)
    sums = jax.ShapeDtypeStruct((1, width), WIDE)
    sums_spec = pl.BlockSpec((1, width), lambda i: (0, 0))
    return pl.pallas_call(
        functools.partial(finish_kernel, windows),
        grid=(clips,),
        in_specs=[
            clip_spec(tokens),
            clip_spec((rows, width)),
            clip_spec((rows, 3 * width)),
            whole(gain.shape),
            layer(w_in.shape[1:], 0),
            clip_spec(travel),
            ANY,
        ]
        + [ANY] * len(after),
        out_specs=[ANY, sums_spec, sums_spec, clip_spec(tokens), clip_spec(tokens)],
        out_shape=[jax.ShapeDtypeStruct(through.shape, through.dtype), sums, sums]
        + [jax.ShapeDtypeStruct(all_clips(tokens, clips), LOW)] * 2,
        input_output_aliases={6: 0},
        compiler_params=params(),
        cost_estimate=cost(15),
        name="finish",
    )(x, mid, triple, gain, w_in, mixed, through, *after)


def outer_rows(place, active, grad, parts, is_split, into=None, after=()):
    total, width = grad.shape
    hidden = active.shape[1]
    steps = hidden // width
    group = parts // steps
    rows = hidden // parts
    if is_split:
        half = group // 2
        spec = pl.BlockSpec((half, rows, width), lambda i, place: (i ^ (place[0] // 2 // half), 0, 0))
        shape = jax.ShapeDtypeStruct((parts // 2, rows, width), LOW)
    else:
        spec = pl.BlockSpec((group, rows, width), lambda i, place: (i, 0, 0))
        shape = jax.ShapeDtypeStruct(into.shape, LOW)
    alias = [] if into is None else [into]
    arrays = 2 if is_split else 1
    return pl.pallas_call(
        functools.partial(outer_kernel, False, is_split),
        grid_spec=pltpu.PrefetchScalarGridSpec(
            num_scalar_prefetch=1,
            grid=(steps,),
            in_specs=[
                pl.BlockSpec((total, width), lambda i, place: (0, i)),
                pl.BlockSpec(
                    (total, width), lambda i, place: (0, 0), pipeline_mode=pl.Buffered(1)
                ),
            ]
            + [ANY] * (len(alias) + len(after)),
            out_specs=[spec] * arrays,
        ),
        out_shape=[shape] * arrays,
        input_output_aliases={3: 0} if alias else {},
        compiler_params=params(),
        cost_estimate=cost(14),
        name="outer_rows",
    )(place, active, grad, *alias, *after)


def outer_columns(place, left, right, last, parts, is_split, after=(), skip=0):
    total, width = left.shape
    steps = right.shape[1] // width
    blocks = steps + (1 if last else 0)
    ins = [place, left, right, *last]
    in_specs = [
        SCALARS,
        whole((total, width)),
        pl.BlockSpec((total, width), lambda i: (0, jnp.minimum(i, steps - 1))),
    ]
    in_specs += [whole((total, width))] * len(last)
    owners, arrays = (parts // 2, 2) if is_split else (parts, 1)
    spec = pl.BlockSpec((owners, width // parts, width), lambda i: (0, i + skip, 0))
    shape = jax.ShapeDtypeStruct((owners, (blocks + skip) * width // parts, width), LOW)
    return pl.pallas_call(
        functools.partial(outer_kernel, bool(last), is_split),
        grid=(blocks,),
        in_specs=in_specs + [ANY] * len(after),
        out_specs=[spec] * arrays,
        out_shape=[shape] * arrays,
        compiler_params=params(),
        cost_estimate=cost(4 * blocks),
        name="outer_columns",
    )(*ins, *after)


def add_all(values):
    total = values[0].astype(WIDE)
    for value in values[1:]:
        total = total + value.astype(WIDE)
    return total.astype(LOW)


def swap(value, axis, offset):
    return lax.ppermute(
        value, axis, [(i, i ^ offset) for i in range(lax.axis_size(axis))]
    )


def sum_frames(send, keep, reverse):
    bits = (lax.axis_size("frame") // 2).bit_length() - 1
    shape = (2,) * bits + keep.shape[1:]
    terms = [keep.reshape(shape), swap(send, "frame", 1).reshape(shape)]
    order = list(range(1, bits + 1))
    if reverse:
        order = order[::-1]
    left = list(range(bits, 0, -1))
    for bit in order:
        axis = left.index(bit)
        left.remove(bit)
        far = add_all([lax.index_in_dim(t, 1, axis, keepdims=False) for t in terms])
        yield far
        terms = [lax.index_in_dim(t, 0, axis, keepdims=False) for t in terms]
        terms.append(swap(far, "frame", 1 << bit))
    yield add_all(terms)


def last_of(steps):
    for value in steps:
        pass
    return value


def sum_clips(total, small):
    size = lax.axis_size("clip")
    rows = -(-total.shape[0] // (16 * size)) * 16
    blocks = jnp.pad(total, ((0, rows * size - total.shape[0]), (0, 0)))
    blocks = blocks.reshape(size, rows, total.shape[1])
    sent = blocks
    if small is not None:
        small = jnp.broadcast_to(small[None], (size,) + small.shape)
        sent = jnp.concatenate([blocks, small], axis=1)
    got = lax.all_to_all(sent, "clip", 0, 0)
    mine = add_all([v[:rows] for v in got])
    if small is not None:
        small = jnp.sum(got[:, rows:].astype(WIDE), axis=0)
    everything = lax.all_to_all(jnp.broadcast_to(mine[None], blocks.shape), "clip", 0, 0)
    return everything.reshape(size * rows, -1), small


def gather_kernel(block, plan, n_in, n_outs, *refs):
    sources, outs = refs[: len(plan)], refs[n_in : n_in + n_outs]
    for source, group in zip(sources, plan):
        width = source.shape[1]
        start = 0
        for out, columns in group:
            length = outs[out].shape[1]
            for c in range(columns):
                outs[out][0, :, c * width : (c + 1) * width] = source[
                    start : start + length, :
                ].astype(WIDE)
                start += length


def gather(block, sources, plan, outs, through):
    filled = not isinstance(outs[0], jax.ShapeDtypeStruct)
    extra = list(outs) if filled else []
    passed = [] if through is None else [through]
    specs = [
        pl.BlockSpec((1,) + v.shape[1:], lambda i: (block, 0, 0)) for v in outs
    ]
    ins = [*sources, *extra, *passed]
    aliases = {len(sources) + i: i for i in range(len(extra))}
    if passed:
        aliases[len(ins) - 1] = len(outs)
    return pl.pallas_call(
        functools.partial(gather_kernel, block, plan, len(ins), len(outs)),
        grid=(1,),
        in_specs=[whole(v.shape) for v in sources] + [ANY] * (len(extra) + len(passed)),
        out_specs=specs + [ANY] * len(passed),
        out_shape=[jax.ShapeDtypeStruct(v.shape, v.dtype) for v in [*outs, *passed]],
        input_output_aliases=aliases,
        compiler_params=params(),
        cost_estimate=cost(4),
        name="gather",
    )(*ins)


def exchange(value):
    return lax.all_to_all(value, "frame", 0, 0)


def local(
    tokens,
    frame_counts,
    norm_gain,
    norm_bias,
    project_in,
    project_out,
    expand_weight,
    expand_bias,
    reduce_weight,
    cotangent,
):
    clips, frames, length, width = tokens.shape
    hidden = expand_weight.shape[2]
    parts = lax.axis_size("frame")
    part = width // parts
    shapes = (clips, frames, length, parts)
    half = clips // 2
    weights = (
        norm_gain, norm_bias, project_in, project_out, expand_weight, expand_bias, reduce_weight
    )
    place = lax.axis_index("frame").astype(jnp.int32).reshape(1)

    out, saved0 = forward(0, frame_counts, tokens, cotangent, weights, None, 0, shapes)
    boundary_a = exchange(out)
    out, saved0 = forward(0, frame_counts, tokens, cotangent, weights, saved0, half, shapes)
    boundary_b = exchange(out)
    cotangent_tubes, saved1 = forward(
        1, frame_counts, boundary_a, None, weights, None, 0, shapes, saved0[9]
    )
    cotangent_tubes = exchange(cotangent_tubes)
    saved1 = forward(1, frame_counts, boundary_b, None, weights, saved1, half, shapes)

    def scatter(value):
        return lax.psum_scatter(value, "frame", scatter_dimension=0, tiled=True)[0]

    normed, triple, recip, raised, attended, middle, normed2, active, slope, stream = saved1
    rows1, pre, mid, bias1, gain12, shift12 = mlp_back(
        1, cotangent_tubes, slope, middle, weights, shapes
    )
    columns = hidden // width
    (mlp1,) = outer_columns(place, normed2, pre, [], parts, False, [], columns)
    (mlp1,) = outer_rows(place, active, rows1, parts, False, mlp1)
    mlp1_scattered = scatter(mlp1)
    grad_triple, gain11, shift11, grad_boundary = attention_back(
        1, stream, mid, triple, recip, raised, attended, weights, shapes, [mlp1]
    )
    grad_boundary = exchange(grad_boundary)
    (attention1,) = outer_columns(
        place, normed, grad_triple, [attended, mid], parts, False
    )
    attention1, mixed = output(active, middle, weights, shapes, attention1)
    attention1_scattered = scatter(attention1)

    normed, triple, recip, raised, attended, middle, normed2, active, slope = saved0[:9]
    mixed, rows0, pre, mid, bias0, gain02, shift02 = mlp_back(
        0, grad_boundary, slope, middle, weights, shapes, [mixed]
    )
    mixed = exchange(mixed)
    mlp1_sum, attention1_sum = lax.psum((mlp1_scattered, attention1_scattered), "clip")
    reduce0 = outer_rows(place, active, rows0, parts, True, None, [mlp1_scattered])
    expand0 = outer_columns(place, normed2, pre, [], parts, True, [reduce0[0]])
    (grad_triple,) = attention_back(
        0, None, mid, triple, recip, raised, attended, weights, shapes, [expand0[0]]
    )
    steps_c, steps_d = sum_frames(*reduce0, False), sum_frames(*expand0, True)
    sent = [next(steps_c), next(steps_d)]
    attention0 = outer_columns(
        place, normed, grad_triple, [attended, mid], parts, True, [*sent, attention1_scattered]
    )
    send, gain01, shift01, grad_tokens, mixed = finish(
        tokens, mid, grad_triple, mixed, weights, shapes, attention0[0]
    )
    cut = send.shape[1] // 2
    steps_a = sum_frames(send[:, :cut], attention0[1][:, :cut], False)
    steps_b = sum_frames(send[:, cut:], attention0[1][:, cut:], True)

    def by_owner(*values):
        return jnp.concatenate([v.reshape(parts, -1) for v in values], axis=1)

    small = by_owner(
        gain01, gain02, shift01, shift02, bias0, gain11, gain12, shift11, shift12, bias1
    ).astype(LOW)
    count = small.shape[1]
    small = jnp.pad(small, ((0, 0), (0, SMALL_ROWS * width - count)))
    small = add_all(list(exchange(small.reshape(parts, SMALL_ROWS, width))))
    last = jnp.concatenate([last_of(steps_a), last_of(steps_b)], axis=0)
    outs = [
        (2, hidden // parts, width),
        (2, part, hidden),
        (2, part, 3 * width),
        (2, part, width),
    ]
    outs = [jax.ShapeDtypeStruct(v, WIDE) for v in outs]
    mlp_plan = ((0, 1), (1, columns))
    attention_plan = ((2, 3), (3, 1))
    mlp0_sum = jnp.concatenate([last_of(steps_c), last_of(steps_d)], axis=0)
    outs = gather(1, [mlp1_sum, attention1_sum], (mlp_plan, attention_plan), outs, mlp0_sum)
    *outs, mlp0_sum = outs
    mlp0_sum, unused = sum_clips(mlp0_sum, None)
    attention0_sum, small = sum_clips(last, small)
    small = small.reshape(-1)[:count].reshape(2, -1)
    grad_reduce, grad_expand, grad_in, grad_out = gather(
        0, [mlp0_sum, attention0_sum], (mlp_plan, attention_plan), outs, None
    )
    return (
        mixed,
        grad_tokens,
        small[:, : 2 * part].reshape(2, 2, part),
        small[:, 2 * part : 4 * part].reshape(2, 2, part),
        grad_in,
        grad_out,
        grad_expand,
        small[:, 4 * part :],
        grad_reduce,
    )


def solution(mesh):
    in_specs = (
        P("clip", "frame", None, None),
        P("clip"),
        P(),
        P(),
        P(),
        P(),
        P(),
        P(),
        P(),
        P("clip", "frame", None, None),
    )
    out_specs = (
        P("clip", "frame", None, None),
        P("clip", "frame", None, None),
        P(None, None, "frame"),
        P(None, None, "frame"),
        P(None, "frame", None),
        P(None, "frame", None),
        P(None, "frame", None),
        P(None, "frame"),
        P(None, "frame", None),
    )
    return jax.shard_map(local, mesh=mesh, in_specs=in_specs, out_specs=out_specs, check_vma=False)
```

```python
import functools

import jax
import jax.numpy as jnp
from jax import lax
from jax.experimental import pallas as pl
from jax.experimental.pallas import tpu as pltpu
from jax.sharding import PartitionSpec as P

HEAD_DIM = 64
TUBE = 16
PAIR = 2 * HEAD_DIM
EPSILON = 1e-05
HALF_ROOT = 0.7071067811865476
BELL_PEAK = 0.3989422804014327
LOW = jnp.bfloat16
WIDE = jnp.float32
VMEM_BYTES = 63 * 1024 * 1024
SMALL_ROWS = 16


def dot(left, right, left_dim=1, right_dim=0):
    return lax.dot_general(
        left, right, (((left_dim,), (right_dim,)), ((), ())), preferred_element_type=WIDE
    )


def normalize(x):
    center = x - jnp.mean(x, axis=-1, keepdims=True)
    scale = lax.rsqrt(jnp.mean(center * center, axis=-1, keepdims=True) + EPSILON)
    return center * scale, scale


def normalize_back(n, scale, gain, grad):
    e = grad * gain
    return scale * (
        e - jnp.mean(e, axis=-1, keepdims=True) - n * jnp.mean(e * n, axis=-1, keepdims=True)
    )


def chunks(total, size):
    return [slice(start, start + size) for start in range(0, total, size)]


def split_heads(first, value):
    zero = jnp.zeros_like(value)
    return jnp.where(first, value, zero), jnp.where(first, zero, value)


def load_window(ref, layout, window):
    if layout == "tokens":
        return ref[0, window]
    if layout == "frames":
        block = ref[:, 0, window]
    else:
        block = ref[:, 0, :, window * TUBE : (window + 1) * TUBE, :]
    return block.reshape(-1, block.shape[-1])


def load_rows(ref, layout, windows):
    if layout == "rows":
        return ref[...]
    return jnp.concatenate([load_window(ref, layout, w) for w in range(windows)], axis=0)


def store_window(ref, layout, window, value):
    if layout == "tokens":
        ref[0, window] = value
    elif layout == "frames":
        ref[:, 0, window] = value.reshape(ref.shape[0], -1, ref.shape[-1])
    else:
        tube = slice(window * TUBE, (window + 1) * TUBE)
        ref[:, 0, :, tube, :] = value.reshape(ref.shape[0], -1, TUBE, ref.shape[-1])


def store_rows(ref, layout, windows, value):
    length = value.shape[0] // windows
    for w in range(windows):
        store_window(ref, layout, w, value[w * length : (w + 1) * length])


def forward_kernel(dims, counts, x, *refs):
    block, windows, length, width, hidden, n_alias, first_clip, passes = dims
    if block == 0:
        cotangent, refs = refs[0], refs[1:]
    gain, shift, w_in_h, w_out_h, w_expand_h, b_expand, w_reduce_h = refs[:7]
    refs = refs[7 + n_alias :]
    if passes:
        refs = refs[1:]
    if block == 0:
        out, *refs = refs
    kept, extra_o, scratch = refs[:9], refs[9], refs[10:]
    buffers, weights, kept_sems, weight_sems = scratch[:9], scratch[9:-2], scratch[-2], scratch[-1]
    normed_o, triple_o, recip_o, raised_o, attended_o, middle_o, normed2_o, active_o, slope_o = buffers
    step = pl.program_id(0)
    clip = first_clip + step
    rows = windows * length

    def place(index):
        size = buffers[index].shape[0]
        return pl.ds(pl.multiple_of(clip * size, size), size)

    def copy_out(index, columns=slice(None)):
        if index == 3:
            target = kept[index].at[place(index)]
        else:
            target = kept[index].at[place(index), columns]
        source = buffers[index] if index == 3 else buffers[index].at[:, columns]
        return pltpu.make_async_copy(source, target, kept_sems.at[index])

    loads = [
        pltpu.make_async_copy(source.at[block], target, weight_sems.at[k])
        for k, (source, target) in enumerate(
            zip((w_in_h, w_out_h, w_expand_h, w_reduce_h), weights)
        )
    ]
    w_in, w_out, w_expand = weights[:3]

    @pl.when(step == 0)
    def _():
        for load in loads:
            load.start()
        loads[0].wait()

    @pl.when(step > 0)
    def _():
        for index in range(7):
            copy_out(index).wait()

    stream = load_rows(x, ("tokens", "tubes")[block], windows)
    if block == 0:
        for w in range(windows):
            store_window(extra_o, "frames", w, load_window(cotangent, "tokens", w))
    else:
        extra_o[...] = stream
    stream = stream.astype(WIDE)
    n, unused = normalize(stream)
    normed_o[...] = (n * gain[block, 0] + shift[block, 0]).astype(LOW)
    copy_out(0).start()
    for c in chunks(3 * width, width):
        triple_o[:, c] = dot(normed_o[...], w_in[:, c]).astype(LOW)
    copy_out(1).start()
    first = lax.broadcasted_iota(jnp.int32, (length, PAIR), 1) < HEAD_DIM
    ones_a, ones_b = split_heads(first, jnp.ones((length, PAIR), LOW))
    if block == 1:
        key = lax.broadcasted_iota(jnp.int32, (1, length), 1)
        kept_key = key // TUBE < counts[clip]
        bias = jnp.where(kept_key, 0.0, -1e30).astype(WIDE)
    for w in range(windows):
        span = slice(w * length, (w + 1) * length)
        for p, c in enumerate(chunks(width, PAIR)):
            queries = triple_o[span, c] * LOW(HEAD_DIM**-0.5)
            keys = triple_o[span, c.start + width : c.stop + width]
            values = triple_o[span, c.start + 2 * width : c.stop + 2 * width]
            raised = []
            for q in split_heads(first, queries):
                scores = dot(q, keys, 1, 1)
                if block == 1:
                    scores = scores + bias
                raised.append(
                    jnp.exp(scores - jnp.max(scores, axis=1, keepdims=True)).astype(LOW)
                )
            raised = jnp.concatenate(raised, axis=1)
            raised_o[w, p] = raised
            values_a, values_b = split_heads(first, values)
            sums = dot(
                raised,
                jnp.concatenate(
                    [
                        jnp.concatenate([values_a, ones_a], axis=1),
                        jnp.concatenate([values_b, ones_b], axis=1),
                    ],
                    axis=0,
                ),
            )
            recip = 1.0 / sums[:, PAIR:]
            recip_o[span, c] = recip
            attended_o[span, c] = (sums[:, :PAIR] * recip).astype(LOW)
    for index in (2, 3, 4):
        copy_out(index).start()

    @pl.when(step == 0)
    def _():
        for load in loads[1:]:
            load.wait()

    @pl.when(step > 0)
    def _():
        for index in (7, 8):
            copy_out(index).wait()

    middle = load_rows(x, ("tokens", "tubes")[block], windows).astype(WIDE)
    middle = middle + dot(attended_o[...], w_out[...])
    middle_o[...] = middle
    copy_out(5).start()
    n, unused = normalize(middle)
    normed2_o[...] = (n * gain[block, 1] + shift[block, 1]).astype(LOW)
    copy_out(6).start()
    total = middle
    for c in chunks(hidden, 512):
        pre = dot(normed2_o[...], w_expand[:, c]) + b_expand[block : block + 1, c]
        below = 0.5 + 0.5 * lax.erf(pre * HALF_ROOT)
        active = (pre * below).astype(LOW)
        active_o[:, c] = active
        slope_o[:, c] = (below + pre * (BELL_PEAK * jnp.exp(-0.5 * pre * pre))).astype(LOW)
        copy_out(7, c).start()
        copy_out(8, c).start()
        if block == 0:
            total = total + dot(active, weights[3][c, :])
    if block == 0:
        store_rows(out, "frames", windows, total.astype(LOW))

    @pl.when(step == pl.num_programs(0) - 1)
    def _():
        for index in range(9):
            copy_out(index).wait()


def output_kernel(windows, active, middle, w_reduce, *refs):
    total = middle[...] + dot(active[...], w_reduce[...])
    store_rows(refs[-1], "tubes", windows, total.astype(LOW))


def mlp_back_kernel(dims, *refs):
    block, windows, width, hidden = dims
    g, slope, middle, gain, w_expand, w_reduce = refs[:6]
    rows_o, pre_o, mid_o, bias_o, gain_o, shift_o = refs[-6:]
    grad = load_rows(g, ("frames", "tubes")[block], windows)
    rows_o[...] = grad

    @pl.when(pl.program_id(0) == 0)
    def _():
        bias_o[...] = jnp.zeros_like(bias_o)
        gain_o[...] = jnp.zeros_like(gain_o)
        shift_o[...] = jnp.zeros_like(shift_o)

    total = None
    for c in chunks(hidden, 512):
        pre = (dot(grad, w_reduce[c, :], 1, 1) * slope[:, c].astype(WIDE)).astype(LOW)
        pre_o[:, c] = pre
        bias_o[:, c] += jnp.sum(pre.astype(WIDE), axis=0, keepdims=True)
        part = dot(pre, w_expand[:, c], 1, 1)
        total = part if total is None else total + part
    n, scale = normalize(middle[...])
    gain_o[...] += jnp.sum(total * n, axis=0, keepdims=True)
    shift_o[...] += jnp.sum(total, axis=0, keepdims=True)
    mid_o[...] = grad.astype(WIDE) + normalize_back(n, scale, gain[block, 1], total)


def attention_back_kernel(dims, *refs):
    block, windows, length, width = dims
    mid, triple, recip, raised, attended, w_out = refs[:6]
    if block == 0:
        triple_o, grad_s = refs[-2:]
    else:
        triple_o, grad_s = refs[-5], refs[-1]
    grad_s[...] = dot(mid[...].astype(LOW), w_out[...], 1, 1).astype(LOW)
    first = lax.broadcasted_iota(jnp.int32, (length, PAIR), 1) < HEAD_DIM
    minus = jnp.full((length, PAIR), -1.0, LOW)
    root = HEAD_DIM**-0.5
    for w in range(windows):
        span = slice(w * length, (w + 1) * length)
        for p, c in enumerate(chunks(width, PAIR)):
            c_keys = slice(c.start + width, c.stop + width)
            c_values = slice(c.start + 2 * width, c.stop + 2 * width)
            grad = grad_s[span, c]
            grad_wide = grad.astype(WIDE)
            share = recip[span, c]
            inner = (grad_wide * attended[span, c].astype(WIDE)).astype(LOW)
            grad_scaled = (grad_wide * share).astype(LOW)
            queries = (triple[span, c].astype(WIDE) * (share * root)).astype(LOW)
            keys = triple[span, c_keys] * LOW(root)
            values = jnp.concatenate([triple[span, c_values], minus], axis=1)
            scores = []
            for i, (a, b) in enumerate(zip(split_heads(first, grad), split_heads(first, inner))):
                delta = dot(jnp.concatenate([a, b], axis=1), values, 1, 1)
                e = raised[w, p, :, i * length : (i + 1) * length]
                scores.append((e.astype(WIDE) * delta).astype(LOW))
            grad_q = (
                dot(
                    jnp.concatenate(scores, axis=1),
                    jnp.concatenate(split_heads(first, keys), axis=0),
                )
                * share
            )
            grad_k = dot(
                jnp.concatenate(scores, axis=0),
                jnp.concatenate(split_heads(first, queries), axis=0),
                0,
                0,
            )
            grad_v = dot(
                jnp.concatenate([raised[w, p, :, :length], raised[w, p, :, length:]], axis=0),
                jnp.concatenate(split_heads(first, grad_scaled), axis=0),
                0,
                0,
            )
            triple_o[span, c] = grad_q.astype(LOW)
            triple_o[span, c_keys] = grad_k.astype(LOW)
            triple_o[span, c_values] = grad_v.astype(LOW)
    if block == 1:
        x, gain, w_in = refs[6:9]
        stream_back(block, windows, "rows", "tubes", x, mid, triple_o, gain, w_in, *refs[-4:-1])


def stream_back(block, windows, x_layout, layout, x, mid, triple, gain, w_in, gain_o, shift_o, out):
    @pl.when(pl.program_id(0) == 0)
    def _():
        gain_o[...] = jnp.zeros_like(gain_o)
        shift_o[...] = jnp.zeros_like(shift_o)

    total = dot(triple[...], w_in[...], 1, 1)
    n, scale = normalize(load_rows(x, x_layout, windows).astype(WIDE))
    gain_o[...] += jnp.sum(total * n, axis=0, keepdims=True)
    shift_o[...] += jnp.sum(total, axis=0, keepdims=True)
    grad_x = (mid[...] + normalize_back(n, scale, gain[block, 0], total)).astype(LOW)
    store_rows(out, layout, windows, grad_x)


def finish_kernel(windows, x, mid, triple, gain, w_in, mixed, *refs):
    gain_o, shift_o, out, mixed_o = refs[-4:]
    stream_back(0, windows, "tokens", "tokens", x, mid, triple, gain, w_in, gain_o, shift_o, out)
    for w in range(windows):
        store_window(mixed_o, "tokens", w, load_window(mixed, "frames", w))


def split_rows(value, place, send, keep):
    value = value.astype(LOW)
    pairs, length = keep.shape[0], keep.shape[1]
    same = place % 2 == 0
    for p in range(pairs):
        low = value[2 * p * length : (2 * p + 1) * length]
        high = value[(2 * p + 1) * length : (2 * p + 2) * length]
        slot = (place // 2 % pairs) ^ p
        keep[slot] = jnp.where(same, low, high)
        send[slot] = jnp.where(same, high, low)


def outer_kernel(has_last, is_split, place, left, right, *refs):
    place = place[0]
    step = pl.program_id(0)
    outs = refs[-2:] if is_split else refs[-1:]

    def store(value):
        if is_split:
            split_rows(value, place, *outs)
        else:
            outs[0][...] = value.astype(LOW).reshape(outs[0].shape)

    if not has_last:
        store(dot(left[...], right[...], 0, 0))
        return
    last = pl.num_programs(0) - 1

    @pl.when(step < last)
    def _():
        store(dot(left[...], right[...], 0, 0))

    @pl.when(step == last)
    def _():
        store(dot(refs[0][...], refs[1][...].astype(LOW), 0, 0))


def whole(shape):
    return pl.BlockSpec(shape, lambda i: (0,) * len(shape), pipeline_mode=pl.Buffered(1))


def layer(shape, block):
    return pl.BlockSpec(
        (None,) + shape, lambda i: (block,) + (0,) * len(shape), pipeline_mode=pl.Buffered(1)
    )


def clip_spec(shape, first=0):
    if len(shape) == 2:
        return pl.BlockSpec(shape, lambda i: (i + first, 0))
    if len(shape) == 3:
        return pl.BlockSpec((1,) + shape, lambda i: (i + first, 0, 0, 0))
    return pl.BlockSpec(
        (shape[0], 1) + shape[1:], lambda i: (0, i + first) + (0,) * (len(shape) - 1)
    )


def all_clips(shape, clips):
    if len(shape) == 2:
        return (clips * shape[0], shape[1])
    if len(shape) == 3:
        return (clips,) + shape
    return (shape[0], clips) + shape[1:]


ANY = pl.BlockSpec(memory_space=pl.ANY)
SCALARS = pl.BlockSpec(memory_space=pltpu.SMEM)


def params():
    return pltpu.CompilerParams(vmem_limit_bytes=VMEM_BYTES)


def cost(micros):
    return pl.CostEstimate(
        flops=int(micros * 350000000), bytes_accessed=int(micros * 1050000), transcendentals=0
    )


def sizes(weights, shapes):
    width, hidden = weights[4].shape[1:]
    clips, windows, length, parts = shapes
    return clips, windows, length, parts, windows * length, width, hidden


def forward(block, counts, x, cotangent, weights, saved, first, shapes, through=None):
    gain, shift, w_in, w_out, w_expand, b_expand, w_reduce = weights
    clips, windows, length, parts, rows, width, hidden = sizes(weights, shapes)
    steps = clips // 2
    travel = (parts, windows, length // parts, width)
    raised = (windows, width // PAIR, length, 2 * length)
    kept = [
        (rows, width), (rows, 3 * width), (rows, width), raised, (rows, width),
        (rows, width), (rows, width), (rows, hidden), (rows, hidden),
    ]
    types = [LOW, LOW, WIDE, LOW, LOW, WIDE, LOW, LOW, LOW]
    buffers = [pltpu.VMEM(shape, kind) for shape, kind in zip(kept, types)]
    extra = travel if block == 0 else (rows, width)
    specs = [ANY] * len(kept) + [clip_spec(extra, first)]
    outs = [
        jax.ShapeDtypeStruct((clips * shape[0],) + shape[1:], kind)
        for shape, kind in zip(kept, types)
    ]
    outs.append(jax.ShapeDtypeStruct(all_clips(extra, clips), LOW))
    loaded = [w_in, w_out, w_expand] + ([w_reduce] if block == 0 else [])
    if block == 0:
        specs = [clip_spec(travel)] + specs
        outs = [jax.ShapeDtypeStruct(all_clips(travel, steps), LOW)] + outs
        ins = [counts, x, cotangent]
        in_specs = [SCALARS] + [clip_spec(v.shape[1:], first) for v in ins[1:]]
    else:
        ins = [counts, x]
        in_specs = [SCALARS, clip_spec(travel)]
    alias = [] if saved is None else list(saved)
    base = 1 if block == 0 else 0
    if through is not None:
        specs = [ANY] + specs
        outs = [jax.ShapeDtypeStruct(through.shape, through.dtype)] + outs
        alias = [through] + alias
    ins += weights
    in_specs += [
        whole(gain.shape),
        whole(shift.shape),
        ANY,
        ANY,
        ANY,
        whole(b_expand.shape),
        ANY,
    ]
    dims = (block, windows, length, width, hidden, len(alias), first, through is not None)
    got = pl.pallas_call(
        functools.partial(forward_kernel, dims),
        grid=(steps,),
        in_specs=in_specs + [ANY] * len(alias),
        out_specs=specs,
        out_shape=outs,
        input_output_aliases={len(ins) + i: base + i for i in range(len(alias))},
        scratch_shapes=buffers
        + [pltpu.VMEM(v.shape[1:], LOW) for v in loaded]
        + [pltpu.SemaphoreType.DMA((len(kept),)), pltpu.SemaphoreType.DMA((len(loaded),))],
        compiler_params=params(),
        cost_estimate=cost(36 if block == 0 else 30),
        name=f"forward_{block}",
    )(*ins, *alias)
    if block == 0 or through is not None:
        return got[0], got[1:]
    return got


def output(active, middle, weights, shapes, through):
    clips, windows, length, parts, rows, width, hidden = sizes(weights, shapes)
    travel = (parts, windows, length // parts, width)
    return pl.pallas_call(
        functools.partial(output_kernel, windows),
        grid=(clips,),
        in_specs=[
            clip_spec((rows, hidden)),
            clip_spec((rows, width)),
            layer(weights[6].shape[1:], 1),
        ]
        + [ANY],
        out_specs=[ANY, clip_spec(travel)],
        out_shape=[
            jax.ShapeDtypeStruct(through.shape, through.dtype),
            jax.ShapeDtypeStruct(all_clips(travel, clips), LOW),
        ],
        input_output_aliases={3: 0},
        compiler_params=params(),
        cost_estimate=cost(14),
        name="output",
    )(active, middle, weights[6], through)


def mlp_back(block, g, slope, middle, weights, shapes, through=()):
    gain, shift, w_in, w_out, w_expand, b_expand, w_reduce = weights
    clips, windows, length, parts, rows, width, hidden = sizes(weights, shapes)
    travel = (parts, windows, length // parts, width)
    kinds = [
        ((rows, width), LOW), ((rows, hidden), LOW), ((rows, width), WIDE),
        ((1, hidden), WIDE), ((1, width), WIDE), ((1, width), WIDE),
    ]
    return pl.pallas_call(
        functools.partial(mlp_back_kernel, (block, windows, width, hidden)),
        grid=(clips,),
        in_specs=[
            clip_spec(travel),
            clip_spec((rows, hidden)),
            clip_spec((rows, width)),
            whole(gain.shape),
            layer(w_expand.shape[1:], block),
            layer(w_reduce.shape[1:], block),
        ]
        + [ANY] * len(through),
        out_specs=[ANY] * len(through)
        + [clip_spec(s) for s, unused in kinds[:3]]
        + [pl.BlockSpec(s, lambda i: (0, 0)) for s, unused in kinds[3:]],
        out_shape=[jax.ShapeDtypeStruct(v.shape, v.dtype) for v in through]
        + [jax.ShapeDtypeStruct(all_clips(s, clips), k) for s, k in kinds[:3]]
        + [jax.ShapeDtypeStruct(s, k) for s, k in kinds[3:]],
        input_output_aliases={6 + i: i for i in range(len(through))},
        compiler_params=params(),
        cost_estimate=cost(100),
        name=f"mlp_back_{block}",
    )(g, slope, middle, gain, w_expand, w_reduce, *through)


def attention_back(block, x, mid, triple, recip, raised, attended, weights, shapes, after=()):
    gain, shift, w_in, w_out, w_expand, b_expand, w_reduce = weights
    clips, windows, length, parts, rows, width, hidden = sizes(weights, shapes)
    travel = (parts, windows, length // parts, width)
    ins = [mid, triple, recip, raised, attended, w_out]
    in_specs = [
        clip_spec((rows, width)),
        clip_spec((rows, 3 * width)),
        clip_spec((rows, width)),
        pl.BlockSpec((windows,) + raised.shape[1:], lambda i: (i, 0, 0, 0)),
        clip_spec((rows, width)),
        layer(w_out.shape[1:], block),
    ]
    out_specs = [clip_spec((rows, 3 * width))]
    out_shape = [jax.ShapeDtypeStruct((clips * rows, 3 * width), LOW)]
    if block == 1:
        ins += [x, gain, w_in]
        in_specs += [clip_spec((rows, width)), whole(gain.shape), layer(w_in.shape[1:], block)]
        out_specs += [pl.BlockSpec((1, width), lambda i: (0, 0))] * 2 + [clip_spec(travel)]
        out_shape += [jax.ShapeDtypeStruct((1, width), WIDE)] * 2
        out_shape += [jax.ShapeDtypeStruct(all_clips(travel, clips), LOW)]
    return pl.pallas_call(
        functools.partial(attention_back_kernel, (block, windows, length, width)),
        grid=(clips,),
        in_specs=in_specs + [ANY] * len(after),
        out_specs=out_specs,
        out_shape=out_shape,
        scratch_shapes=[pltpu.VMEM((rows, width), LOW)],
        compiler_params=params(),
        cost_estimate=cost(42 if block else 30),
        name=f"attention_back_{block}",
    )(*ins, *after)


def finish(x, mid, triple, mixed, weights, shapes, through, after=()):
    gain, shift, w_in, w_out, w_expand, b_expand, w_reduce = weights
    clips, windows, length, parts, rows, width, hidden = sizes(weights, shapes)
    travel = (parts, windows, length // parts, width)
    tokens = (windows, length, width)
    sums = jax.ShapeDtypeStruct((1, width), WIDE)
    sums_spec = pl.BlockSpec((1, width), lambda i: (0, 0))
    return pl.pallas_call(
        functools.partial(finish_kernel, windows),
        grid=(clips,),
        in_specs=[
            clip_spec(tokens),
            clip_spec((rows, width)),
            clip_spec((rows, 3 * width)),
            whole(gain.shape),
            layer(w_in.shape[1:], 0),
            clip_spec(travel),
            ANY,
        ]
        + [ANY] * len(after),
        out_specs=[ANY, sums_spec, sums_spec, clip_spec(tokens), clip_spec(tokens)],
        out_shape=[jax.ShapeDtypeStruct(through.shape, through.dtype), sums, sums]
        + [jax.ShapeDtypeStruct(all_clips(tokens, clips), LOW)] * 2,
        input_output_aliases={6: 0},
        compiler_params=params(),
        cost_estimate=cost(15),
        name="finish",
    )(x, mid, triple, gain, w_in, mixed, through, *after)


def outer_rows(place, active, grad, parts, is_split, into=None, after=()):
    total, width = grad.shape
    hidden = active.shape[1]
    steps = hidden // width
    group = parts // steps
    rows = hidden // parts
    if is_split:
        half = group // 2
        spec = pl.BlockSpec((half, rows, width), lambda i, place: (i ^ (place[0] // 2 // half), 0, 0))
        shape = jax.ShapeDtypeStruct((parts // 2, rows, width), LOW)
    else:
        spec = pl.BlockSpec((group, rows, width), lambda i, place: (i, 0, 0))
        shape = jax.ShapeDtypeStruct(into.shape, LOW)
    alias = [] if into is None else [into]
    arrays = 2 if is_split else 1
    return pl.pallas_call(
        functools.partial(outer_kernel, False, is_split),
        grid_spec=pltpu.PrefetchScalarGridSpec(
            num_scalar_prefetch=1,
            grid=(steps,),
            in_specs=[
                pl.BlockSpec((total, width), lambda i, place: (0, i)),
                pl.BlockSpec(
                    (total, width), lambda i, place: (0, 0), pipeline_mode=pl.Buffered(1)
                ),
            ]
            + [ANY] * (len(alias) + len(after)),
            out_specs=[spec] * arrays,
        ),
        out_shape=[shape] * arrays,
        input_output_aliases={3: 0} if alias else {},
        compiler_params=params(),
        cost_estimate=cost(14),
        name="outer_rows",
    )(place, active, grad, *alias, *after)


def outer_columns(place, left, right, last, parts, is_split, after=(), skip=0, through=()):
    total, width = left.shape
    steps = right.shape[1] // width
    blocks = steps + (1 if last else 0)
    ins = [place, left, right, *last]
    in_specs = [
        SCALARS,
        whole((total, width)),
        pl.BlockSpec((total, width), lambda i: (0, jnp.minimum(i, steps - 1))),
    ]
    in_specs += [whole((total, width))] * len(last)
    owners, arrays = (parts // 2, 2) if is_split else (parts, 1)
    spec = pl.BlockSpec((owners, width // parts, width), lambda i: (0, i + skip, 0))
    shape = jax.ShapeDtypeStruct((owners, (blocks + skip) * width // parts, width), LOW)
    return pl.pallas_call(
        functools.partial(outer_kernel, bool(last), is_split),
        grid=(blocks,),
        in_specs=in_specs + [ANY] * (len(through) + len(after)),
        out_specs=[ANY] * len(through) + [spec] * arrays,
        out_shape=[jax.ShapeDtypeStruct(v.shape, v.dtype) for v in through] + [shape] * arrays,
        input_output_aliases={len(ins) + i: i for i in range(len(through))},
        compiler_params=params(),
        cost_estimate=cost(4 * blocks),
        name="outer_columns",
    )(*ins, *through, *after)


def add_all(values):
    total = values[0].astype(WIDE)
    for value in values[1:]:
        total = total + value.astype(WIDE)
    return total.astype(LOW)


def swap(value, axis, offset):
    return lax.ppermute(
        value, axis, [(i, i ^ offset) for i in range(lax.axis_size(axis))]
    )


def sum_frames(send, keep, reverse):
    bits = (lax.axis_size("frame") // 2).bit_length() - 1
    shape = (2,) * bits + keep.shape[1:]
    terms = [keep.reshape(shape), swap(send, "frame", 1).reshape(shape)]
    order = list(range(1, bits + 1))
    if reverse:
        order = order[::-1]
    left = list(range(bits, 0, -1))
    for bit in order:
        axis = left.index(bit)
        left.remove(bit)
        far = add_all([lax.index_in_dim(t, 1, axis, keepdims=False) for t in terms])
        yield far
        terms = [lax.index_in_dim(t, 0, axis, keepdims=False) for t in terms]
        terms.append(swap(far, "frame", 1 << bit))
    yield add_all(terms)


def last_of(steps):
    for value in steps:
        pass
    return value


def clip_blocks(total):
    size = lax.axis_size("clip")
    rows = -(-total.shape[0] // (16 * size)) * 16
    total = jnp.pad(total, ((0, rows * size - total.shape[0]), (0, 0)))
    return total.reshape(size, rows, total.shape[1])


def over_clips(*values):
    value = values[0] if len(values) == 1 else jnp.concatenate(values, axis=1)
    got = lax.all_to_all(value, "clip", 0, 0)
    cuts = [sum(v.shape[1] for v in values[: i + 1]) for i in range(len(values))]
    return [got[:, cut - v.shape[1] : cut] for cut, v in zip(cuts, values)]


def to_all_clips(value):
    return jnp.broadcast_to(value[None], (lax.axis_size("clip"),) + value.shape)


def gather_kernel(block, plan, n_in, n_outs, *refs):
    sources, outs = refs[: len(plan)], refs[n_in : n_in + n_outs]
    for source, group in zip(sources, plan):
        width = source.shape[1]
        start = 0
        for out, columns in group:
            length = outs[out].shape[1]
            for c in range(columns):
                outs[out][0, :, c * width : (c + 1) * width] = source[
                    start : start + length, :
                ].astype(WIDE)
                start += length


def gather(block, sources, plan, outs):
    filled = not isinstance(outs[0], jax.ShapeDtypeStruct)
    extra = list(outs) if filled else []
    specs = [
        pl.BlockSpec((1,) + v.shape[1:], lambda i: (block, 0, 0)) for v in outs
    ]
    ins = [*sources, *extra]
    aliases = {len(sources) + i: i for i in range(len(extra))}
    return pl.pallas_call(
        functools.partial(gather_kernel, block, plan, len(ins), len(outs)),
        grid=(1,),
        in_specs=[whole(v.shape) for v in sources] + [ANY] * len(extra),
        out_specs=specs,
        out_shape=[jax.ShapeDtypeStruct(v.shape, v.dtype) for v in outs],
        input_output_aliases=aliases,
        compiler_params=params(),
        cost_estimate=cost(4),
        name="gather",
    )(*ins)


def exchange(value):
    return lax.all_to_all(value, "frame", 0, 0)


def local(
    tokens,
    frame_counts,
    norm_gain,
    norm_bias,
    project_in,
    project_out,
    expand_weight,
    expand_bias,
    reduce_weight,
    cotangent,
):
    clips, frames, length, width = tokens.shape
    hidden = expand_weight.shape[2]
    parts = lax.axis_size("frame")
    part = width // parts
    shapes = (clips, frames, length, parts)
    half = clips // 2
    weights = (
        norm_gain, norm_bias, project_in, project_out, expand_weight, expand_bias, reduce_weight
    )
    place = lax.axis_index("frame").astype(jnp.int32).reshape(1)

    out, saved0 = forward(0, frame_counts, tokens, cotangent, weights, None, 0, shapes)
    boundary_a = exchange(out)
    out, saved0 = forward(0, frame_counts, tokens, cotangent, weights, saved0, half, shapes)
    boundary_b = exchange(out)
    cotangent_tubes, saved1 = forward(
        1, frame_counts, boundary_a, None, weights, None, 0, shapes, saved0[9]
    )
    cotangent_tubes = exchange(cotangent_tubes)
    saved1 = forward(1, frame_counts, boundary_b, None, weights, saved1, half, shapes)

    def scatter(value):
        return lax.psum_scatter(value, "frame", scatter_dimension=0, tiled=True)[0]

    normed, triple, recip, raised, attended, middle, normed2, active, slope, stream = saved1
    rows1, pre, mid, bias1, gain12, shift12 = mlp_back(
        1, cotangent_tubes, slope, middle, weights, shapes
    )
    columns = hidden // width
    (mlp1,) = outer_columns(place, normed2, pre, [], parts, False, [], columns)
    (mlp1,) = outer_rows(place, active, rows1, parts, False, mlp1)
    mlp1_scattered = scatter(mlp1)
    grad_triple, gain11, shift11, grad_boundary = attention_back(
        1, stream, mid, triple, recip, raised, attended, weights, shapes, [mlp1]
    )
    grad_boundary = exchange(grad_boundary)
    (attention1,) = outer_columns(
        place, normed, grad_triple, [attended, mid], parts, False
    )
    attention1, mixed = output(active, middle, weights, shapes, attention1)
    attention1_scattered = scatter(attention1)

    normed, triple, recip, raised, attended, middle, normed2, active, slope = saved0[:9]
    mixed, rows0, pre, mid, bias0, gain02, shift02 = mlp_back(
        0, grad_boundary, slope, middle, weights, shapes, [mixed]
    )
    mixed = exchange(mixed)
    mlp1_sum = lax.psum(mlp1_scattered, "clip")
    reduce0 = outer_rows(place, active, rows0, parts, True, None, [mlp1_scattered])
    expand0 = outer_columns(
        place, normed2, pre, [attended, mid], parts, True, [reduce0[0]]
    )
    (grad_triple,) = attention_back(
        0, None, mid, triple, recip, raised, attended, weights, shapes, [expand0[0]]
    )
    steps_c, steps_d = sum_frames(*reduce0, False), sum_frames(*expand0, True)
    sent = [next(steps_c), next(steps_d)]
    attention1_scattered, gain01, shift01, grad_tokens, mixed = finish(
        tokens, mid, grad_triple, mixed, weights, shapes, attention1_scattered, sent
    )
    backward = [list(range(lax.axis_size("clip")))[::-1]]
    attention1_sum = lax.psum(attention1_scattered, "clip", axis_index_groups=backward)
    sent = [next(steps_c), next(steps_d)]

    def by_owner(*values):
        return jnp.concatenate([v.reshape(parts, -1) for v in values], axis=1)

    small = by_owner(
        gain01, gain02, shift01, shift02, bias0, gain11, gain12, shift11, shift12, bias1
    ).astype(LOW)
    count = small.shape[1]
    small = jnp.pad(small, ((0, 0), (0, SMALL_ROWS * width - count)))
    small, send, keep = outer_columns(
        place, normed, grad_triple, [], parts, True, [*sent, mlp1_sum], 0,
        [small.reshape(parts, SMALL_ROWS, width)],
    )
    cut = send.shape[1] // 2
    steps_a = sum_frames(send[:, :cut], keep[:, :cut], False)
    steps_b = sum_frames(send[:, cut:], keep[:, cut:], True)
    small = add_all(list(exchange(small)))
    last = jnp.concatenate([last_of(steps_a), last_of(steps_b)], axis=0)
    outs = [
        (2, hidden // parts, width),
        (2, part, hidden),
        (2, part, 3 * width),
        (2, part, width),
    ]
    outs = [jax.ShapeDtypeStruct(v, WIDE) for v in outs]
    mlp0_sum = jnp.concatenate([last_of(steps_c), last_of(steps_d)], axis=0)
    (mlp0_sum,) = over_clips(clip_blocks(mlp0_sum))
    mlp0_sum = to_all_clips(add_all(list(mlp0_sum)))
    mlp0_sum, in0_sum, small = over_clips(mlp0_sum, clip_blocks(last), to_all_clips(small))
    in0_sum = to_all_clips(add_all(list(in0_sum)))
    (in0_sum,) = over_clips(in0_sum)
    small = jnp.sum(small.astype(WIDE), axis=0).reshape(-1)[:count].reshape(2, -1)
    outs = gather(
        1,
        [mlp1_sum, attention1_sum],
        (((0, 1), (1, columns)), ((2, 3), (3, 1))),
        outs,
    )
    grad_reduce, grad_expand, grad_in, grad_out = gather(
        0,
        [mlp0_sum.reshape(-1, width), in0_sum.reshape(-1, width)],
        (((0, 1), (1, columns), (3, 1)), ((2, 3),)),
        outs,
    )
    return (
        mixed,
        grad_tokens,
        small[:, : 2 * part].reshape(2, 2, part),
        small[:, 2 * part : 4 * part].reshape(2, 2, part),
        grad_in,
        grad_out,
        grad_expand,
        small[:, 4 * part :],
        grad_reduce,
    )


def solution(mesh):
    in_specs = (
        P("clip", "frame", None, None),
        P("clip"),
        P(),
        P(),
        P(),
        P(),
        P(),
        P(),
        P(),
        P("clip", "frame", None, None),
    )
    out_specs = (
        P("clip", "frame", None, None),
        P("clip", "frame", None, None),
        P(None, None, "frame"),
        P(None, None, "frame"),
        P(None, "frame", None),
        P(None, "frame", None),
        P(None, "frame", None),
        P(None, "frame"),
        P(None, "frame", None),
    )
    return jax.shard_map(local, mesh=mesh, in_specs=in_specs, out_specs=out_specs, check_vma=False)
```

```python
import functools

import jax
import jax.numpy as jnp
from jax import lax
from jax.experimental import pallas as pl
from jax.experimental.pallas import tpu as pltpu
from jax.sharding import PartitionSpec as P

HEAD_DIM = 64
TUBE = 16
PAIR = 2 * HEAD_DIM
EPSILON = 1e-05
HALF_ROOT = 0.7071067811865476
BELL_PEAK = 0.3989422804014327
LOW = jnp.bfloat16
WIDE = jnp.float32
VMEM_BYTES = 63 * 1024 * 1024
SMALL_ROWS = 16


def dot(left, right, left_dim=1, right_dim=0):
    return lax.dot_general(
        left, right, (((left_dim,), (right_dim,)), ((), ())), preferred_element_type=WIDE
    )


def normalize(x):
    center = x - jnp.mean(x, axis=-1, keepdims=True)
    scale = lax.rsqrt(jnp.mean(center * center, axis=-1, keepdims=True) + EPSILON)
    return center * scale, scale


def normalize_back(n, scale, gain, grad):
    e = grad * gain
    return scale * (
        e - jnp.mean(e, axis=-1, keepdims=True) - n * jnp.mean(e * n, axis=-1, keepdims=True)
    )


def chunks(total, size):
    return [slice(start, start + size) for start in range(0, total, size)]


def split_heads(first, value):
    zero = jnp.zeros_like(value)
    return jnp.where(first, value, zero), jnp.where(first, zero, value)


def load_window(ref, layout, window):
    if layout == "tokens":
        return ref[0, window]
    if layout == "frames":
        block = ref[:, 0, window]
    else:
        block = ref[:, 0, :, window * TUBE : (window + 1) * TUBE, :]
    return block.reshape(-1, block.shape[-1])


def load_rows(ref, layout, windows):
    if layout == "rows":
        return ref[...]
    return jnp.concatenate([load_window(ref, layout, w) for w in range(windows)], axis=0)


def store_window(ref, layout, window, value):
    if layout == "tokens":
        ref[0, window] = value
    elif layout == "frames":
        ref[:, 0, window] = value.reshape(ref.shape[0], -1, ref.shape[-1])
    else:
        tube = slice(window * TUBE, (window + 1) * TUBE)
        ref[:, 0, :, tube, :] = value.reshape(ref.shape[0], -1, TUBE, ref.shape[-1])


def store_rows(ref, layout, windows, value):
    length = value.shape[0] // windows
    for w in range(windows):
        store_window(ref, layout, w, value[w * length : (w + 1) * length])


def forward_kernel(dims, counts, x, *refs):
    block, windows, length, width, hidden, n_alias, first_clip, passes = dims
    if block == 0:
        cotangent, refs = refs[0], refs[1:]
    gain, shift, w_in_h, w_out_h, w_expand_h, b_expand, w_reduce_h = refs[:7]
    refs = refs[7 + n_alias :]
    if passes:
        refs = refs[1:]
    if block == 0:
        out, *refs = refs
    kept, extra_o, scratch = refs[:9], refs[9], refs[10:]
    buffers, weights, kept_sems, weight_sems = scratch[:9], scratch[9:-2], scratch[-2], scratch[-1]
    normed_o, triple_o, recip_o, raised_o, attended_o, middle_o, normed2_o, active_o, slope_o = buffers
    step = pl.program_id(0)
    clip = first_clip + step
    rows = windows * length

    def place(index):
        size = buffers[index].shape[0]
        return pl.ds(pl.multiple_of(clip * size, size), size)

    def copy_out(index, columns=slice(None)):
        if index == 3:
            target = kept[index].at[place(index)]
        else:
            target = kept[index].at[place(index), columns]
        source = buffers[index] if index == 3 else buffers[index].at[:, columns]
        return pltpu.make_async_copy(source, target, kept_sems.at[index])

    loads = [
        pltpu.make_async_copy(source.at[block], target, weight_sems.at[k])
        for k, (source, target) in enumerate(
            zip((w_in_h, w_out_h, w_expand_h, w_reduce_h), weights)
        )
    ]
    w_in, w_out, w_expand = weights[:3]

    @pl.when(step == 0)
    def _():
        for load in loads:
            load.start()
        loads[0].wait()

    @pl.when(step > 0)
    def _():
        for index in range(7):
            copy_out(index).wait()

    stream = load_rows(x, ("tokens", "tubes")[block], windows)
    if block == 0:
        for w in range(windows):
            store_window(extra_o, "frames", w, load_window(cotangent, "tokens", w))
    else:
        extra_o[...] = stream
    stream = stream.astype(WIDE)
    n, unused = normalize(stream)
    normed_o[...] = (n * gain[block, 0] + shift[block, 0]).astype(LOW)
    copy_out(0).start()
    for c in chunks(3 * width, width):
        triple_o[:, c] = dot(normed_o[...], w_in[:, c]).astype(LOW)
    copy_out(1).start()
    first = lax.broadcasted_iota(jnp.int32, (length, PAIR), 1) < HEAD_DIM
    ones_a, ones_b = split_heads(first, jnp.ones((length, PAIR), LOW))
    if block == 1:
        key = lax.broadcasted_iota(jnp.int32, (1, length), 1)
        kept_key = key // TUBE < counts[clip]
        bias = jnp.where(kept_key, 0.0, -1e30).astype(WIDE)
    for w in range(windows):
        span = slice(w * length, (w + 1) * length)
        for p, c in enumerate(chunks(width, PAIR)):
            queries = triple_o[span, c] * LOW(HEAD_DIM**-0.5)
            keys = triple_o[span, c.start + width : c.stop + width]
            values = triple_o[span, c.start + 2 * width : c.stop + 2 * width]
            raised = []
            for q in split_heads(first, queries):
                scores = dot(q, keys, 1, 1)
                if block == 1:
                    scores = scores + bias
                raised.append(
                    jnp.exp(scores - jnp.max(scores, axis=1, keepdims=True)).astype(LOW)
                )
            raised = jnp.concatenate(raised, axis=1)
            raised_o[w, p] = raised
            values_a, values_b = split_heads(first, values)
            sums = dot(
                raised,
                jnp.concatenate(
                    [
                        jnp.concatenate([values_a, ones_a], axis=1),
                        jnp.concatenate([values_b, ones_b], axis=1),
                    ],
                    axis=0,
                ),
            )
            recip = 1.0 / sums[:, PAIR:]
            recip_o[span, c] = recip
            attended_o[span, c] = (sums[:, :PAIR] * recip).astype(LOW)
    for index in (2, 3, 4):
        copy_out(index).start()

    @pl.when(step == 0)
    def _():
        for load in loads[1:]:
            load.wait()

    @pl.when(step > 0)
    def _():
        for index in (7, 8):
            copy_out(index).wait()

    middle = load_rows(x, ("tokens", "tubes")[block], windows).astype(WIDE)
    middle = middle + dot(attended_o[...], w_out[...])
    middle_o[...] = middle
    copy_out(5).start()
    n, unused = normalize(middle)
    normed2_o[...] = (n * gain[block, 1] + shift[block, 1]).astype(LOW)
    copy_out(6).start()
    total = middle
    for c in chunks(hidden, 512):
        pre = dot(normed2_o[...], w_expand[:, c]) + b_expand[block : block + 1, c]
        below = 0.5 + 0.5 * lax.erf(pre * HALF_ROOT)
        active = (pre * below).astype(LOW)
        active_o[:, c] = active
        slope_o[:, c] = (below + pre * (BELL_PEAK * jnp.exp(-0.5 * pre * pre))).astype(LOW)
        copy_out(7, c).start()
        copy_out(8, c).start()
        if block == 0:
            total = total + dot(active, weights[3][c, :])
    if block == 0:
        store_rows(out, "frames", windows, total.astype(LOW))

    @pl.when(step == pl.num_programs(0) - 1)
    def _():
        for index in range(9):
            copy_out(index).wait()


def output_kernel(windows, active, middle, w_reduce, *refs):
    total = middle[...] + dot(active[...], w_reduce[...])
    store_rows(refs[-1], "tubes", windows, total.astype(LOW))


def mlp_back_kernel(dims, *refs):
    block, windows, width, hidden = dims
    g, slope, middle, gain, w_expand, w_reduce = refs[:6]
    rows_o, pre_o, mid_o, bias_o, gain_o, shift_o = refs[-6:]
    grad = load_rows(g, ("frames", "tubes")[block], windows)
    rows_o[...] = grad

    @pl.when(pl.program_id(0) == 0)
    def _():
        bias_o[...] = jnp.zeros_like(bias_o)
        gain_o[...] = jnp.zeros_like(gain_o)
        shift_o[...] = jnp.zeros_like(shift_o)

    total = None
    for c in chunks(hidden, 512):
        pre = (dot(grad, w_reduce[c, :], 1, 1) * slope[:, c].astype(WIDE)).astype(LOW)
        pre_o[:, c] = pre
        bias_o[:, c] += jnp.sum(pre.astype(WIDE), axis=0, keepdims=True)
        part = dot(pre, w_expand[:, c], 1, 1)
        total = part if total is None else total + part
    n, scale = normalize(middle[...])
    gain_o[...] += jnp.sum(total * n, axis=0, keepdims=True)
    shift_o[...] += jnp.sum(total, axis=0, keepdims=True)
    mid_o[...] = grad.astype(WIDE) + normalize_back(n, scale, gain[block, 1], total)


def attention_back_kernel(dims, *refs):
    block, windows, length, width = dims
    mid, triple, recip, raised, attended, w_out = refs[:6]
    if block == 0:
        triple_o, grad_s = refs[-2:]
    else:
        triple_o, grad_s = refs[-5], refs[-1]
    grad_s[...] = dot(mid[...].astype(LOW), w_out[...], 1, 1).astype(LOW)
    first = lax.broadcasted_iota(jnp.int32, (length, PAIR), 1) < HEAD_DIM
    minus = jnp.full((length, PAIR), -1.0, LOW)
    root = HEAD_DIM**-0.5
    for w in range(windows):
        span = slice(w * length, (w + 1) * length)
        for p, c in enumerate(chunks(width, PAIR)):
            c_keys = slice(c.start + width, c.stop + width)
            c_values = slice(c.start + 2 * width, c.stop + 2 * width)
            grad = grad_s[span, c]
            grad_wide = grad.astype(WIDE)
            share = recip[span, c]
            inner = (grad_wide * attended[span, c].astype(WIDE)).astype(LOW)
            grad_scaled = (grad_wide * share).astype(LOW)
            queries = (triple[span, c].astype(WIDE) * (share * root)).astype(LOW)
            keys = triple[span, c_keys] * LOW(root)
            values = jnp.concatenate([triple[span, c_values], minus], axis=1)
            scores = []
            for i, (a, b) in enumerate(zip(split_heads(first, grad), split_heads(first, inner))):
                delta = dot(jnp.concatenate([a, b], axis=1), values, 1, 1)
                e = raised[w, p, :, i * length : (i + 1) * length]
                scores.append((e.astype(WIDE) * delta).astype(LOW))
            grad_q = (
                dot(
                    jnp.concatenate(scores, axis=1),
                    jnp.concatenate(split_heads(first, keys), axis=0),
                )
                * share
            )
            grad_k = dot(
                jnp.concatenate(scores, axis=0),
                jnp.concatenate(split_heads(first, queries), axis=0),
                0,
                0,
            )
            grad_v = dot(
                jnp.concatenate([raised[w, p, :, :length], raised[w, p, :, length:]], axis=0),
                jnp.concatenate(split_heads(first, grad_scaled), axis=0),
                0,
                0,
            )
            triple_o[span, c] = grad_q.astype(LOW)
            triple_o[span, c_keys] = grad_k.astype(LOW)
            triple_o[span, c_values] = grad_v.astype(LOW)
    if block == 1:
        x, gain, w_in = refs[6:9]
        stream_back(block, windows, "rows", "tubes", x, mid, triple_o, gain, w_in, *refs[-4:-1])


def stream_back(block, windows, x_layout, layout, x, mid, triple, gain, w_in, gain_o, shift_o, out):
    @pl.when(pl.program_id(0) == 0)
    def _():
        gain_o[...] = jnp.zeros_like(gain_o)
        shift_o[...] = jnp.zeros_like(shift_o)

    total = dot(triple[...], w_in[...], 1, 1)
    n, scale = normalize(load_rows(x, x_layout, windows).astype(WIDE))
    gain_o[...] += jnp.sum(total * n, axis=0, keepdims=True)
    shift_o[...] += jnp.sum(total, axis=0, keepdims=True)
    grad_x = (mid[...] + normalize_back(n, scale, gain[block, 0], total)).astype(LOW)
    store_rows(out, layout, windows, grad_x)


def finish_kernel(windows, x, mid, triple, gain, w_in, mixed, *refs):
    gain_o, shift_o, out, mixed_o = refs[-4:]
    stream_back(0, windows, "tokens", "tokens", x, mid, triple, gain, w_in, gain_o, shift_o, out)
    for w in range(windows):
        store_window(mixed_o, "tokens", w, load_window(mixed, "frames", w))


def split_rows(value, place, send, keep):
    value = value.astype(LOW)
    pairs, length = keep.shape[0], keep.shape[1]
    same = place % 2 == 0
    for p in range(pairs):
        low = value[2 * p * length : (2 * p + 1) * length]
        high = value[(2 * p + 1) * length : (2 * p + 2) * length]
        slot = (place // 2 % pairs) ^ p
        keep[slot] = jnp.where(same, low, high)
        send[slot] = jnp.where(same, high, low)


def outer_kernel(has_last, is_split, place, left, right, *refs):
    place = place[0]
    step = pl.program_id(0)
    outs = refs[-2:] if is_split else refs[-1:]

    def store(value):
        if is_split:
            split_rows(value, place, *outs)
        else:
            outs[0][...] = value.astype(LOW).reshape(outs[0].shape)

    if not has_last:
        store(dot(left[...], right[...], 0, 0))
        return
    last = pl.num_programs(0) - 1

    @pl.when(step < last)
    def _():
        store(dot(left[...], right[...], 0, 0))

    @pl.when(step == last)
    def _():
        store(dot(refs[0][...], refs[1][...].astype(LOW), 0, 0))


def whole(shape):
    return pl.BlockSpec(shape, lambda i: (0,) * len(shape), pipeline_mode=pl.Buffered(1))


def layer(shape, block):
    return pl.BlockSpec(
        (None,) + shape, lambda i: (block,) + (0,) * len(shape), pipeline_mode=pl.Buffered(1)
    )


def clip_spec(shape, first=0):
    if len(shape) == 2:
        return pl.BlockSpec(shape, lambda i: (i + first, 0))
    if len(shape) == 3:
        return pl.BlockSpec((1,) + shape, lambda i: (i + first, 0, 0, 0))
    return pl.BlockSpec(
        (shape[0], 1) + shape[1:], lambda i: (0, i + first) + (0,) * (len(shape) - 1)
    )


def all_clips(shape, clips):
    if len(shape) == 2:
        return (clips * shape[0], shape[1])
    if len(shape) == 3:
        return (clips,) + shape
    return (shape[0], clips) + shape[1:]


def window_spec(layout, shapes, width):
    clips, windows, length, parts = shapes
    owned = length // parts
    if layout == "tokens":
        return pl.BlockSpec((1, 1, length, width), lambda i: (i // windows, i % windows, 0, 0))
    if layout == "frames":
        return pl.BlockSpec(
            (parts, 1, 1, owned, width), lambda i: (0, i // windows, i % windows, 0, 0)
        )
    if layout == "tubes":
        return pl.BlockSpec(
            (parts, 1, windows, TUBE, width), lambda i: (0, i // windows, 0, i % windows, 0)
        )
    return pl.BlockSpec((length, width), lambda i: (i, 0))


ANY = pl.BlockSpec(memory_space=pl.ANY)
SCALARS = pl.BlockSpec(memory_space=pltpu.SMEM)


def params():
    return pltpu.CompilerParams(vmem_limit_bytes=VMEM_BYTES)


def cost(micros):
    return pl.CostEstimate(
        flops=int(micros * 350000000), bytes_accessed=int(micros * 1050000), transcendentals=0
    )


def sizes(weights, shapes):
    width, hidden = weights[4].shape[1:]
    clips, windows, length, parts = shapes
    return clips, windows, length, parts, windows * length, width, hidden


def forward(block, counts, x, cotangent, weights, saved, first, shapes, through=None):
    gain, shift, w_in, w_out, w_expand, b_expand, w_reduce = weights
    clips, windows, length, parts, rows, width, hidden = sizes(weights, shapes)
    steps = clips // 2
    travel = (parts, windows, length // parts, width)
    raised = (windows, width // PAIR, length, 2 * length)
    kept = [
        (rows, width), (rows, 3 * width), (rows, width), raised, (rows, width),
        (rows, width), (rows, width), (rows, hidden), (rows, hidden),
    ]
    types = [LOW, LOW, WIDE, LOW, LOW, WIDE, LOW, LOW, LOW]
    buffers = [pltpu.VMEM(shape, kind) for shape, kind in zip(kept, types)]
    extra = travel if block == 0 else (rows, width)
    specs = [ANY] * len(kept) + [clip_spec(extra, first)]
    outs = [
        jax.ShapeDtypeStruct((clips * shape[0],) + shape[1:], kind)
        for shape, kind in zip(kept, types)
    ]
    outs.append(jax.ShapeDtypeStruct(all_clips(extra, clips), LOW))
    loaded = [w_in, w_out, w_expand] + ([w_reduce] if block == 0 else [])
    if block == 0:
        specs = [clip_spec(travel)] + specs
        outs = [jax.ShapeDtypeStruct(all_clips(travel, steps), LOW)] + outs
        ins = [counts, x, cotangent]
        in_specs = [SCALARS] + [clip_spec(v.shape[1:], first) for v in ins[1:]]
    else:
        ins = [counts, x]
        in_specs = [SCALARS, clip_spec(travel)]
    alias = [] if saved is None else list(saved)
    base = 1 if block == 0 else 0
    if through is not None:
        specs = [ANY] + specs
        outs = [jax.ShapeDtypeStruct(through.shape, through.dtype)] + outs
        alias = [through] + alias
    ins += weights
    in_specs += [
        whole(gain.shape),
        whole(shift.shape),
        ANY,
        ANY,
        ANY,
        whole(b_expand.shape),
        ANY,
    ]
    dims = (block, windows, length, width, hidden, len(alias), first, through is not None)
    got = pl.pallas_call(
        functools.partial(forward_kernel, dims),
        grid=(steps,),
        in_specs=in_specs + [ANY] * len(alias),
        out_specs=specs,
        out_shape=outs,
        input_output_aliases={len(ins) + i: base + i for i in range(len(alias))},
        scratch_shapes=buffers
        + [pltpu.VMEM(v.shape[1:], LOW) for v in loaded]
        + [pltpu.SemaphoreType.DMA((len(kept),)), pltpu.SemaphoreType.DMA((len(loaded),))],
        compiler_params=params(),
        cost_estimate=cost(36 if block == 0 else 30),
        name=f"forward_{block}",
    )(*ins, *alias)
    if block == 0 or through is not None:
        return got[0], got[1:]
    return got


def output(active, middle, weights, shapes):
    clips, windows, length, parts, rows, width, hidden = sizes(weights, shapes)
    travel = (parts, windows, length // parts, width)
    return pl.pallas_call(
        functools.partial(output_kernel, windows),
        grid=(clips,),
        in_specs=[
            clip_spec((rows, hidden)),
            clip_spec((rows, width)),
            layer(weights[6].shape[1:], 1),
        ],
        out_specs=clip_spec(travel),
        out_shape=jax.ShapeDtypeStruct(all_clips(travel, clips), LOW),
        compiler_params=params(),
        cost_estimate=cost(14),
        name="output",
    )(active, middle, weights[6])


def mlp_back(block, g, slope, middle, weights, shapes, through=()):
    gain, shift, w_in, w_out, w_expand, b_expand, w_reduce = weights
    clips, windows, length, parts, rows, width, hidden = sizes(weights, shapes)
    travel = (parts, windows, length // parts, width)
    kinds = [
        ((rows, width), LOW), ((rows, hidden), LOW), ((rows, width), WIDE),
        ((1, hidden), WIDE), ((1, width), WIDE), ((1, width), WIDE),
    ]
    return pl.pallas_call(
        functools.partial(mlp_back_kernel, (block, windows, width, hidden)),
        grid=(clips,),
        in_specs=[
            clip_spec(travel),
            clip_spec((rows, hidden)),
            clip_spec((rows, width)),
            whole(gain.shape),
            layer(w_expand.shape[1:], block),
            layer(w_reduce.shape[1:], block),
        ]
        + [ANY] * len(through),
        out_specs=[ANY] * len(through)
        + [clip_spec(s) for s, unused in kinds[:3]]
        + [pl.BlockSpec(s, lambda i: (0, 0)) for s, unused in kinds[3:]],
        out_shape=[jax.ShapeDtypeStruct(v.shape, v.dtype) for v in through]
        + [jax.ShapeDtypeStruct(all_clips(s, clips), k) for s, k in kinds[:3]]
        + [jax.ShapeDtypeStruct(s, k) for s, k in kinds[3:]],
        input_output_aliases={6 + i: i for i in range(len(through))},
        compiler_params=params(),
        cost_estimate=cost(400),
        name=f"mlp_back_{block}",
    )(g, slope, middle, gain, w_expand, w_reduce, *through)


def attention_back(block, x, mid, triple, recip, raised, attended, weights, shapes, after=()):
    gain, shift, w_in, w_out, w_expand, b_expand, w_reduce = weights
    clips, windows, length, parts, rows, width, hidden = sizes(weights, shapes)
    travel = (parts, windows, length // parts, width)
    flat = window_spec("rows", shapes, width)
    wide = window_spec("rows", shapes, 3 * width)
    ins = [mid, triple, recip, raised, attended, w_out]
    in_specs = [
        flat,
        wide,
        flat,
        pl.BlockSpec((1,) + raised.shape[1:], lambda i: (i, 0, 0, 0)),
        flat,
        layer(w_out.shape[1:], block),
    ]
    out_specs = [wide]
    out_shape = [jax.ShapeDtypeStruct((clips * rows, 3 * width), LOW)]
    if block == 1:
        ins += [x, gain, w_in]
        in_specs += [flat, whole(gain.shape), layer(w_in.shape[1:], block)]
        out_specs += [pl.BlockSpec((1, width), lambda i: (0, 0))] * 2
        out_specs += [window_spec("tubes", shapes, width)]
        out_shape += [jax.ShapeDtypeStruct((1, width), WIDE)] * 2
        out_shape += [jax.ShapeDtypeStruct(all_clips(travel, clips), LOW)]
    return pl.pallas_call(
        functools.partial(attention_back_kernel, (block, 1, length, width)),
        grid=(clips * windows,),
        in_specs=in_specs + [ANY] * len(after),
        out_specs=out_specs,
        out_shape=out_shape,
        scratch_shapes=[pltpu.VMEM((length, width), LOW)],
        compiler_params=params(),
        cost_estimate=cost(42 if block else 0.01),
        name=f"attention_back_{block}",
    )(*ins, *after)


def finish(x, mid, triple, mixed, weights, shapes, through, after=()):
    gain, shift, w_in, w_out, w_expand, b_expand, w_reduce = weights
    clips, windows, length, parts, rows, width, hidden = sizes(weights, shapes)
    travel = (parts, windows, length // parts, width)
    tokens = (windows, length, width)
    sums = jax.ShapeDtypeStruct((1, width), WIDE)
    sums_spec = pl.BlockSpec((1, width), lambda i: (0, 0))
    return pl.pallas_call(
        functools.partial(finish_kernel, windows),
        grid=(clips,),
        in_specs=[
            clip_spec(tokens),
            clip_spec((rows, width)),
            clip_spec((rows, 3 * width)),
            whole(gain.shape),
            layer(w_in.shape[1:], 0),
            clip_spec(travel),
        ]
        + [ANY] * (len(through) + len(after)),
        out_specs=[ANY] * len(through)
        + [sums_spec, sums_spec, clip_spec(tokens), clip_spec(tokens)],
        out_shape=[jax.ShapeDtypeStruct(v.shape, v.dtype) for v in through]
        + [sums, sums]
        + [jax.ShapeDtypeStruct(all_clips(tokens, clips), LOW)] * 2,
        input_output_aliases={6 + i: i for i in range(len(through))},
        compiler_params=params(),
        cost_estimate=cost(0.01),
        name="finish",
    )(x, mid, triple, gain, w_in, mixed, *through, *after)


def outer_rows(place, active, grad, parts, is_split, after=()):
    total, width = grad.shape
    hidden = active.shape[1]
    steps = hidden // width
    group = parts // steps
    rows = hidden // parts
    if is_split:
        half = group // 2
        spec = pl.BlockSpec((half, rows, width), lambda i, place: (i ^ (place[0] // 2 // half), 0, 0))
        shape = jax.ShapeDtypeStruct((parts // 2, rows, width), LOW)
    else:
        spec = pl.BlockSpec((group, rows, width), lambda i, place: (i, 0, 0))
        shape = jax.ShapeDtypeStruct((parts, rows, width), LOW)
    arrays = 2 if is_split else 1
    return pl.pallas_call(
        functools.partial(outer_kernel, False, is_split),
        grid_spec=pltpu.PrefetchScalarGridSpec(
            num_scalar_prefetch=1,
            grid=(steps,),
            in_specs=[
                pl.BlockSpec((total, width), lambda i, place: (0, i)),
                pl.BlockSpec(
                    (total, width), lambda i, place: (0, 0), pipeline_mode=pl.Buffered(1)
                ),
            ]
            + [ANY] * len(after),
            out_specs=[spec] * arrays,
        ),
        out_shape=[shape] * arrays,
        compiler_params=params(),
        cost_estimate=cost(14),
        name="outer_rows",
    )(place, active, grad, *after)


def outer_columns(
    place, left, right, last, parts, is_split, after=(), skip=0, through=(), room=0, into=()
):
    total, width = left.shape
    steps = right.shape[1] // width
    blocks = steps + (1 if last else 0)
    ins = [place, left, right, *last]
    in_specs = [
        SCALARS,
        whole((total, width)),
        pl.BlockSpec((total, width), lambda i: (0, jnp.minimum(i, steps - 1))),
    ]
    in_specs += [whole((total, width))] * len(last)
    owners, arrays = (parts // 2, 2) if is_split else (parts, 1)
    spec = pl.BlockSpec((owners, width // parts, width), lambda i: (0, i + skip, 0))
    shape = jax.ShapeDtypeStruct((owners, (blocks + skip + room) * width // parts, width), LOW)
    aliases = {len(ins) + i: i for i in range(len(through))}
    if into:
        aliases[len(ins)] = 0
    return pl.pallas_call(
        functools.partial(outer_kernel, bool(last), is_split),
        grid=(blocks,),
        in_specs=in_specs + [ANY] * (len(into) + len(through) + len(after)),
        out_specs=[ANY] * len(through) + [spec] * arrays,
        out_shape=[jax.ShapeDtypeStruct(v.shape, v.dtype) for v in through] + [shape] * arrays,
        input_output_aliases=aliases,
        compiler_params=params(),
        cost_estimate=cost(4 * blocks if blocks > 3 else 1),
        name="outer_columns",
    )(*ins, *into, *through, *after)


def add_all(values):
    total = values[0].astype(WIDE)
    for value in values[1:]:
        total = total + value.astype(WIDE)
    return total.astype(LOW)


def swap(value, axis, offset):
    return lax.ppermute(
        value, axis, [(i, i ^ offset) for i in range(lax.axis_size(axis))]
    )


def sum_frames(send, keep, reverse):
    bits = (lax.axis_size("frame") // 2).bit_length() - 1
    shape = (2,) * bits + keep.shape[1:]
    terms = [keep.reshape(shape), swap(send, "frame", 1).reshape(shape)]
    order = list(range(1, bits + 1))
    if reverse:
        order = order[::-1]
    left = list(range(bits, 0, -1))
    for bit in order:
        axis = left.index(bit)
        left.remove(bit)
        far = add_all([lax.index_in_dim(t, 1, axis, keepdims=False) for t in terms])
        again = yield far
        if again is not None:
            terms[0] = again.reshape(shape)
        terms = [lax.index_in_dim(t, 0, axis, keepdims=False) for t in terms]
        terms.append(swap(far, "frame", 1 << bit))
    yield add_all(terms)


def last_of(steps):
    for value in steps:
        pass
    return value


def clip_blocks(total):
    size = lax.axis_size("clip")
    rows = -(-total.shape[0] // (16 * size)) * 16
    total = jnp.pad(total, ((0, rows * size - total.shape[0]), (0, 0)))
    return total.reshape(size, rows, total.shape[1])


def over_clips(*values):
    value = values[0] if len(values) == 1 else jnp.concatenate(values, axis=1)
    got = lax.all_to_all(value, "clip", 0, 0)
    cuts = [sum(v.shape[1] for v in values[: i + 1]) for i in range(len(values))]
    return [got[:, cut - v.shape[1] : cut] for cut, v in zip(cuts, values)]


def to_all_clips(value):
    return jnp.broadcast_to(value[None], (lax.axis_size("clip"),) + value.shape)


def gather_kernel(block, plan, n_in, n_outs, *refs):
    sources, outs = refs[: len(plan)], refs[n_in : n_in + n_outs]
    for source, group in zip(sources, plan):
        width = source.shape[1]
        start = 0
        for out, columns in group:
            length = outs[out].shape[1]
            for c in range(columns):
                outs[out][0, :, c * width : (c + 1) * width] = source[
                    start : start + length, :
                ].astype(WIDE)
                start += length


def gather(block, sources, plan, outs, through=()):
    filled = not isinstance(outs[0], jax.ShapeDtypeStruct)
    extra = list(outs) if filled else []
    specs = [
        pl.BlockSpec((1,) + v.shape[1:], lambda i: (block, 0, 0)) for v in outs
    ]
    ins = [*sources, *extra, *through]
    aliases = {len(sources) + i: i for i in range(len(extra))}
    aliases.update({len(ins) - len(through) + i: len(outs) + i for i in range(len(through))})
    return pl.pallas_call(
        functools.partial(gather_kernel, block, plan, len(ins), len(outs)),
        grid=(1,),
        in_specs=[whole(v.shape) for v in sources] + [ANY] * (len(extra) + len(through)),
        out_specs=specs + [ANY] * len(through),
        out_shape=[jax.ShapeDtypeStruct(v.shape, v.dtype) for v in [*outs, *through]],
        input_output_aliases=aliases,
        compiler_params=params(),
        cost_estimate=cost(4),
        name="gather",
    )(*ins)


def exchange(value):
    return lax.all_to_all(value, "frame", 0, 0)


def local(
    tokens,
    frame_counts,
    norm_gain,
    norm_bias,
    project_in,
    project_out,
    expand_weight,
    expand_bias,
    reduce_weight,
    cotangent,
):
    clips, frames, length, width = tokens.shape
    hidden = expand_weight.shape[2]
    parts = lax.axis_size("frame")
    part = width // parts
    shapes = (clips, frames, length, parts)
    half = clips // 2
    weights = (
        norm_gain, norm_bias, project_in, project_out, expand_weight, expand_bias, reduce_weight
    )
    place = lax.axis_index("frame").astype(jnp.int32).reshape(1)

    out, saved0 = forward(0, frame_counts, tokens, cotangent, weights, None, 0, shapes)
    boundary_a = exchange(out)
    out, saved0 = forward(0, frame_counts, tokens, cotangent, weights, saved0, half, shapes)
    boundary_b = exchange(out)
    cotangent_tubes, saved1 = forward(
        1, frame_counts, boundary_a, None, weights, None, 0, shapes, saved0[9]
    )
    cotangent_tubes = exchange(cotangent_tubes)
    saved1 = forward(1, frame_counts, boundary_b, None, weights, saved1, half, shapes)

    def scatter(value):
        return lax.psum_scatter(value, "frame", scatter_dimension=0, tiled=True)[0]

    normed, triple, recip, raised, attended, middle, normed2, active, slope, stream = saved1
    mixed = output(active, middle, weights, shapes)
    mixed, rows1, pre, mid, bias1, gain12, shift12 = mlp_back(
        1, cotangent_tubes, slope, middle, weights, shapes, [mixed]
    )
    mixed = exchange(mixed)
    columns = hidden // width
    (reduce1,) = outer_rows(place, active, rows1, parts, False)
    reduce1_sum = scatter(reduce1)
    grad_triple, gain11, shift11, grad_boundary = attention_back(
        1, stream, mid, triple, recip, raised, attended, weights, shapes, [reduce1]
    )
    grad_boundary = exchange(grad_boundary)
    (rest1,) = outer_columns(place, normed2, pre, [], parts, False, room=columns)
    (rest1,) = outer_columns(
        place, normed, grad_triple, [attended, mid], parts, False, [reduce1_sum], columns,
        into=[rest1],
    )

    normed, triple, recip, raised, attended, middle, normed2, active, slope = saved0[:9]
    rows0, pre, mid, bias0, gain02, shift02 = mlp_back(
        0, grad_boundary, slope, middle, weights, shapes, ()
    )
    rest1_sum = scatter(rest1)
    reduce0 = outer_rows(place, active, rows0, parts, True)
    expand0 = outer_columns(
        place, normed2, pre, [attended, mid], parts, True, [reduce0[0]]
    )
    (grad_triple,) = attention_back(
        0, None, mid, triple, recip, raised, attended, weights, shapes, [expand0[0], rest1_sum]
    )
    steps_c, steps_d = sum_frames(*reduce0, False), sum_frames(*expand0, True)
    sent = [next(steps_c), next(steps_d)]
    keep_r, keep_e, gain01, shift01, grad_tokens, mixed = finish(
        tokens, mid, grad_triple, mixed, weights, shapes,
        [reduce0[1], expand0[1]], sent,
    )
    reduce1_sum, rest1_sum = lax.psum((reduce1_sum, rest1_sum), "clip")
    sent = [steps_c.send(keep_r), steps_d.send(keep_e)]

    def by_owner(*values):
        return jnp.concatenate([v.reshape(parts, -1) for v in values], axis=1)

    small = by_owner(
        gain01, gain02, shift01, shift02, bias0, gain11, gain12, shift11, shift12, bias1
    ).astype(LOW)
    count = small.shape[1]
    small = jnp.pad(small, ((0, 0), (0, SMALL_ROWS * width - count)))
    small, send, keep = outer_columns(
        place, normed, grad_triple, [], parts, True, sent, 0,
        [small.reshape(parts, SMALL_ROWS, width)],
    )
    outs = [
        (2, hidden // parts, width),
        (2, part, hidden),
        (2, part, 3 * width),
        (2, part, width),
    ]
    outs = [jax.ShapeDtypeStruct(v, WIDE) for v in outs]
    *outs, keep = gather(
        1,
        [reduce1_sum, rest1_sum],
        (((0, 1),), ((1, columns), (2, 3), (3, 1))),
        outs,
        [keep],
    )
    cut = send.shape[1] // 2
    steps_a = sum_frames(send[:, :cut], keep[:, :cut], False)
    steps_b = sum_frames(send[:, cut:], keep[:, cut:], True)
    small = add_all(list(exchange(small)))
    last = jnp.concatenate([last_of(steps_a), last_of(steps_b)], axis=0)
    mlp0_sum = jnp.concatenate([last_of(steps_c), last_of(steps_d)], axis=0)
    (mlp0_sum,) = over_clips(clip_blocks(mlp0_sum))
    mlp0_sum = to_all_clips(add_all(list(mlp0_sum)))
    mlp0_sum, in0_sum, small = over_clips(mlp0_sum, clip_blocks(last), to_all_clips(small))
    in0_sum = to_all_clips(add_all(list(in0_sum)))
    (in0_sum,) = over_clips(in0_sum)
    small = jnp.sum(small.astype(WIDE), axis=0).reshape(-1)[:count].reshape(2, -1)
    grad_reduce, grad_expand, grad_in, grad_out = gather(
        0,
        [mlp0_sum.reshape(-1, width), in0_sum.reshape(-1, width)],
        (((0, 1), (1, columns), (3, 1)), ((2, 3),)),
        outs,
    )
    return (
        mixed,
        grad_tokens,
        small[:, : 2 * part].reshape(2, 2, part),
        small[:, 2 * part : 4 * part].reshape(2, 2, part),
        grad_in,
        grad_out,
        grad_expand,
        small[:, 4 * part :],
        grad_reduce,
    )


def solution(mesh):
    in_specs = (
        P("clip", "frame", None, None),
        P("clip"),
        P(),
        P(),
        P(),
        P(),
        P(),
        P(),
        P(),
        P("clip", "frame", None, None),
    )
    out_specs = (
        P("clip", "frame", None, None),
        P("clip", "frame", None, None),
        P(None, None, "frame"),
        P(None, None, "frame"),
        P(None, "frame", None),
        P(None, "frame", None),
        P(None, "frame", None),
        P(None, "frame"),
        P(None, "frame", None),
    )
    return jax.shard_map(local, mesh=mesh, in_specs=in_specs, out_specs=out_specs, check_vma=False)
```

```python
import functools

import jax
import jax.numpy as jnp
from jax import lax
from jax.experimental import pallas as pl
from jax.experimental.pallas import tpu as pltpu
from jax.sharding import PartitionSpec as P

HEAD_DIM = 64
TUBE = 16
PAIR = 2 * HEAD_DIM
EPSILON = 1e-05
HALF_ROOT = 0.7071067811865476
BELL_PEAK = 0.3989422804014327
LOW = jnp.bfloat16
WIDE = jnp.float32
VMEM_BYTES = 63 * 1024 * 1024
SMALL_ROWS = 16


def dot(left, right, left_dim=1, right_dim=0):
    return lax.dot_general(
        left, right, (((left_dim,), (right_dim,)), ((), ())), preferred_element_type=WIDE
    )


def normalize(x):
    center = x - jnp.mean(x, axis=-1, keepdims=True)
    scale = lax.rsqrt(jnp.mean(center * center, axis=-1, keepdims=True) + EPSILON)
    return center * scale, scale


def normalize_back(n, scale, gain, grad):
    e = grad * gain
    return scale * (
        e - jnp.mean(e, axis=-1, keepdims=True) - n * jnp.mean(e * n, axis=-1, keepdims=True)
    )


def chunks(total, size):
    return [slice(start, start + size) for start in range(0, total, size)]


def split_heads(first, value):
    zero = jnp.zeros_like(value)
    return jnp.where(first, value, zero), jnp.where(first, zero, value)


def load_window(ref, layout, window):
    if layout == "tokens":
        return ref[0, window]
    if layout == "frames":
        block = ref[:, 0, window]
    else:
        block = ref[:, 0, :, window * TUBE : (window + 1) * TUBE, :]
    return block.reshape(-1, block.shape[-1])


def load_rows(ref, layout, windows):
    if layout == "rows":
        return ref[...]
    return jnp.concatenate([load_window(ref, layout, w) for w in range(windows)], axis=0)


def store_window(ref, layout, window, value):
    if layout == "tokens":
        ref[0, window] = value
    elif layout == "frames":
        ref[:, 0, window] = value.reshape(ref.shape[0], -1, ref.shape[-1])
    else:
        tube = slice(window * TUBE, (window + 1) * TUBE)
        ref[:, 0, :, tube, :] = value.reshape(ref.shape[0], -1, TUBE, ref.shape[-1])


def store_rows(ref, layout, windows, value):
    length = value.shape[0] // windows
    for w in range(windows):
        store_window(ref, layout, w, value[w * length : (w + 1) * length])


def forward_kernel(dims, counts, x, *refs):
    block, windows, length, width, hidden, n_alias, first_clip, passes = dims
    if block == 0:
        cotangent, refs = refs[0], refs[1:]
    gain, shift, w_in_h, w_out_h, w_expand_h, b_expand, w_reduce_h = refs[:7]
    refs = refs[7 + n_alias :]
    if passes:
        refs = refs[1:]
    if block == 0:
        out, *refs = refs
    kept, extra_o, scratch = refs[:9], refs[9], refs[10:]
    buffers, weights, kept_sems, weight_sems = scratch[:9], scratch[9:-2], scratch[-2], scratch[-1]
    normed_o, triple_o, recip_o, raised_o, attended_o, middle_o, normed2_o, active_o, slope_o = buffers
    step = pl.program_id(0)
    clip = first_clip + step
    rows = windows * length

    def place(index):
        size = buffers[index].shape[0]
        return pl.ds(pl.multiple_of(clip * size, size), size)

    def copy_out(index, columns=slice(None)):
        if index == 3:
            target = kept[index].at[place(index)]
        else:
            target = kept[index].at[place(index), columns]
        source = buffers[index] if index == 3 else buffers[index].at[:, columns]
        return pltpu.make_async_copy(source, target, kept_sems.at[index])

    loads = [
        pltpu.make_async_copy(source.at[block], target, weight_sems.at[k])
        for k, (source, target) in enumerate(
            zip((w_in_h, w_out_h, w_expand_h, w_reduce_h), weights)
        )
    ]
    w_in, w_out, w_expand = weights[:3]

    @pl.when(step == 0)
    def _():
        for load in loads:
            load.start()
        loads[0].wait()

    @pl.when(step > 0)
    def _():
        for index in range(7):
            copy_out(index).wait()

    stream = load_rows(x, ("tokens", "tubes")[block], windows)
    if block == 0:
        for w in range(windows):
            store_window(extra_o, "frames", w, load_window(cotangent, "tokens", w))
    else:
        extra_o[...] = stream
    stream = stream.astype(WIDE)
    n, unused = normalize(stream)
    normed_o[...] = (n * gain[block, 0] + shift[block, 0]).astype(LOW)
    copy_out(0).start()
    for c in chunks(3 * width, width):
        triple_o[:, c] = dot(normed_o[...], w_in[:, c]).astype(LOW)
    copy_out(1).start()
    first = lax.broadcasted_iota(jnp.int32, (length, PAIR), 1) < HEAD_DIM
    ones_a, ones_b = split_heads(first, jnp.ones((length, PAIR), LOW))
    if block == 1:
        key = lax.broadcasted_iota(jnp.int32, (1, length), 1)
        kept_key = key // TUBE < counts[clip]
        bias = jnp.where(kept_key, 0.0, -1e30).astype(WIDE)
    for w in range(windows):
        span = slice(w * length, (w + 1) * length)
        for p, c in enumerate(chunks(width, PAIR)):
            queries = triple_o[span, c] * LOW(HEAD_DIM**-0.5)
            keys = triple_o[span, c.start + width : c.stop + width]
            values = triple_o[span, c.start + 2 * width : c.stop + 2 * width]
            raised = []
            for q in split_heads(first, queries):
                scores = dot(q, keys, 1, 1)
                if block == 1:
                    scores = scores + bias
                raised.append(
                    jnp.exp(scores - jnp.max(scores, axis=1, keepdims=True)).astype(LOW)
                )
            raised = jnp.concatenate(raised, axis=1)
            raised_o[w, p] = raised
            values_a, values_b = split_heads(first, values)
            sums = dot(
                raised,
                jnp.concatenate(
                    [
                        jnp.concatenate([values_a, ones_a], axis=1),
                        jnp.concatenate([values_b, ones_b], axis=1),
                    ],
                    axis=0,
                ),
            )
            recip = 1.0 / sums[:, PAIR:]
            recip_o[span, c] = recip
            attended_o[span, c] = (sums[:, :PAIR] * recip).astype(LOW)
    for index in (2, 3, 4):
        copy_out(index).start()

    @pl.when(step == 0)
    def _():
        for load in loads[1:]:
            load.wait()

    @pl.when(step > 0)
    def _():
        for index in (7, 8):
            copy_out(index).wait()

    middle = load_rows(x, ("tokens", "tubes")[block], windows).astype(WIDE)
    middle = middle + dot(attended_o[...], w_out[...])
    middle_o[...] = middle
    copy_out(5).start()
    n, unused = normalize(middle)
    normed2_o[...] = (n * gain[block, 1] + shift[block, 1]).astype(LOW)
    copy_out(6).start()
    total = middle
    for c in chunks(hidden, 512):
        pre = dot(normed2_o[...], w_expand[:, c]) + b_expand[block : block + 1, c]
        below = 0.5 + 0.5 * lax.erf(pre * HALF_ROOT)
        active = (pre * below).astype(LOW)
        active_o[:, c] = active
        slope_o[:, c] = (below + pre * (BELL_PEAK * jnp.exp(-0.5 * pre * pre))).astype(LOW)
        copy_out(7, c).start()
        copy_out(8, c).start()
        if block == 0:
            total = total + dot(active, weights[3][c, :])
    if block == 0:
        store_rows(out, "frames", windows, total.astype(LOW))

    @pl.when(step == pl.num_programs(0) - 1)
    def _():
        for index in range(9):
            copy_out(index).wait()


def output_kernel(windows, active, middle, w_reduce, *refs):
    total = middle[...] + dot(active[...], w_reduce[...])
    store_rows(refs[-1], "tubes", windows, total.astype(LOW))


def mlp_back_kernel(dims, *refs):
    block, windows, width, hidden = dims
    g, slope, middle, gain, w_expand, w_reduce = refs[:6]
    rows_o, pre_o, mid_o, bias_o, gain_o, shift_o = refs[-6:]
    grad = load_rows(g, ("frames", "tubes")[block], windows)
    rows_o[...] = grad

    @pl.when(pl.program_id(0) == 0)
    def _():
        bias_o[...] = jnp.zeros_like(bias_o)
        gain_o[...] = jnp.zeros_like(gain_o)
        shift_o[...] = jnp.zeros_like(shift_o)

    total = None
    for c in chunks(hidden, 1024):
        pre = (dot(grad, w_reduce[c, :], 1, 1) * slope[:, c].astype(WIDE)).astype(LOW)
        pre_o[:, c] = pre
        bias_o[:, c] += jnp.sum(pre.astype(WIDE), axis=0, keepdims=True)
        part = dot(pre, w_expand[:, c], 1, 1)
        total = part if total is None else total + part
    n, scale = normalize(middle[...])
    gain_o[...] += jnp.sum(total * n, axis=0, keepdims=True)
    shift_o[...] += jnp.sum(total, axis=0, keepdims=True)
    mid_o[...] = grad.astype(WIDE) + normalize_back(n, scale, gain[block, 1], total)


def attention_back_kernel(dims, *refs):
    block, windows, length, width = dims
    mid, triple, recip, raised, attended, w_out = refs[:6]
    if block == 0:
        triple_o, grad_s = refs[-2:]
    else:
        triple_o, grad_s = refs[-5], refs[-1]
    grad_s[...] = dot(mid[...].astype(LOW), w_out[...], 1, 1).astype(LOW)
    first = lax.broadcasted_iota(jnp.int32, (length, PAIR), 1) < HEAD_DIM
    minus = jnp.full((length, PAIR), -1.0, LOW)
    root = HEAD_DIM**-0.5
    for w in range(windows):
        span = slice(w * length, (w + 1) * length)
        for p, c in enumerate(chunks(width, PAIR)):
            c_keys = slice(c.start + width, c.stop + width)
            c_values = slice(c.start + 2 * width, c.stop + 2 * width)
            grad = grad_s[span, c]
            grad_wide = grad.astype(WIDE)
            share = recip[span, c]
            inner = (grad_wide * attended[span, c].astype(WIDE)).astype(LOW)
            grad_scaled = (grad_wide * share).astype(LOW)
            queries = (triple[span, c].astype(WIDE) * (share * root)).astype(LOW)
            keys = triple[span, c_keys] * LOW(root)
            values = jnp.concatenate([triple[span, c_values], minus], axis=1)
            scores = []
            for i, (a, b) in enumerate(zip(split_heads(first, grad), split_heads(first, inner))):
                delta = dot(jnp.concatenate([a, b], axis=1), values, 1, 1)
                e = raised[w, p, :, i * length : (i + 1) * length]
                scores.append((e.astype(WIDE) * delta).astype(LOW))
            grad_q = (
                dot(
                    jnp.concatenate(scores, axis=1),
                    jnp.concatenate(split_heads(first, keys), axis=0),
                )
                * share
            )
            grad_k = dot(
                jnp.concatenate(scores, axis=0),
                jnp.concatenate(split_heads(first, queries), axis=0),
                0,
                0,
            )
            grad_v = dot(
                jnp.concatenate([raised[w, p, :, :length], raised[w, p, :, length:]], axis=0),
                jnp.concatenate(split_heads(first, grad_scaled), axis=0),
                0,
                0,
            )
            triple_o[span, c] = grad_q.astype(LOW)
            triple_o[span, c_keys] = grad_k.astype(LOW)
            triple_o[span, c_values] = grad_v.astype(LOW)
    if block == 1:
        x, gain, w_in = refs[6:9]
        stream_back(block, windows, "rows", "tubes", x, mid, triple_o, gain, w_in, *refs[-4:-1])


def stream_back(block, windows, x_layout, layout, x, mid, triple, gain, w_in, gain_o, shift_o, out):
    @pl.when(pl.program_id(0) == 0)
    def _():
        gain_o[...] = jnp.zeros_like(gain_o)
        shift_o[...] = jnp.zeros_like(shift_o)

    stream = load_rows(x, x_layout, windows)
    length = stream.shape[0] // windows
    totals = [dot(triple[span, :], w_in[...], 1, 1) for span in chunks(windows * length, length)]
    for w, (span, total) in enumerate(zip(chunks(windows * length, length), totals)):
        n, scale = normalize(stream[span].astype(WIDE))
        gain_o[...] += jnp.sum(total * n, axis=0, keepdims=True)
        shift_o[...] += jnp.sum(total, axis=0, keepdims=True)
        grad_x = (mid[span, :] + normalize_back(n, scale, gain[block, 0], total)).astype(LOW)
        store_window(out, layout, w, grad_x)


def finish_kernel(windows, x, mid, triple, gain, w_in, mixed, *refs):
    gain_o, shift_o, out, mixed_o = refs[-4:]
    stream_back(0, windows, "tokens", "tokens", x, mid, triple, gain, w_in, gain_o, shift_o, out)
    for w in range(windows):
        store_window(mixed_o, "tokens", w, load_window(mixed, "frames", w))


def split_rows(value, place, send, keep):
    value = value.astype(LOW)
    pairs, length = keep.shape[0], keep.shape[1]
    same = place % 2 == 0
    for p in range(pairs):
        low = value[2 * p * length : (2 * p + 1) * length]
        high = value[(2 * p + 1) * length : (2 * p + 2) * length]
        slot = (place // 2 % pairs) ^ p
        keep[slot] = jnp.where(same, low, high)
        send[slot] = jnp.where(same, high, low)


def outer_kernel(has_last, is_split, place, left, right, *refs):
    place = place[0]
    step = pl.program_id(0)
    outs = refs[-2:] if is_split else refs[-1:]

    def store(value):
        if is_split:
            split_rows(value, place, *outs)
        else:
            outs[0][...] = value.astype(LOW).reshape(outs[0].shape)

    if not has_last:
        store(dot(left[...], right[...], 0, 0))
        return
    last = pl.num_programs(0) - 1

    @pl.when(step < last)
    def _():
        store(dot(left[...], right[...], 0, 0))

    @pl.when(step == last)
    def _():
        store(dot(refs[0][...], refs[1][...].astype(LOW), 0, 0))


def whole(shape):
    return pl.BlockSpec(shape, lambda i: (0,) * len(shape), pipeline_mode=pl.Buffered(1))


def layer(shape, block):
    return pl.BlockSpec(
        (None,) + shape, lambda i: (block,) + (0,) * len(shape), pipeline_mode=pl.Buffered(1)
    )


def clip_spec(shape, first=0):
    if len(shape) == 2:
        return pl.BlockSpec(shape, lambda i: (i + first, 0))
    if len(shape) == 3:
        return pl.BlockSpec((1,) + shape, lambda i: (i + first, 0, 0, 0))
    return pl.BlockSpec(
        (shape[0], 1) + shape[1:], lambda i: (0, i + first) + (0,) * (len(shape) - 1)
    )


def all_clips(shape, clips):
    if len(shape) == 2:
        return (clips * shape[0], shape[1])
    if len(shape) == 3:
        return (clips,) + shape
    return (shape[0], clips) + shape[1:]


def window_spec(layout, shapes, width):
    clips, windows, length, parts = shapes
    owned = length // parts
    if layout == "tokens":
        return pl.BlockSpec((1, 1, length, width), lambda i: (i // windows, i % windows, 0, 0))
    if layout == "frames":
        return pl.BlockSpec(
            (parts, 1, 1, owned, width), lambda i: (0, i // windows, i % windows, 0, 0)
        )
    if layout == "tubes":
        return pl.BlockSpec(
            (parts, 1, windows, TUBE, width), lambda i: (0, i // windows, 0, i % windows, 0)
        )
    return pl.BlockSpec((length, width), lambda i: (i, 0))


ANY = pl.BlockSpec(memory_space=pl.ANY)
SCALARS = pl.BlockSpec(memory_space=pltpu.SMEM)


def params():
    return pltpu.CompilerParams(vmem_limit_bytes=VMEM_BYTES)


def cost(micros):
    return pl.CostEstimate(
        flops=int(micros * 350000000), bytes_accessed=int(micros * 1050000), transcendentals=0
    )


def sizes(weights, shapes):
    width, hidden = weights[4].shape[1:]
    clips, windows, length, parts = shapes
    return clips, windows, length, parts, windows * length, width, hidden


def forward(block, counts, x, cotangent, weights, saved, first, shapes, through=None):
    gain, shift, w_in, w_out, w_expand, b_expand, w_reduce = weights
    clips, windows, length, parts, rows, width, hidden = sizes(weights, shapes)
    steps = clips // 2
    travel = (parts, windows, length // parts, width)
    raised = (windows, width // PAIR, length, 2 * length)
    kept = [
        (rows, width), (rows, 3 * width), (rows, width), raised, (rows, width),
        (rows, width), (rows, width), (rows, hidden), (rows, hidden),
    ]
    types = [LOW, LOW, WIDE, LOW, LOW, WIDE, LOW, LOW, LOW]
    buffers = [pltpu.VMEM(shape, kind) for shape, kind in zip(kept, types)]
    extra = travel if block == 0 else (rows, width)
    specs = [ANY] * len(kept) + [clip_spec(extra, first)]
    outs = [
        jax.ShapeDtypeStruct((clips * shape[0],) + shape[1:], kind)
        for shape, kind in zip(kept, types)
    ]
    outs.append(jax.ShapeDtypeStruct(all_clips(extra, clips), LOW))
    loaded = [w_in, w_out, w_expand] + ([w_reduce] if block == 0 else [])
    if block == 0:
        specs = [clip_spec(travel)] + specs
        outs = [jax.ShapeDtypeStruct(all_clips(travel, steps), LOW)] + outs
        ins = [counts, x, cotangent]
        in_specs = [SCALARS] + [clip_spec(v.shape[1:], first) for v in ins[1:]]
    else:
        ins = [counts, x]
        in_specs = [SCALARS, clip_spec(travel)]
    alias = [] if saved is None else list(saved)
    base = 1 if block == 0 else 0
    if through is not None:
        specs = [ANY] + specs
        outs = [jax.ShapeDtypeStruct(through.shape, through.dtype)] + outs
        alias = [through] + alias
    ins += weights
    in_specs += [
        whole(gain.shape),
        whole(shift.shape),
        ANY,
        ANY,
        ANY,
        whole(b_expand.shape),
        ANY,
    ]
    dims = (block, windows, length, width, hidden, len(alias), first, through is not None)
    got = pl.pallas_call(
        functools.partial(forward_kernel, dims),
        grid=(steps,),
        in_specs=in_specs + [ANY] * len(alias),
        out_specs=specs,
        out_shape=outs,
        input_output_aliases={len(ins) + i: base + i for i in range(len(alias))},
        scratch_shapes=buffers
        + [pltpu.VMEM(v.shape[1:], LOW) for v in loaded]
        + [pltpu.SemaphoreType.DMA((len(kept),)), pltpu.SemaphoreType.DMA((len(loaded),))],
        compiler_params=params(),
        cost_estimate=cost(36 if block == 0 else 30),
        name=f"forward_{block}",
    )(*ins, *alias)
    if block == 0 or through is not None:
        return got[0], got[1:]
    return got


def output(active, middle, weights, shapes):
    clips, windows, length, parts, rows, width, hidden = sizes(weights, shapes)
    travel = (parts, windows, length // parts, width)
    return pl.pallas_call(
        functools.partial(output_kernel, windows),
        grid=(clips,),
        in_specs=[
            clip_spec((rows, hidden)),
            clip_spec((rows, width)),
            layer(weights[6].shape[1:], 1),
        ],
        out_specs=clip_spec(travel),
        out_shape=jax.ShapeDtypeStruct(all_clips(travel, clips), LOW),
        compiler_params=params(),
        cost_estimate=cost(14),
        name="output",
    )(active, middle, weights[6])


def mlp_back(block, g, slope, middle, weights, shapes, through=()):
    gain, shift, w_in, w_out, w_expand, b_expand, w_reduce = weights
    clips, windows, length, parts, rows, width, hidden = sizes(weights, shapes)
    travel = (parts, windows, length // parts, width)
    kinds = [
        ((rows, width), LOW), ((rows, hidden), LOW), ((rows, width), WIDE),
        ((1, hidden), WIDE), ((1, width), WIDE), ((1, width), WIDE),
    ]
    return pl.pallas_call(
        functools.partial(mlp_back_kernel, (block, windows, width, hidden)),
        grid=(clips,),
        in_specs=[
            clip_spec(travel),
            clip_spec((rows, hidden)),
            clip_spec((rows, width)),
            whole(gain.shape),
            layer(w_expand.shape[1:], block),
            layer(w_reduce.shape[1:], block),
        ]
        + [ANY] * len(through),
        out_specs=[ANY] * len(through)
        + [clip_spec(s) for s, unused in kinds[:3]]
        + [pl.BlockSpec(s, lambda i: (0, 0)) for s, unused in kinds[3:]],
        out_shape=[jax.ShapeDtypeStruct(v.shape, v.dtype) for v in through]
        + [jax.ShapeDtypeStruct(all_clips(s, clips), k) for s, k in kinds[:3]]
        + [jax.ShapeDtypeStruct(s, k) for s, k in kinds[3:]],
        input_output_aliases={6 + i: i for i in range(len(through))},
        compiler_params=params(),
        cost_estimate=cost(400),
        name=f"mlp_back_{block}",
    )(g, slope, middle, gain, w_expand, w_reduce, *through)


def attention_back(block, x, mid, triple, recip, raised, attended, weights, shapes, after=()):
    gain, shift, w_in, w_out, w_expand, b_expand, w_reduce = weights
    clips, windows, length, parts, rows, width, hidden = sizes(weights, shapes)
    travel = (parts, windows, length // parts, width)
    flat = window_spec("rows", shapes, width)
    wide = window_spec("rows", shapes, 3 * width)
    ins = [mid, triple, recip, raised, attended, w_out]
    in_specs = [
        flat,
        wide,
        flat,
        pl.BlockSpec((1,) + raised.shape[1:], lambda i: (i, 0, 0, 0)),
        flat,
        layer(w_out.shape[1:], block),
    ]
    out_specs = [wide]
    out_shape = [jax.ShapeDtypeStruct((clips * rows, 3 * width), LOW)]
    if block == 1:
        ins += [x, gain, w_in]
        in_specs += [flat, whole(gain.shape), layer(w_in.shape[1:], block)]
        out_specs += [pl.BlockSpec((1, width), lambda i: (0, 0))] * 2
        out_specs += [window_spec("tubes", shapes, width)]
        out_shape += [jax.ShapeDtypeStruct((1, width), WIDE)] * 2
        out_shape += [jax.ShapeDtypeStruct(all_clips(travel, clips), LOW)]
    return pl.pallas_call(
        functools.partial(attention_back_kernel, (block, 1, length, width)),
        grid=(clips * windows,),
        in_specs=in_specs + [ANY] * len(after),
        out_specs=out_specs,
        out_shape=out_shape,
        scratch_shapes=[pltpu.VMEM((length, width), LOW)],
        compiler_params=params(),
        cost_estimate=cost(42 if block else 0.01),
        name=f"attention_back_{block}",
    )(*ins, *after)


def finish(x, mid, triple, mixed, weights, shapes, through, after=()):
    gain, shift, w_in, w_out, w_expand, b_expand, w_reduce = weights
    clips, windows, length, parts, rows, width, hidden = sizes(weights, shapes)
    travel = (parts, windows, length // parts, width)
    tokens = (windows, length, width)
    sums = jax.ShapeDtypeStruct((1, width), WIDE)
    sums_spec = pl.BlockSpec((1, width), lambda i: (0, 0))
    return pl.pallas_call(
        functools.partial(finish_kernel, windows),
        grid=(clips,),
        in_specs=[
            clip_spec(tokens),
            clip_spec((rows, width)),
            clip_spec((rows, 3 * width)),
            whole(gain.shape),
            layer(w_in.shape[1:], 0),
            clip_spec(travel),
        ]
        + [ANY] * (len(through) + len(after)),
        out_specs=[ANY] * len(through)
        + [sums_spec, sums_spec, clip_spec(tokens), clip_spec(tokens)],
        out_shape=[jax.ShapeDtypeStruct(v.shape, v.dtype) for v in through]
        + [sums, sums]
        + [jax.ShapeDtypeStruct(all_clips(tokens, clips), LOW)] * 2,
        input_output_aliases={6 + i: i for i in range(len(through))},
        compiler_params=params(),
        cost_estimate=cost(0.01),
        name="finish",
    )(x, mid, triple, gain, w_in, mixed, *through, *after)


def outer_rows(place, active, grad, parts, is_split, after=()):
    total, width = grad.shape
    hidden = active.shape[1]
    steps = hidden // width
    group = parts // steps
    rows = hidden // parts
    if is_split:
        half = group // 2
        spec = pl.BlockSpec((half, rows, width), lambda i, place: (i ^ (place[0] // 2 // half), 0, 0))
        shape = jax.ShapeDtypeStruct((parts // 2, rows, width), LOW)
    else:
        spec = pl.BlockSpec((group, rows, width), lambda i, place: (i, 0, 0))
        shape = jax.ShapeDtypeStruct((parts, rows, width), LOW)
    arrays = 2 if is_split else 1
    return pl.pallas_call(
        functools.partial(outer_kernel, False, is_split),
        grid_spec=pltpu.PrefetchScalarGridSpec(
            num_scalar_prefetch=1,
            grid=(steps,),
            in_specs=[
                pl.BlockSpec((total, width), lambda i, place: (0, i)),
                pl.BlockSpec(
                    (total, width), lambda i, place: (0, 0), pipeline_mode=pl.Buffered(1)
                ),
            ]
            + [ANY] * len(after),
            out_specs=[spec] * arrays,
        ),
        out_shape=[shape] * arrays,
        compiler_params=params(),
        cost_estimate=cost(14),
        name="outer_rows",
    )(place, active, grad, *after)


def outer_columns(
    place, left, right, last, parts, is_split, after=(), skip=0, through=(), room=0, into=()
):
    total, width = left.shape
    steps = right.shape[1] // width
    blocks = steps + (1 if last else 0)
    ins = [place, left, right, *last]
    in_specs = [
        SCALARS,
        whole((total, width)),
        pl.BlockSpec((total, width), lambda i: (0, jnp.minimum(i, steps - 1))),
    ]
    in_specs += [whole((total, width))] * len(last)
    owners, arrays = (parts // 2, 2) if is_split else (parts, 1)
    spec = pl.BlockSpec((owners, width // parts, width), lambda i: (0, i + skip, 0))
    shape = jax.ShapeDtypeStruct((owners, (blocks + skip + room) * width // parts, width), LOW)
    aliases = {len(ins) + i: i for i in range(len(through))}
    if into:
        aliases[len(ins)] = 0
    return pl.pallas_call(
        functools.partial(outer_kernel, bool(last), is_split),
        grid=(blocks,),
        in_specs=in_specs + [ANY] * (len(into) + len(through) + len(after)),
        out_specs=[ANY] * len(through) + [spec] * arrays,
        out_shape=[jax.ShapeDtypeStruct(v.shape, v.dtype) for v in through] + [shape] * arrays,
        input_output_aliases=aliases,
        compiler_params=params(),
        cost_estimate=cost(4 * blocks if blocks > 3 else 1),
        name="outer_columns",
    )(*ins, *into, *through, *after)


def add_all(values):
    total = values[0].astype(WIDE)
    for value in values[1:]:
        total = total + value.astype(WIDE)
    return total.astype(LOW)


def swap(value, axis, offset):
    return lax.ppermute(
        value, axis, [(i, i ^ offset) for i in range(lax.axis_size(axis))]
    )


def sum_frames(send, keep, reverse):
    bits = (lax.axis_size("frame") // 2).bit_length() - 1
    shape = (2,) * bits + keep.shape[1:]
    terms = [keep.reshape(shape), swap(send, "frame", 1).reshape(shape)]
    order = list(range(1, bits + 1))
    if reverse:
        order = order[::-1]
    left = list(range(bits, 0, -1))
    for bit in order:
        axis = left.index(bit)
        left.remove(bit)
        far = add_all([lax.index_in_dim(t, 1, axis, keepdims=False) for t in terms])
        again = yield far
        if again is not None:
            terms[0] = again.reshape(shape)
        terms = [lax.index_in_dim(t, 0, axis, keepdims=False) for t in terms]
        terms.append(swap(far, "frame", 1 << bit))
    yield add_all(terms)


def last_of(steps):
    for value in steps:
        pass
    return value


def clip_blocks(total):
    size = lax.axis_size("clip")
    rows = -(-total.shape[0] // (16 * size)) * 16
    total = jnp.pad(total, ((0, rows * size - total.shape[0]), (0, 0)))
    return total.reshape(size, rows, total.shape[1])


def over_clips(*values):
    value = values[0] if len(values) == 1 else jnp.concatenate(values, axis=1)
    got = lax.all_to_all(value, "clip", 0, 0)
    cuts = [sum(v.shape[1] for v in values[: i + 1]) for i in range(len(values))]
    return [got[:, cut - v.shape[1] : cut] for cut, v in zip(cuts, values)]


def to_all_clips(value):
    return jnp.broadcast_to(value[None], (lax.axis_size("clip"),) + value.shape)


def gather_kernel(block, plan, n_in, n_outs, *refs):
    sources, outs = refs[: len(plan)], refs[n_in : n_in + n_outs]
    for source, group in zip(sources, plan):
        width = source.shape[1]
        start = 0
        for out, columns in group:
            length = outs[out].shape[1]
            for c in range(columns):
                outs[out][0, :, c * width : (c + 1) * width] = source[
                    start : start + length, :
                ].astype(WIDE)
                start += length


def gather(block, sources, plan, outs, through=()):
    filled = not isinstance(outs[0], jax.ShapeDtypeStruct)
    extra = list(outs) if filled else []
    specs = [
        pl.BlockSpec((1,) + v.shape[1:], lambda i: (block, 0, 0)) for v in outs
    ]
    ins = [*sources, *extra, *through]
    aliases = {len(sources) + i: i for i in range(len(extra))}
    aliases.update({len(ins) - len(through) + i: len(outs) + i for i in range(len(through))})
    return pl.pallas_call(
        functools.partial(gather_kernel, block, plan, len(ins), len(outs)),
        grid=(1,),
        in_specs=[whole(v.shape) for v in sources] + [ANY] * (len(extra) + len(through)),
        out_specs=specs + [ANY] * len(through),
        out_shape=[jax.ShapeDtypeStruct(v.shape, v.dtype) for v in [*outs, *through]],
        input_output_aliases=aliases,
        compiler_params=params(),
        cost_estimate=cost(4),
        name="gather",
    )(*ins)


def exchange(value):
    return lax.all_to_all(value, "frame", 0, 0)


def local(
    tokens,
    frame_counts,
    norm_gain,
    norm_bias,
    project_in,
    project_out,
    expand_weight,
    expand_bias,
    reduce_weight,
    cotangent,
):
    clips, frames, length, width = tokens.shape
    hidden = expand_weight.shape[2]
    parts = lax.axis_size("frame")
    part = width // parts
    shapes = (clips, frames, length, parts)
    half = clips // 2
    weights = (
        norm_gain, norm_bias, project_in, project_out, expand_weight, expand_bias, reduce_weight
    )
    place = lax.axis_index("frame").astype(jnp.int32).reshape(1)

    out, saved0 = forward(0, frame_counts, tokens, cotangent, weights, None, 0, shapes)
    boundary_a = exchange(out)
    out, saved0 = forward(0, frame_counts, tokens, cotangent, weights, saved0, half, shapes)
    boundary_b = exchange(out)
    cotangent_tubes, saved1 = forward(
        1, frame_counts, boundary_a, None, weights, None, 0, shapes, saved0[9]
    )
    cotangent_tubes = exchange(cotangent_tubes)
    saved1 = forward(1, frame_counts, boundary_b, None, weights, saved1, half, shapes)

    def scatter(value):
        return lax.psum_scatter(value, "frame", scatter_dimension=0, tiled=True)[0]

    normed, triple, recip, raised, attended, middle, normed2, active, slope, stream = saved1
    mixed = output(active, middle, weights, shapes)
    mixed, rows1, pre, mid, bias1, gain12, shift12 = mlp_back(
        1, cotangent_tubes, slope, middle, weights, shapes, [mixed]
    )
    mixed = exchange(mixed)
    columns = hidden // width
    (reduce1,) = outer_rows(place, active, rows1, parts, False)
    reduce1_sum = scatter(reduce1)
    grad_triple, gain11, shift11, grad_boundary = attention_back(
        1, stream, mid, triple, recip, raised, attended, weights, shapes, [reduce1]
    )
    grad_boundary = exchange(grad_boundary)
    (rest1,) = outer_columns(place, normed2, pre, [], parts, False, room=columns)
    (rest1,) = outer_columns(
        place, normed, grad_triple, [attended, mid], parts, False, [reduce1_sum], columns,
        into=[rest1],
    )

    normed, triple, recip, raised, attended, middle, normed2, active, slope = saved0[:9]
    rows0, pre, mid, bias0, gain02, shift02 = mlp_back(
        0, grad_boundary, slope, middle, weights, shapes, ()
    )
    rest1_sum = scatter(rest1)
    reduce0 = outer_rows(place, active, rows0, parts, True)
    expand0 = outer_columns(
        place, normed2, pre, [attended, mid], parts, True, [reduce0[0]]
    )
    (grad_triple,) = attention_back(
        0, None, mid, triple, recip, raised, attended, weights, shapes, [expand0[0], rest1_sum]
    )
    steps_c, steps_d = sum_frames(*reduce0, False), sum_frames(*expand0, True)
    sent = [next(steps_c), next(steps_d)]
    keep_r, keep_e, gain01, shift01, grad_tokens, mixed = finish(
        tokens, mid, grad_triple, mixed, weights, shapes,
        [reduce0[1], expand0[1]], sent,
    )
    reduce1_sum, rest1_sum = lax.psum((reduce1_sum, rest1_sum), "clip")
    sent = [steps_c.send(keep_r), steps_d.send(keep_e)]

    def by_owner(*values):
        return jnp.concatenate([v.reshape(parts, -1) for v in values], axis=1)

    small = by_owner(
        gain01, gain02, shift01, shift02, bias0, gain11, gain12, shift11, shift12, bias1
    ).astype(LOW)
    count = small.shape[1]
    small = jnp.pad(small, ((0, 0), (0, SMALL_ROWS * width - count)))
    small, send, keep = outer_columns(
        place, normed, grad_triple, [], parts, True, sent, 0,
        [small.reshape(parts, SMALL_ROWS, width)],
    )
    outs = [
        (2, hidden // parts, width),
        (2, part, hidden),
        (2, part, 3 * width),
        (2, part, width),
    ]
    outs = [jax.ShapeDtypeStruct(v, WIDE) for v in outs]
    *outs, keep = gather(
        1,
        [reduce1_sum, rest1_sum],
        (((0, 1),), ((1, columns), (2, 3), (3, 1))),
        outs,
        [keep],
    )
    cut = send.shape[1] // 2
    steps_a = sum_frames(send[:, :cut], keep[:, :cut], False)
    steps_b = sum_frames(send[:, cut:], keep[:, cut:], True)
    small = add_all(list(exchange(small)))
    last = jnp.concatenate([last_of(steps_a), last_of(steps_b)], axis=0)
    mlp0_sum = jnp.concatenate([last_of(steps_c), last_of(steps_d)], axis=0)
    (mlp0_sum,) = over_clips(clip_blocks(mlp0_sum))
    mlp0_sum = to_all_clips(add_all(list(mlp0_sum)))
    mlp0_sum, in0_sum, small = over_clips(mlp0_sum, clip_blocks(last), to_all_clips(small))
    in0_sum = to_all_clips(add_all(list(in0_sum)))
    (in0_sum,) = over_clips(in0_sum)
    small = jnp.sum(small.astype(WIDE), axis=0).reshape(-1)[:count].reshape(2, -1)
    grad_reduce, grad_expand, grad_in, grad_out = gather(
        0,
        [mlp0_sum.reshape(-1, width), in0_sum.reshape(-1, width)],
        (((0, 1), (1, columns), (3, 1)), ((2, 3),)),
        outs,
    )
    return (
        mixed,
        grad_tokens,
        small[:, : 2 * part].reshape(2, 2, part),
        small[:, 2 * part : 4 * part].reshape(2, 2, part),
        grad_in,
        grad_out,
        grad_expand,
        small[:, 4 * part :],
        grad_reduce,
    )


def solution(mesh):
    in_specs = (
        P("clip", "frame", None, None),
        P("clip"),
        P(),
        P(),
        P(),
        P(),
        P(),
        P(),
        P(),
        P("clip", "frame", None, None),
    )
    out_specs = (
        P("clip", "frame", None, None),
        P("clip", "frame", None, None),
        P(None, None, "frame"),
        P(None, None, "frame"),
        P(None, "frame", None),
        P(None, "frame", None),
        P(None, "frame", None),
        P(None, "frame"),
        P(None, "frame", None),
    )
    return jax.shard_map(local, mesh=mesh, in_specs=in_specs, out_specs=out_specs, check_vma=False)
```

```python
import functools

import jax
import jax.numpy as jnp
from jax import lax
from jax.experimental import pallas as pl
from jax.experimental.pallas import tpu as pltpu
from jax.sharding import PartitionSpec as P

HEAD_DIM = 64
TUBE = 16
PAIR = 2 * HEAD_DIM
EPSILON = 1e-05
HALF_ROOT = 0.7071067811865476
BELL_PEAK = 0.3989422804014327
LOW = jnp.bfloat16
WIDE = jnp.float32
VMEM_BYTES = 63 * 1024 * 1024
SMALL_ROWS = 16


def dot(left, right, left_dim=1, right_dim=0):
    return lax.dot_general(
        left, right, (((left_dim,), (right_dim,)), ((), ())), preferred_element_type=WIDE
    )


def normalize(x):
    center = x - jnp.mean(x, axis=-1, keepdims=True)
    scale = lax.rsqrt(jnp.mean(center * center, axis=-1, keepdims=True) + EPSILON)
    return center * scale, scale


def normalize_back(n, scale, gain, grad):
    e = grad * gain
    return scale * (
        e - jnp.mean(e, axis=-1, keepdims=True) - n * jnp.mean(e * n, axis=-1, keepdims=True)
    )


def chunks(total, size):
    return [slice(start, start + size) for start in range(0, total, size)]


def split_heads(first, value):
    zero = jnp.zeros_like(value)
    return jnp.where(first, value, zero), jnp.where(first, zero, value)


def load_window(ref, layout, window):
    if layout == "tokens":
        return ref[0, window]
    if layout == "frames":
        block = ref[:, 0, window]
    else:
        block = ref[:, 0, :, window * TUBE : (window + 1) * TUBE, :]
    return block.reshape(-1, block.shape[-1])


def load_rows(ref, layout, windows):
    if layout == "rows":
        return ref[...]
    return jnp.concatenate([load_window(ref, layout, w) for w in range(windows)], axis=0)


def store_window(ref, layout, window, value):
    if layout == "tokens":
        ref[0, window] = value
    elif layout == "frames":
        ref[:, 0, window] = value.reshape(ref.shape[0], -1, ref.shape[-1])
    else:
        tube = slice(window * TUBE, (window + 1) * TUBE)
        ref[:, 0, :, tube, :] = value.reshape(ref.shape[0], -1, TUBE, ref.shape[-1])


def store_rows(ref, layout, windows, value):
    length = value.shape[0] // windows
    for w in range(windows):
        store_window(ref, layout, w, value[w * length : (w + 1) * length])


def forward_kernel(dims, counts, x, *refs):
    block, windows, length, width, hidden, n_alias, first_clip, passes = dims
    if block == 0:
        cotangent, refs = refs[0], refs[1:]
    gain, shift, w_in_h, w_out_h, w_expand_h, b_expand, w_reduce_h = refs[:7]
    refs = refs[7 + n_alias :]
    if passes:
        refs = refs[1:]
    if block == 0:
        out, *refs = refs
    kept, extra_o, scratch = refs[:9], refs[9], refs[10:]
    buffers, weights, kept_sems, weight_sems = scratch[:9], scratch[9:-2], scratch[-2], scratch[-1]
    normed_o, triple_o, recip_o, raised_o, attended_o, middle_o, normed2_o, active_o, slope_o = buffers
    step = pl.program_id(0)
    clip = first_clip + step
    rows = windows * length

    def place(index):
        size = buffers[index].shape[0]
        return pl.ds(pl.multiple_of(clip * size, size), size)

    def copy_out(index, columns=slice(None)):
        if index == 3:
            target = kept[index].at[place(index)]
        else:
            target = kept[index].at[place(index), columns]
        source = buffers[index] if index == 3 else buffers[index].at[:, columns]
        return pltpu.make_async_copy(source, target, kept_sems.at[index])

    loads = [
        pltpu.make_async_copy(source.at[block], target, weight_sems.at[k])
        for k, (source, target) in enumerate(
            zip((w_in_h, w_out_h, w_expand_h, w_reduce_h), weights)
        )
    ]
    w_in, w_out, w_expand = weights[:3]

    @pl.when(step == 0)
    def _():
        for load in loads:
            load.start()
        loads[0].wait()

    @pl.when(step > 0)
    def _():
        for index in range(7):
            copy_out(index).wait()

    stream = load_rows(x, ("tokens", "tubes")[block], windows)
    if block == 0:
        for w in range(windows):
            store_window(extra_o, "frames", w, load_window(cotangent, "tokens", w))
    else:
        extra_o[...] = stream
    stream = stream.astype(WIDE)
    n, unused = normalize(stream)
    normed_o[...] = (n * gain[block, 0] + shift[block, 0]).astype(LOW)
    copy_out(0).start()
    for c in chunks(3 * width, width):
        triple_o[:, c] = dot(normed_o[...], w_in[:, c]).astype(LOW)
    copy_out(1).start()
    first = lax.broadcasted_iota(jnp.int32, (length, PAIR), 1) < HEAD_DIM
    ones_a, ones_b = split_heads(first, jnp.ones((length, PAIR), LOW))
    if block == 1:
        key = lax.broadcasted_iota(jnp.int32, (1, length), 1)
        kept_key = key // TUBE < counts[clip]
        bias = jnp.where(kept_key, 0.0, -1e30).astype(WIDE)
    for w in range(windows):
        span = slice(w * length, (w + 1) * length)
        for p, c in enumerate(chunks(width, PAIR)):
            queries = triple_o[span, c] * LOW(HEAD_DIM**-0.5)
            keys = triple_o[span, c.start + width : c.stop + width]
            values = triple_o[span, c.start + 2 * width : c.stop + 2 * width]
            raised = []
            for q in split_heads(first, queries):
                scores = dot(q, keys, 1, 1)
                if block == 1:
                    scores = scores + bias
                raised.append(
                    jnp.exp(scores - jnp.max(scores, axis=1, keepdims=True)).astype(LOW)
                )
            raised = jnp.concatenate(raised, axis=1)
            raised_o[w, p] = raised
            values_a, values_b = split_heads(first, values)
            sums = dot(
                raised,
                jnp.concatenate(
                    [
                        jnp.concatenate([values_a, ones_a], axis=1),
                        jnp.concatenate([values_b, ones_b], axis=1),
                    ],
                    axis=0,
                ),
            )
            recip = 1.0 / sums[:, PAIR:]
            recip_o[span, c] = recip
            attended_o[span, c] = (sums[:, :PAIR] * recip).astype(LOW)
    for index in (2, 3, 4):
        copy_out(index).start()

    @pl.when(step == 0)
    def _():
        for load in loads[1:]:
            load.wait()

    @pl.when(step > 0)
    def _():
        for index in (7, 8):
            copy_out(index).wait()

    middle = load_rows(x, ("tokens", "tubes")[block], windows).astype(WIDE)
    middle = middle + dot(attended_o[...], w_out[...])
    middle_o[...] = middle
    copy_out(5).start()
    n, unused = normalize(middle)
    normed2_o[...] = (n * gain[block, 1] + shift[block, 1]).astype(LOW)
    copy_out(6).start()
    total = middle
    for c in chunks(hidden, 512):
        pre = dot(normed2_o[...], w_expand[:, c]) + b_expand[block : block + 1, c]
        below = 0.5 + 0.5 * lax.erf(pre * HALF_ROOT)
        active = (pre * below).astype(LOW)
        active_o[:, c] = active
        slope_o[:, c] = (below + pre * (BELL_PEAK * jnp.exp(-0.5 * pre * pre))).astype(LOW)
        copy_out(7, c).start()
        copy_out(8, c).start()
        if block == 0:
            total = total + dot(active, weights[3][c, :])
    if block == 0:
        store_rows(out, "frames", windows, total.astype(LOW))

    @pl.when(step == pl.num_programs(0) - 1)
    def _():
        for index in range(9):
            copy_out(index).wait()


def output_kernel(windows, active, middle, w_reduce, *refs):
    total = middle[...] + dot(active[...], w_reduce[...])
    store_rows(refs[-1], "tubes", windows, total.astype(LOW))


def mlp_back_kernel(dims, *refs):
    block, windows, width, hidden = dims
    g, slope, middle, gain, w_expand, w_reduce = refs[:6]
    rows_o, pre_o, mid_o, bias_o, gain_o, shift_o = refs[-6:]
    grad = load_rows(g, ("frames", "tubes")[block], windows)
    rows_o[...] = grad

    @pl.when(pl.program_id(0) == 0)
    def _():
        bias_o[...] = jnp.zeros_like(bias_o)
        gain_o[...] = jnp.zeros_like(gain_o)
        shift_o[...] = jnp.zeros_like(shift_o)

    total = None
    for c in chunks(hidden, 1024):
        pre = (dot(grad, w_reduce[c, :], 1, 1) * slope[:, c].astype(WIDE)).astype(LOW)
        pre_o[:, c] = pre
        bias_o[:, c] += jnp.sum(pre.astype(WIDE), axis=0, keepdims=True)
        part = dot(pre, w_expand[:, c], 1, 1)
        total = part if total is None else total + part
    n, scale = normalize(middle[...])
    gain_o[...] += jnp.sum(total * n, axis=0, keepdims=True)
    shift_o[...] += jnp.sum(total, axis=0, keepdims=True)
    mid_o[...] = grad.astype(WIDE) + normalize_back(n, scale, gain[block, 1], total)


def attention_back_kernel(dims, *refs):
    block, windows, length, width = dims
    mid, triple, recip, raised, attended, w_out = refs[:6]
    if block == 0:
        triple_o, grad_s = refs[-2:]
    else:
        triple_o, grad_s = refs[-5], refs[-1]
    grad_s[...] = dot(mid[...].astype(LOW), w_out[...], 1, 1).astype(LOW)
    first = lax.broadcasted_iota(jnp.int32, (length, PAIR), 1) < HEAD_DIM
    minus = jnp.full((length, PAIR), -1.0, LOW)
    root = HEAD_DIM**-0.5
    for w in range(windows):
        span = slice(w * length, (w + 1) * length)
        for p, c in enumerate(chunks(width, PAIR)):
            c_keys = slice(c.start + width, c.stop + width)
            c_values = slice(c.start + 2 * width, c.stop + 2 * width)
            grad = grad_s[span, c]
            grad_wide = grad.astype(WIDE)
            share = recip[span, c]
            inner = (grad_wide * attended[span, c].astype(WIDE)).astype(LOW)
            grad_scaled = (grad_wide * share).astype(LOW)
            queries = (triple[span, c].astype(WIDE) * (share * root)).astype(LOW)
            keys = triple[span, c_keys] * LOW(root)
            values = jnp.concatenate([triple[span, c_values], minus], axis=1)
            scores = []
            for i, (a, b) in enumerate(zip(split_heads(first, grad), split_heads(first, inner))):
                delta = dot(jnp.concatenate([a, b], axis=1), values, 1, 1)
                e = raised[w, p, :, i * length : (i + 1) * length]
                scores.append((e.astype(WIDE) * delta).astype(LOW))
            grad_q = (
                dot(
                    jnp.concatenate(scores, axis=1),
                    jnp.concatenate(split_heads(first, keys), axis=0),
                )
                * share
            )
            grad_k = dot(
                jnp.concatenate(scores, axis=0),
                jnp.concatenate(split_heads(first, queries), axis=0),
                0,
                0,
            )
            grad_v = dot(
                jnp.concatenate([raised[w, p, :, :length], raised[w, p, :, length:]], axis=0),
                jnp.concatenate(split_heads(first, grad_scaled), axis=0),
                0,
                0,
            )
            triple_o[span, c] = grad_q.astype(LOW)
            triple_o[span, c_keys] = grad_k.astype(LOW)
            triple_o[span, c_values] = grad_v.astype(LOW)
    if block == 1:
        x, gain, w_in = refs[6:9]
        stream_back(block, windows, "rows", "tubes", x, mid, triple_o, gain, w_in, *refs[-4:-1])


def stream_back(block, windows, x_layout, layout, x, mid, triple, gain, w_in, gain_o, shift_o, out):
    @pl.when(pl.program_id(0) == 0)
    def _():
        gain_o[...] = jnp.zeros_like(gain_o)
        shift_o[...] = jnp.zeros_like(shift_o)

    stream = load_rows(x, x_layout, windows)
    length = stream.shape[0] // windows
    totals = [dot(triple[span, :], w_in[...], 1, 1) for span in chunks(windows * length, length)]
    for w, (span, total) in enumerate(zip(chunks(windows * length, length), totals)):
        n, scale = normalize(stream[span].astype(WIDE))
        gain_o[...] += jnp.sum(total * n, axis=0, keepdims=True)
        shift_o[...] += jnp.sum(total, axis=0, keepdims=True)
        grad_x = (mid[span, :] + normalize_back(n, scale, gain[block, 0], total)).astype(LOW)
        store_window(out, layout, w, grad_x)


def finish_kernel(windows, x, mid, triple, gain, w_in, mixed, *refs):
    gain_o, shift_o, out, mixed_o = refs[-4:]
    stream_back(0, windows, "tokens", "tokens", x, mid, triple, gain, w_in, gain_o, shift_o, out)
    for w in range(windows):
        store_window(mixed_o, "tokens", w, load_window(mixed, "frames", w))


def split_rows(value, place, send, keep):
    value = value.astype(LOW)
    pairs, length = keep.shape[0], keep.shape[1]
    same = place % 2 == 0
    for p in range(pairs):
        low = value[2 * p * length : (2 * p + 1) * length]
        high = value[(2 * p + 1) * length : (2 * p + 2) * length]
        slot = (place // 2 % pairs) ^ p
        keep[slot] = jnp.where(same, low, high)
        send[slot] = jnp.where(same, high, low)


def outer_kernel(has_last, is_split, place, left, right, *refs):
    place = place[0]
    step = pl.program_id(0)
    outs = refs[-2:] if is_split else refs[-1:]

    def store(value):
        if is_split:
            split_rows(value, place, *outs)
        else:
            outs[0][...] = value.astype(LOW).reshape(outs[0].shape)

    if not has_last:
        store(dot(left[...], right[...], 0, 0))
        return
    last = pl.num_programs(0) - 1

    @pl.when(step < last)
    def _():
        store(dot(left[...], right[...], 0, 0))

    @pl.when(step == last)
    def _():
        store(dot(refs[0][...], refs[1][...].astype(LOW), 0, 0))


def whole(shape):
    return pl.BlockSpec(shape, lambda i: (0,) * len(shape), pipeline_mode=pl.Buffered(1))


def layer(shape, block):
    return pl.BlockSpec(
        (None,) + shape, lambda i: (block,) + (0,) * len(shape), pipeline_mode=pl.Buffered(1)
    )


def clip_spec(shape, first=0):
    if len(shape) == 2:
        return pl.BlockSpec(shape, lambda i: (i + first, 0))
    if len(shape) == 3:
        return pl.BlockSpec((1,) + shape, lambda i: (i + first, 0, 0, 0))
    return pl.BlockSpec(
        (shape[0], 1) + shape[1:], lambda i: (0, i + first) + (0,) * (len(shape) - 1)
    )


def all_clips(shape, clips):
    if len(shape) == 2:
        return (clips * shape[0], shape[1])
    if len(shape) == 3:
        return (clips,) + shape
    return (shape[0], clips) + shape[1:]


def window_spec(layout, shapes, width):
    clips, windows, length, parts = shapes
    owned = length // parts
    if layout == "tokens":
        return pl.BlockSpec((1, 1, length, width), lambda i: (i // windows, i % windows, 0, 0))
    if layout == "frames":
        return pl.BlockSpec(
            (parts, 1, 1, owned, width), lambda i: (0, i // windows, i % windows, 0, 0)
        )
    if layout == "tubes":
        return pl.BlockSpec(
            (parts, 1, windows, TUBE, width), lambda i: (0, i // windows, 0, i % windows, 0)
        )
    return pl.BlockSpec((length, width), lambda i: (i, 0))


ANY = pl.BlockSpec(memory_space=pl.ANY)
SCALARS = pl.BlockSpec(memory_space=pltpu.SMEM)


def params():
    return pltpu.CompilerParams(vmem_limit_bytes=VMEM_BYTES)


def cost(micros):
    return pl.CostEstimate(
        flops=int(micros * 350000000), bytes_accessed=int(micros * 1050000), transcendentals=0
    )


def sizes(weights, shapes):
    width, hidden = weights[4].shape[1:]
    clips, windows, length, parts = shapes
    return clips, windows, length, parts, windows * length, width, hidden


def forward(block, counts, x, cotangent, weights, saved, first, shapes, through=None):
    gain, shift, w_in, w_out, w_expand, b_expand, w_reduce = weights
    clips, windows, length, parts, rows, width, hidden = sizes(weights, shapes)
    steps = clips // 2
    travel = (parts, windows, length // parts, width)
    raised = (windows, width // PAIR, length, 2 * length)
    kept = [
        (rows, width), (rows, 3 * width), (rows, width), raised, (rows, width),
        (rows, width), (rows, width), (rows, hidden), (rows, hidden),
    ]
    types = [LOW, LOW, WIDE, LOW, LOW, WIDE, LOW, LOW, LOW]
    buffers = [pltpu.VMEM(shape, kind) for shape, kind in zip(kept, types)]
    extra = travel if block == 0 else (rows, width)
    specs = [ANY] * len(kept) + [clip_spec(extra, first)]
    outs = [
        jax.ShapeDtypeStruct((clips * shape[0],) + shape[1:], kind)
        for shape, kind in zip(kept, types)
    ]
    outs.append(jax.ShapeDtypeStruct(all_clips(extra, clips), LOW))
    loaded = [w_in, w_out, w_expand] + ([w_reduce] if block == 0 else [])
    if block == 0:
        specs = [clip_spec(travel)] + specs
        outs = [jax.ShapeDtypeStruct(all_clips(travel, steps), LOW)] + outs
        ins = [counts, x, cotangent]
        in_specs = [SCALARS] + [clip_spec(v.shape[1:], first) for v in ins[1:]]
    else:
        ins = [counts, x]
        in_specs = [SCALARS, clip_spec(travel)]
    alias = [] if saved is None else list(saved)
    base = 1 if block == 0 else 0
    if through is not None:
        specs = [ANY] + specs
        outs = [jax.ShapeDtypeStruct(through.shape, through.dtype)] + outs
        alias = [through] + alias
    ins += weights
    in_specs += [
        whole(gain.shape),
        whole(shift.shape),
        ANY,
        ANY,
        ANY,
        whole(b_expand.shape),
        ANY,
    ]
    dims = (block, windows, length, width, hidden, len(alias), first, through is not None)
    got = pl.pallas_call(
        functools.partial(forward_kernel, dims),
        grid=(steps,),
        in_specs=in_specs + [ANY] * len(alias),
        out_specs=specs,
        out_shape=outs,
        input_output_aliases={len(ins) + i: base + i for i in range(len(alias))},
        scratch_shapes=buffers
        + [pltpu.VMEM(v.shape[1:], LOW) for v in loaded]
        + [pltpu.SemaphoreType.DMA((len(kept),)), pltpu.SemaphoreType.DMA((len(loaded),))],
        compiler_params=params(),
        cost_estimate=cost(36 if block == 0 else 30),
        name=f"forward_{block}",
    )(*ins, *alias)
    if block == 0 or through is not None:
        return got[0], got[1:]
    return got


def output(active, middle, weights, shapes):
    clips, windows, length, parts, rows, width, hidden = sizes(weights, shapes)
    travel = (parts, windows, length // parts, width)
    return pl.pallas_call(
        functools.partial(output_kernel, windows),
        grid=(clips,),
        in_specs=[
            clip_spec((rows, hidden)),
            clip_spec((rows, width)),
            layer(weights[6].shape[1:], 1),
        ],
        out_specs=clip_spec(travel),
        out_shape=jax.ShapeDtypeStruct(all_clips(travel, clips), LOW),
        compiler_params=params(),
        cost_estimate=cost(14),
        name="output",
    )(active, middle, weights[6])


def mlp_back(block, g, slope, middle, weights, shapes, through=()):
    gain, shift, w_in, w_out, w_expand, b_expand, w_reduce = weights
    clips, windows, length, parts, rows, width, hidden = sizes(weights, shapes)
    travel = (parts, windows, length // parts, width)
    kinds = [
        ((rows, width), LOW), ((rows, hidden), LOW), ((rows, width), WIDE),
        ((1, hidden), WIDE), ((1, width), WIDE), ((1, width), WIDE),
    ]
    return pl.pallas_call(
        functools.partial(mlp_back_kernel, (block, windows, width, hidden)),
        grid=(clips,),
        in_specs=[
            clip_spec(travel),
            clip_spec((rows, hidden)),
            clip_spec((rows, width)),
            whole(gain.shape),
            layer(w_expand.shape[1:], block),
            layer(w_reduce.shape[1:], block),
        ]
        + [ANY] * len(through),
        out_specs=[ANY] * len(through)
        + [clip_spec(s) for s, unused in kinds[:3]]
        + [pl.BlockSpec(s, lambda i: (0, 0)) for s, unused in kinds[3:]],
        out_shape=[jax.ShapeDtypeStruct(v.shape, v.dtype) for v in through]
        + [jax.ShapeDtypeStruct(all_clips(s, clips), k) for s, k in kinds[:3]]
        + [jax.ShapeDtypeStruct(s, k) for s, k in kinds[3:]],
        input_output_aliases={6 + i: i for i in range(len(through))},
        compiler_params=params(),
        cost_estimate=cost(400),
        name=f"mlp_back_{block}",
    )(g, slope, middle, gain, w_expand, w_reduce, *through)


def attention_back(block, x, mid, triple, recip, raised, attended, weights, shapes, after=()):
    gain, shift, w_in, w_out, w_expand, b_expand, w_reduce = weights
    clips, windows, length, parts, rows, width, hidden = sizes(weights, shapes)
    travel = (parts, windows, length // parts, width)
    flat = window_spec("rows", shapes, width)
    wide = window_spec("rows", shapes, 3 * width)
    ins = [mid, triple, recip, raised, attended, w_out]
    in_specs = [
        flat,
        wide,
        flat,
        pl.BlockSpec((1,) + raised.shape[1:], lambda i: (i, 0, 0, 0)),
        flat,
        layer(w_out.shape[1:], block),
    ]
    out_specs = [wide]
    out_shape = [jax.ShapeDtypeStruct((clips * rows, 3 * width), LOW)]
    if block == 1:
        ins += [x, gain, w_in]
        in_specs += [flat, whole(gain.shape), layer(w_in.shape[1:], block)]
        out_specs += [pl.BlockSpec((1, width), lambda i: (0, 0))] * 2
        out_specs += [window_spec("tubes", shapes, width)]
        out_shape += [jax.ShapeDtypeStruct((1, width), WIDE)] * 2
        out_shape += [jax.ShapeDtypeStruct(all_clips(travel, clips), LOW)]
    return pl.pallas_call(
        functools.partial(attention_back_kernel, (block, 1, length, width)),
        grid=(clips * windows,),
        in_specs=in_specs + [ANY] * len(after),
        out_specs=out_specs,
        out_shape=out_shape,
        scratch_shapes=[pltpu.VMEM((length, width), LOW)],
        compiler_params=params(),
        cost_estimate=cost(42 if block else 0.01),
        name=f"attention_back_{block}",
    )(*ins, *after)


def finish(x, mid, triple, mixed, weights, shapes, through, after=()):
    gain, shift, w_in, w_out, w_expand, b_expand, w_reduce = weights
    clips, windows, length, parts, rows, width, hidden = sizes(weights, shapes)
    travel = (parts, windows, length // parts, width)
    tokens = (windows, length, width)
    sums = jax.ShapeDtypeStruct((1, width), WIDE)
    sums_spec = pl.BlockSpec((1, width), lambda i: (0, 0))
    return pl.pallas_call(
        functools.partial(finish_kernel, windows),
        grid=(clips,),
        in_specs=[
            clip_spec(tokens),
            clip_spec((rows, width)),
            clip_spec((rows, 3 * width)),
            whole(gain.shape),
            layer(w_in.shape[1:], 0),
            clip_spec(travel),
        ]
        + [ANY] * (len(through) + len(after)),
        out_specs=[ANY] * len(through)
        + [sums_spec, sums_spec, clip_spec(tokens), clip_spec(tokens)],
        out_shape=[jax.ShapeDtypeStruct(v.shape, v.dtype) for v in through]
        + [sums, sums]
        + [jax.ShapeDtypeStruct(all_clips(tokens, clips), LOW)] * 2,
        input_output_aliases={6 + i: i for i in range(len(through))},
        compiler_params=params(),
        cost_estimate=cost(0.01),
        name="finish",
    )(x, mid, triple, gain, w_in, mixed, *through, *after)


def outer_rows(place, active, grad, parts, is_split, after=()):
    total, width = grad.shape
    hidden = active.shape[1]
    steps = hidden // width
    group = parts // steps
    rows = hidden // parts
    if is_split:
        half = group // 2
        spec = pl.BlockSpec((half, rows, width), lambda i, place: (i ^ (place[0] // 2 // half), 0, 0))
        shape = jax.ShapeDtypeStruct((parts // 2, rows, width), LOW)
    else:
        spec = pl.BlockSpec((group, rows, width), lambda i, place: (i, 0, 0))
        shape = jax.ShapeDtypeStruct((parts, rows, width), LOW)
    arrays = 2 if is_split else 1
    return pl.pallas_call(
        functools.partial(outer_kernel, False, is_split),
        grid_spec=pltpu.PrefetchScalarGridSpec(
            num_scalar_prefetch=1,
            grid=(steps,),
            in_specs=[
                pl.BlockSpec((total, width), lambda i, place: (0, i)),
                pl.BlockSpec(
                    (total, width), lambda i, place: (0, 0), pipeline_mode=pl.Buffered(1)
                ),
            ]
            + [ANY] * len(after),
            out_specs=[spec] * arrays,
        ),
        out_shape=[shape] * arrays,
        compiler_params=params(),
        cost_estimate=cost(14),
        name="outer_rows",
    )(place, active, grad, *after)


def outer_columns(
    place, left, right, last, parts, is_split, after=(), skip=0, through=(), room=0, into=()
):
    total, width = left.shape
    steps = right.shape[1] // width
    blocks = steps + (1 if last else 0)
    ins = [place, left, right, *last]
    in_specs = [
        SCALARS,
        whole((total, width)),
        pl.BlockSpec((total, width), lambda i: (0, jnp.minimum(i, steps - 1))),
    ]
    in_specs += [whole((total, width))] * len(last)
    owners, arrays = (parts // 2, 2) if is_split else (parts, 1)
    spec = pl.BlockSpec((owners, width // parts, width), lambda i: (0, i + skip, 0))
    shape = jax.ShapeDtypeStruct((owners, (blocks + skip + room) * width // parts, width), LOW)
    aliases = {len(ins) + i: i for i in range(len(through))}
    if into:
        aliases[len(ins)] = 0
    return pl.pallas_call(
        functools.partial(outer_kernel, bool(last), is_split),
        grid=(blocks,),
        in_specs=in_specs + [ANY] * (len(into) + len(through) + len(after)),
        out_specs=[ANY] * len(through) + [spec] * arrays,
        out_shape=[jax.ShapeDtypeStruct(v.shape, v.dtype) for v in through] + [shape] * arrays,
        input_output_aliases=aliases,
        compiler_params=params(),
        cost_estimate=cost(4 * blocks if blocks > 3 else 1),
        name="outer_columns",
    )(*ins, *into, *through, *after)


def add_all(values):
    total = values[0].astype(WIDE)
    for value in values[1:]:
        total = total + value.astype(WIDE)
    return total.astype(LOW)


def swap(value, axis, offset):
    return lax.ppermute(
        value, axis, [(i, i ^ offset) for i in range(lax.axis_size(axis))]
    )


def sum_frames(send, keep, reverse):
    bits = (lax.axis_size("frame") // 2).bit_length() - 1
    shape = (2,) * bits + keep.shape[1:]
    terms = [keep.reshape(shape), swap(send, "frame", 1).reshape(shape)]
    order = list(range(1, bits + 1))
    if reverse:
        order = order[::-1]
    left = list(range(bits, 0, -1))
    for bit in order:
        axis = left.index(bit)
        left.remove(bit)
        far = add_all([lax.index_in_dim(t, 1, axis, keepdims=False) for t in terms])
        again = yield far
        if again is not None:
            terms[0] = again.reshape(shape)
        terms = [lax.index_in_dim(t, 0, axis, keepdims=False) for t in terms]
        terms.append(swap(far, "frame", 1 << bit))
    yield add_all(terms)


def last_of(steps):
    for value in steps:
        pass
    return value


def clip_blocks(total):
    size = lax.axis_size("clip")
    rows = -(-total.shape[0] // (8 * size)) * 8
    total = jnp.pad(total, ((0, rows * size - total.shape[0]), (0, 0)))
    return total.reshape(size, rows, total.shape[1])


def over_clips(*values):
    value = values[0] if len(values) == 1 else jnp.concatenate(values, axis=1)
    got = lax.all_to_all(value, "clip", 0, 0)
    cuts = [sum(v.shape[1] for v in values[: i + 1]) for i in range(len(values))]
    return [got[:, cut - v.shape[1] : cut] for cut, v in zip(cuts, values)]


def to_all_clips(value):
    return jnp.broadcast_to(value[None], (lax.axis_size("clip"),) + value.shape)


def gather_kernel(block, plan, n_in, n_outs, *refs):
    sources, outs = refs[: len(plan)], refs[n_in : n_in + n_outs]
    for source, group in zip(sources, plan):
        width = source.shape[1]
        start = 0
        for out, columns in group:
            length = outs[out].shape[1]
            for c in range(columns):
                outs[out][0, :, c * width : (c + 1) * width] = source[
                    start : start + length, :
                ].astype(WIDE)
                start += length


def gather(block, sources, plan, outs, through=()):
    filled = not isinstance(outs[0], jax.ShapeDtypeStruct)
    extra = list(outs) if filled else []
    specs = [
        pl.BlockSpec((1,) + v.shape[1:], lambda i: (block, 0, 0)) for v in outs
    ]
    ins = [*sources, *extra, *through]
    aliases = {len(sources) + i: i for i in range(len(extra))}
    aliases.update({len(ins) - len(through) + i: len(outs) + i for i in range(len(through))})
    return pl.pallas_call(
        functools.partial(gather_kernel, block, plan, len(ins), len(outs)),
        grid=(1,),
        in_specs=[whole(v.shape) for v in sources] + [ANY] * (len(extra) + len(through)),
        out_specs=specs + [ANY] * len(through),
        out_shape=[jax.ShapeDtypeStruct(v.shape, v.dtype) for v in [*outs, *through]],
        input_output_aliases=aliases,
        compiler_params=params(),
        cost_estimate=cost(4),
        name="gather",
    )(*ins)


def exchange(value):
    return lax.all_to_all(value, "frame", 0, 0)


def local(
    tokens,
    frame_counts,
    norm_gain,
    norm_bias,
    project_in,
    project_out,
    expand_weight,
    expand_bias,
    reduce_weight,
    cotangent,
):
    clips, frames, length, width = tokens.shape
    hidden = expand_weight.shape[2]
    parts = lax.axis_size("frame")
    part = width // parts
    shapes = (clips, frames, length, parts)
    half = clips // 2
    weights = (
        norm_gain, norm_bias, project_in, project_out, expand_weight, expand_bias, reduce_weight
    )
    place = lax.axis_index("frame").astype(jnp.int32).reshape(1)

    out, saved0 = forward(0, frame_counts, tokens, cotangent, weights, None, 0, shapes)
    boundary_a = exchange(out)
    out, saved0 = forward(0, frame_counts, tokens, cotangent, weights, saved0, half, shapes)
    boundary_b = exchange(out)
    cotangent_tubes, saved1 = forward(
        1, frame_counts, boundary_a, None, weights, None, 0, shapes, saved0[9]
    )
    cotangent_tubes = exchange(cotangent_tubes)
    saved1 = forward(1, frame_counts, boundary_b, None, weights, saved1, half, shapes)

    def scatter(value):
        return lax.psum_scatter(value, "frame", scatter_dimension=0, tiled=True)[0]

    normed, triple, recip, raised, attended, middle, normed2, active, slope, stream = saved1
    mixed = output(active, middle, weights, shapes)
    mixed, rows1, pre, mid, bias1, gain12, shift12 = mlp_back(
        1, cotangent_tubes, slope, middle, weights, shapes, [mixed]
    )
    mixed = exchange(mixed)
    columns = hidden // width
    (reduce1,) = outer_rows(place, active, rows1, parts, False)
    reduce1_sum = scatter(reduce1)
    grad_triple, gain11, shift11, grad_boundary = attention_back(
        1, stream, mid, triple, recip, raised, attended, weights, shapes, [reduce1]
    )
    grad_boundary = exchange(grad_boundary)
    (rest1,) = outer_columns(place, normed2, pre, [], parts, False, room=columns)
    (rest1,) = outer_columns(
        place, normed, grad_triple, [attended, mid], parts, False, [reduce1_sum], columns,
        into=[rest1],
    )

    normed, triple, recip, raised, attended, middle, normed2, active, slope = saved0[:9]
    rows0, pre, mid, bias0, gain02, shift02 = mlp_back(
        0, grad_boundary, slope, middle, weights, shapes, ()
    )
    rest1_sum = scatter(rest1)
    reduce0 = outer_rows(place, active, rows0, parts, True)
    expand0 = outer_columns(
        place, normed2, pre, [attended, mid], parts, True, [reduce0[0]]
    )
    (grad_triple,) = attention_back(
        0, None, mid, triple, recip, raised, attended, weights, shapes, [expand0[0], rest1_sum]
    )
    steps_c, steps_d = sum_frames(*reduce0, False), sum_frames(*expand0, True)
    sent = [next(steps_c), next(steps_d)]
    keep_r, keep_e, gain01, shift01, grad_tokens, mixed = finish(
        tokens, mid, grad_triple, mixed, weights, shapes,
        [reduce0[1], expand0[1]], sent,
    )
    reduce1_sum, rest1_sum = lax.psum((reduce1_sum, rest1_sum), "clip")
    sent = [steps_c.send(keep_r), steps_d.send(keep_e)]

    def by_owner(*values):
        return jnp.concatenate([v.reshape(parts, -1) for v in values], axis=1)

    small = by_owner(
        gain01, gain02, shift01, shift02, bias0, gain11, gain12, shift11, shift12, bias1
    ).astype(LOW)
    count = small.shape[1]
    small = jnp.pad(small, ((0, 0), (0, SMALL_ROWS * width - count)))
    small, send, keep = outer_columns(
        place, normed, grad_triple, [], parts, True, sent, 0,
        [small.reshape(parts, SMALL_ROWS, width)],
    )
    outs = [
        (2, hidden // parts, width),
        (2, part, hidden),
        (2, part, 3 * width),
        (2, part, width),
    ]
    outs = [jax.ShapeDtypeStruct(v, WIDE) for v in outs]
    *outs, keep = gather(
        1,
        [reduce1_sum, rest1_sum],
        (((0, 1),), ((1, columns), (2, 3), (3, 1))),
        outs,
        [keep],
    )
    cut = send.shape[1] // 2
    steps_a = sum_frames(send[:, :cut], keep[:, :cut], False)
    steps_b = sum_frames(send[:, cut:], keep[:, cut:], True)
    small = add_all(list(exchange(small)))
    last = jnp.concatenate([last_of(steps_a), last_of(steps_b)], axis=0)
    mlp0_sum = jnp.concatenate([last_of(steps_c), last_of(steps_d)], axis=0)
    (mlp0_sum,) = over_clips(clip_blocks(mlp0_sum))
    mlp0_sum = to_all_clips(add_all(list(mlp0_sum)))
    mlp0_sum, in0_sum, small = over_clips(mlp0_sum, clip_blocks(last), to_all_clips(small))
    in0_sum = to_all_clips(add_all(list(in0_sum)))
    (in0_sum,) = over_clips(in0_sum)
    small = jnp.sum(small.astype(WIDE), axis=0).reshape(-1)[:count].reshape(2, -1)
    grad_reduce, grad_expand, grad_in, grad_out = gather(
        0,
        [mlp0_sum.reshape(-1, width), in0_sum.reshape(-1, width)],
        (((0, 1), (1, columns), (3, 1)), ((2, 3),)),
        outs,
    )
    return (
        mixed,
        grad_tokens,
        small[:, : 2 * part].reshape(2, 2, part),
        small[:, 2 * part : 4 * part].reshape(2, 2, part),
        grad_in,
        grad_out,
        grad_expand,
        small[:, 4 * part :],
        grad_reduce,
    )


def solution(mesh):
    in_specs = (
        P("clip", "frame", None, None),
        P("clip"),
        P(),
        P(),
        P(),
        P(),
        P(),
        P(),
        P(),
        P("clip", "frame", None, None),
    )
    out_specs = (
        P("clip", "frame", None, None),
        P("clip", "frame", None, None),
        P(None, None, "frame"),
        P(None, None, "frame"),
        P(None, "frame", None),
        P(None, "frame", None),
        P(None, "frame", None),
        P(None, "frame"),
        P(None, "frame", None),
    )
    return jax.shard_map(local, mesh=mesh, in_specs=in_specs, out_specs=out_specs, check_vma=False)
```
